1024 devices in a mesh: bricks: 256 (over x, z, core), gz: 4 (over y).
Axes of the slice: x: 4, y: 4, z: 32, core: 2. Of those that a mesh axis runs over, the one named last changes fastest.
Arguments:
- source: float32 [12, 512, 16, 128], P(None, 'bricks', 'gz'), may hold values from -6 to 6
- reaction: bfloat16 [12, 12, 512, 16, 128], P(None, None, 'bricks', 'gz'), may hold values from -0.1 to 2, as said below
- smoother: bfloat16 [12, 12, 512, 16, 128], P(None, None, 'bricks', 'gz'), may hold values from -0.025 to 0.5
- diffusion: float32 [12], replicated, may hold values from 0.3 to 1.5
- active: int32 [256, 4, 4], P('bricks', 'gz'), may hold values 0 or 1
Outputs:
- update: float32 [12, 512, 16, 128], P(None, 'bricks', 'gz')
- new_residual: float32 [12, 512, 16, 128], P(None, 'bricks', 'gz')
The draws below stay inside these ranges and needn't reach their ends.
Inputs may be any that keep to these rules, and one draw needn't show every extreme that they name: `reaction`: each cell's block has diagonal entries of 0.2 to 2.0 and other entries of magnitude 0.1 or less.
All inputs are finite; a program needn't handle non-finite values. No bound on the sum of `active` on one device may be relied on, other than what follows from the above.
Results may differ from the reference program's by a relative error of at most 0.0003.
Values sent between devices are 32-bit elements; how exact they have to be, the bound alone decides.
No kernel may reach another device: no remote copies, remote signals or barrier semaphores. Data moves between devices by JAX's collectives and lax.ppermute only.
A program may use at most 32 MiB of HBM per device.

```python
import math
import jax
import jax.numpy as jnp
from jax import lax

COMP = 12
NY = 128
BX = 2
BZ = 4
BY = 32
CYCLES = 2
CSWEEPS = 3
NX = 512
NZ = 16


def reaction_tables(key):
    rate_key = jax.random.fold_in(key, 11)
    pair_key = jax.random.fold_in(key, 12)
    spread_key = jax.random.fold_in(key, 13)
    rates = jnp.exp(jax.random.uniform(rate_key, (COMP, NX, NZ, NY), jnp.float32, math.log(0.2), math.log(2.0)))
    coeffs = jnp.exp(jax.random.uniform(spread_key, (COMP,), jnp.float32, math.log(0.3), math.log(1.5)))
    rates = jnp.clip(rates, 0.2, 2.0)
    coeffs = jnp.clip(coeffs, 0.3, 1.5)
    couplings = jax.random.uniform(pair_key, (COMP, COMP, NX, NZ, NY), jnp.float32, -0.099, 0.099)
    return (rates, couplings, coeffs)


def draw_reaction(key, part):
    rates, couplings, coeffs = reaction_tables(key)
    eye_table = jnp.eye(COMP, dtype=jnp.float32)[:, :, None, None, None]
    return (couplings * (1.0 - eye_table) + eye_table * rates[None]).astype(jnp.bfloat16)


def draw_smoother(key, part):
    rates, couplings, coeffs = reaction_tables(key)
    eye_table = jnp.eye(COMP, dtype=jnp.float32)[:, :, None, None, None]
    totals = rates + 6.0 * coeffs[:, None, None, None]
    inverse = eye_table / totals[None] - couplings * (1.0 - eye_table) / (totals[:, None] * totals[None])
    return inverse.astype(jnp.bfloat16)


def draw_diffusion(key, part):
    rates, couplings, coeffs = reaction_tables(key)
    return coeffs


def touch_ends(entries, stream_key, least, high):
    longest = entries.shape.index(max(entries.shape))
    spots = []
    for shift in (0, 1):
        where = [jax.random.randint(jax.random.fold_in(stream_key, axis), (), 0, length) for axis, length in enumerate(entries.shape)]
        where[longest] = (where[longest] + shift) % entries.shape[longest]
        spots.append(tuple(where))
    return entries.at[spots[0]].set(least).at[spots[1]].set(high)


def levels(stream_key, shape, shards, low, high):
    level = 1.0
    for position, blocks in shards:
        steps = jax.random.uniform(jax.random.fold_in(jax.random.fold_in(stream_key, 6), position), (blocks,), jnp.float32, low / len(shards), high / len(shards))
        level = level * jnp.repeat(jnp.exp(steps), shape[position] // blocks).reshape((-1,) + (1,) * (len(shape) - 1 - position))
    return level


def noise(own_key, shape, deviation, most, split=(), held_as=jnp.bfloat16):
    entries = deviation * jax.random.normal(own_key, shape, jnp.float32)
    if split:
        entries = entries * levels(own_key, shape, split, -0.22, 0.18)
    return jnp.clip(entries, -most, most).astype(held_as)


def setup_inputs(seed: int = 0) -> dict:
    seeds = jax.random.split(jax.random.key(seed), 6)
    return {
        "source": noise(seeds[0], (COMP, NX, NZ, NY), 1.0, 6.0, ((1, 256), (2, 4)), jnp.float32),
        "reaction": draw_reaction(jax.random.fold_in(seeds[5], 71), 0),
        "smoother": draw_smoother(jax.random.fold_in(seeds[5], 71), 0),
        "diffusion": draw_diffusion(jax.random.fold_in(seeds[5], 71), 0),
        "active": touch_ends((jax.random.randint(seeds[4], (NX // BX, NZ // BZ, NY // BY), 0, 4) < 3).astype(jnp.int32), jax.random.fold_in(seeds[4], 1), 0, 1),
    }


def spread_mask(bricks_on, size_x, size_z, size_y):
    weights = bricks_on.astype(jnp.float32)
    count_x, count_z, count_y = weights.shape
    tiled = jnp.broadcast_to(weights[:, None, :, None, :, None], (count_x, size_x, count_z, size_z, count_y, size_y))
    return tiled.reshape(count_x * size_x, count_z * size_z, count_y * size_y)


def brick_mean(blocks, size_x, size_z, size_y):
    comps = blocks.shape[0]
    shaped = blocks.reshape(comps, comps, blocks.shape[2] // size_x, size_x, blocks.shape[3] // size_z, size_z, blocks.shape[4] // size_y, size_y)
    return jnp.mean(shaped.astype(jnp.float32), axis=(3, 5, 7))


def brick_apply(blocks, vector, size_x, size_z, size_y):
    comps = blocks.shape[1]
    shaped = vector.reshape(comps, blocks.shape[2], size_x, blocks.shape[3], size_z, blocks.shape[4], size_y)
    result = jnp.sum(blocks[:, :, :, None, :, None, :, None] * shaped[None], axis=1)
    return result.reshape(vector.shape)


def cell_apply(blocks, vector):
    def one_slab(number):
        slab_blocks = lax.dynamic_index_in_dim(blocks, number, 2, keepdims=False)
        slab_vector = lax.dynamic_index_in_dim(vector, number, 1, keepdims=False)
        return jnp.sum(slab_blocks.astype(jnp.float32) * slab_vector[None], axis=1)

    stacked = lax.map(one_slab, jnp.arange(vector.shape[1], dtype=jnp.int32))
    return jnp.moveaxis(stacked, 0, 1)


def neighbor_sum(padded):
    totals = padded[:, 2:, 1:-1, 1:-1] + padded[:, :-2, 1:-1, 1:-1]
    totals = totals + padded[:, 1:-1, 2:, 1:-1] + padded[:, 1:-1, :-2, 1:-1]
    return totals + padded[:, 1:-1, 1:-1, 2:] + padded[:, 1:-1, 1:-1, :-2]


def squeeze_dim(padded, axis):
    length = (padded.shape[axis] - 2) // 2
    parts = [lax.slice_in_dim(padded, offset, offset + 2 * length - 1, 2, axis) for offset in range(4)]
    return (parts[0] + 3.0 * parts[1] + 3.0 * parts[2] + parts[3]) * 0.125


def coarsen(padded):
    return squeeze_dim(squeeze_dim(squeeze_dim(padded, 1), 2), 3)


def stretch_dim(padded, axis):
    length = padded.shape[axis] - 2
    lower = lax.slice_in_dim(padded, 0, length, 1, axis)
    middle = lax.slice_in_dim(padded, 1, length + 1, 1, axis)
    upper = lax.slice_in_dim(padded, 2, length + 2, 1, axis)
    even_rows = 0.75 * middle + 0.25 * lower
    odd_rows = 0.75 * middle + 0.25 * upper
    joined = jnp.stack([even_rows, odd_rows], axis=axis + 1)
    new_shape = list(even_rows.shape)
    new_shape[axis] = 2 * length
    return joined.reshape(new_shape)


def refine(padded):
    return stretch_dim(stretch_dim(stretch_dim(padded, 1), 2), 3)


def pad_all(values):
    return jnp.pad(values, ((0, 0), (1, 1), (1, 1), (1, 1)))


def reference(source, reaction, smoother, diffusion, active):
    fine_mask = spread_mask(active, BX, BZ, BY)
    coarse_mask = spread_mask(active, BX // 2, BZ // 2, BY // 2)
    coeffs = diffusion[:, None, None, None]
    coarse_react = brick_mean(reaction, BX, BZ, BY)
    coarse_smooth = brick_mean(smoother, BX, BZ, BY)

    def fine_operator(vector):
        padded = pad_all(fine_mask * vector)
        inner = cell_apply(reaction, vector) + coeffs * (6.0 * vector - neighbor_sum(padded))
        return fine_mask * inner + (1.0 - fine_mask) * vector

    def fine_smooth(resid):
        return fine_mask * cell_apply(smoother, resid) + (1.0 - fine_mask) * resid

    def coarse_smooth_step(resid):
        return coarse_mask * brick_apply(coarse_smooth, resid, BX // 2, BZ // 2, BY // 2) + (1.0 - coarse_mask) * resid

    def coarse_operator(vector):
        padded = pad_all(coarse_mask * vector)
        inner = brick_apply(coarse_react, vector, BX // 2, BZ // 2, BY // 2) + 0.25 * coeffs * (6.0 * vector - neighbor_sum(padded))
        return coarse_mask * inner + (1.0 - coarse_mask) * vector

    update = source
    for cycle_no in range(CYCLES):
        if cycle_no == 0:
            update = fine_smooth(source)
        else:
            update = update + fine_smooth(source - fine_operator(update))
        coarse_rhs = coarsen(pad_all(source - fine_operator(update)))
        coarse_sol = coarse_smooth_step(coarse_rhs)
        for sweep_no in range(CSWEEPS - 1):
            coarse_sol = coarse_sol + coarse_smooth_step(coarse_rhs - coarse_operator(coarse_sol))
        update = update + refine(pad_all(coarse_sol))
        update = update + fine_smooth(source - fine_operator(update))
    return update, source - fine_operator(update)
```

```python
import functools

import jax
import jax.numpy as jnp
from jax import lax
from jax.experimental import pallas as pl
from jax.experimental.pallas import tpu as pltpu
from jax.sharding import Mesh
from jax.sharding import PartitionSpec as P

COMP = 12
HALF = 6
F32 = jnp.float32
BF16 = jnp.bfloat16
X_AXES = ("xg", "xc", "core")
TILE = (8, 128)
CHANNELS = 11
CENTRE = 3
VMEM_LIMIT = 32 * 1024 * 1024


def rows(shape=TILE):
    return lax.broadcasted_iota(jnp.int32, shape, 0)


def lanes(shape=TILE):
    return lax.broadcasted_iota(jnp.int32, shape, 1)


def up(x, by):
    return pltpu.roll(x, 8 - by, 0)


def down(x, by):
    return pltpu.roll(x, by, 0)


def pick(cond, a, b):
    return jnp.where(cond, a, b)


def hat(diff):
    inner = jnp.logical_or(diff == 0, diff == 1)
    outer = jnp.logical_or(diff == -1, diff == 2)
    return jnp.where(inner, 3.0, jnp.where(outer, 1.0, 0.0)).astype(F32)


def split(x, parts):
    pieces = []
    for _ in range(parts):
        piece = x.astype(BF16)
        pieces.append(piece)
        x = x - piece.astype(F32)
    return pieces


def dot(a, b):
    return jnp.dot(a, b, preferred_element_type=F32)


def dot_right(x, weights, parts=3):
    total = None
    for piece in split(x, parts):
        term = dot(piece, weights)
        total = term if total is None else total + term
    return total


def dot_left(weights, x, parts=3):
    total = None
    for piece in split(x, parts):
        term = dot(weights, piece)
        total = term if total is None else total + term
    return total


def fine_mask_of(act_ref):
    brick = lanes() // 32
    out = jnp.zeros(TILE, F32)
    for b in range(4):
        out = jnp.where(brick == b, act_ref[b].astype(F32), out)
    return out


def packed_mask_of(act_ref):
    brick = (lanes() % 64) // 16
    out = jnp.zeros(TILE, F32)
    for b in range(4):
        out = jnp.where(brick == b, act_ref[b].astype(F32), out)
    return out


def load(ref):
    return [ref[c] for c in range(COMP)]


def block_product(blocks_ref, vec):
    out = []
    for c in range(COMP):
        acc = None
        for d in range(0, COMP, 2):
            pair = blocks_ref[pl.ds((c * COMP + d) * 8, 16), :].astype(F32)
            term = pair[:8] * vec[d] + pair[8:] * vec[d + 1]
            acc = term if acc is None else acc + term
        out.append(acc)
    return out


def smooth(smoother_ref, mask, resid):
    prod = block_product(smoother_ref, resid)
    return [mask * a + (1.0 - mask) * r for a, r in zip(prod, resid)]


def neighbours(mv, hx, hz):
    z = rows() % 4
    lane = lanes()
    total = down(mv, 4) + hx + hz
    total = total + jnp.where(z > 0, down(mv, 1), 0.0) + jnp.where(z < 3, up(mv, 1), 0.0)
    total = total + jnp.where(lane > 0, pltpu.roll(mv, 1, 1), 0.0)
    return total + jnp.where(lane < 127, pltpu.roll(mv, 127, 1), 0.0)


def operator(reaction_ref, diff_ref, mask, vec, hx, hz):
    prod = block_product(reaction_ref, vec)
    out = []
    for c in range(COMP):
        v = vec[c]
        inner = prod[c] + diff_ref[c] * (6.0 * v - neighbours(mask * v, hx[c], hz[c]))
        out.append(mask * inner + (1.0 - mask) * v)
    return out


def write_faces(sc_ref, mask, vec, face_ref, swap_ref):
    core, zd = sc_ref[0], sc_ref[1]
    s = rows()
    low_half = s < 4
    z = s % 4
    mv = [mask * v for v in vec]
    first = core == 0
    for j in range(HALF):
        a, b = mv[j], mv[j + HALF]
        to_high = jnp.where(low_half, down(a, 4), b)
        to_low = jnp.where(low_half, a, down(b, 4))
        in_chip = pick(first, to_high, to_low)
        swap_ref[j] = pick(first, to_low, to_high)
        z_up = jnp.where(z == 0, up(a, 3), jnp.where(z == 1, up(b, 2), 0.0))
        z_down = jnp.where(z == 3, down(a, 3), jnp.where(z == 2, down(b, 2), 0.0))
        for other in range(4):
            along = pick(other > zd, z_up, z_down)
            face_ref[other, j] = pick(first, along, in_chip)
            face_ref[4 + other, j] = pick(first, in_chip, along)


def read_faces(sc_ref, face_ref, swap_ref):
    core, zd = sc_ref[0], sc_ref[1]
    s = rows()
    low_half = s < 4
    z = s % 4
    first = core == 0
    chip_at = (1 - core) * 4 + zd
    low_at = core * 4 + jnp.maximum(zd - 1, 0)
    high_at = core * 4 + jnp.minimum(zd + 1, 3)
    has_low = jnp.logical_and(z == 0, zd > 0)
    has_high = jnp.logical_and(z == 3, zd < 3)
    hx, hz = [None] * COMP, [None] * COMP
    for j in range(HALF):
        chip = face_ref[chip_at, j]
        cross = swap_ref[j]
        low = pick(first, cross, chip)
        high = pick(first, chip, cross)
        hx[j] = jnp.where(low_half, low, down(high, 4))
        hx[j + HALF] = jnp.where(low_half, down(low, 4), high)
        zl = face_ref[low_at, j]
        zh = face_ref[high_at, j]
        hz[j] = jnp.where(has_low, zl, jnp.where(has_high, zh, 0.0))
        hz[j + HALF] = jnp.where(has_low, up(zl, 1), jnp.where(has_high, down(zh, 1), 0.0))
    return hx, hz


def contributions(resid):
    l, o = rows((128, 128)), lanes((128, 128))
    low = jnp.where(o < 64, hat(l - 2 * o), 0.0).astype(BF16)
    high = jnp.where(o >= 64, hat(l - 2 * (o - 64)), 0.0).astype(BF16)
    a = jnp.concatenate(resid[:HALF], axis=0)
    b = jnp.concatenate(resid[HALF:], axis=0)
    along_y = (dot_right(a, low) + dot_right(b, high)) * 0.125
    tiles = [along_y[8 * j : 8 * j + 8] for j in range(HALF)]
    stacked = jnp.concatenate(
        [jnp.concatenate(tiles[:3], axis=1), jnp.concatenate(tiles[3:], axis=1)], axis=0
    )
    o, k = rows((24, 16)), lanes((24, 16))
    x, group, zr = o // 8, (o % 8) // 4, o % 4
    xi, zi = (k % 8) // 4, k % 4
    weights = hat(xi - 2 * (x - 1)) * hat(zi - 2 * (zr - 1))
    weights = jnp.where(group == k // 8, weights, 0.0).astype(BF16)
    result = dot_left(weights, stacked) * (1.0 / 64.0)
    out = []
    for jj in range(3):
        for x in range(3):
            out.append(result[8 * x : 8 * x + 8, 128 * jj : 128 * jj + 128])
    return out


def packed_blocks(smoother_ref, reaction_ref, act_ref, sums_ref):
    l, o = rows((128, 128)), lanes((128, 128))
    weights = jnp.where(l // 32 == o % 4, 1.0 / 256.0, 0.0).astype(BF16)
    zero = jnp.zeros((16, 128), F32)
    for a, ref in enumerate((smoother_ref, reaction_ref)):
        for n in range(0, COMP * COMP, 2):
            pair = ref[pl.ds(n * 8, 16), :].astype(F32)
            sums_ref[a, pl.ds(n, 1), :] = jnp.sum(pair[:8], axis=0, keepdims=True)
            sums_ref[a, pl.ds(n + 1, 1), :] = jnp.sum(pair[8:], axis=0, keepdims=True)
        sums_ref[a, pl.ds(144, 16), :] = zero
        sums_ref[a] = dot_right(sums_ref[a], weights)
    s, lane = rows((16, 128)), lanes((16, 128))
    out = zero
    for k in range(8):
        for a in range(2):
            for half in range(2):
                part = sums_ref[a, pl.ds(72 * half + 9 * k, 16), :]
                out = jnp.where(lane // 4 == 4 * k + 2 * a + half, part, out)
    coarse = jnp.broadcast_to(packed_mask_of(act_ref)[:1], (16, 128))
    fine = jnp.broadcast_to(fine_mask_of(act_ref)[:1], (16, 128))
    return jnp.where(s < 9, out, jnp.where(s == 9, coarse, jnp.where(s == 10, fine, 0.0)))


def expand_channel(get_row):
    owner = rows() // 2
    out = jnp.broadcast_to(get_row(0), TILE)
    for zd in range(1, 4):
        out = jnp.where(owner == zd, jnp.broadcast_to(get_row(zd), TILE), out)
    return out


def coarse_product(bx_ref, which, w, vec):
    left = lanes() < 64
    both = [None] * COMP
    for j in range(HALF):
        turned = pltpu.roll(vec[j], 64, 1)
        both[j] = jnp.where(left, vec[j], turned)
        both[j + HALF] = jnp.where(left, turned, vec[j])
    out = []
    for j in range(HALF):
        acc = None
        for d in range(COMP):
            term = bx_ref[w, j * COMP + d, which] * both[d]
            acc = term if acc is None else acc + term
        out.append(acc)
    return out


def coarse_smooth(bx_ref, mask, w, resid):
    prod = coarse_product(bx_ref, 0, w, resid)
    return [mask * a + (1.0 - mask) * r for a, r in zip(prod, resid)]


def expand_blocks(win_ref, bx_ref):
    flat = jnp.concatenate([win_ref[w, r] for w in range(7) for r in range(9)], axis=0)
    pieces = split(flat, 2)
    l, o = rows((128, 256)), lanes((128, 256))
    target = (o // 128) * 8 + ((o % 128) // 64) * 4 + (o % 64) // 16
    for k in range(8):
        weights = jnp.where(l == 16 * k + target, 1.0, 0.0).astype(BF16)
        out = dot(pieces[0], weights) + dot(pieces[1], weights)
        for w in range(7):
            for r in range(9):
                tile = out[(w * 9 + r) * 8 : (w * 9 + r) * 8 + 8]
                bx_ref[w, 9 * k + r, 0] = tile[:, :128]
                bx_ref[w, 9 * k + r, 1] = tile[:, 128:]


def solve_coarse(sc_ref, diff_ref, rhs, win_ref, bx_ref):
    s, lane = rows(), lanes()
    left = lane < 64
    inner_lane = lane % 64
    coeffs = [
        0.25 * jnp.where(left, jnp.full(TILE, diff_ref[j], F32), jnp.full(TILE, diff_ref[j + HALF], F32))
        for j in range(HALF)
    ]
    masks = [win_ref[w, 9] for w in range(7)]
    b = [rhs(w) for w in range(7)]
    v = [coarse_smooth(bx_ref, masks[w], w, b[w]) for w in range(7)]
    for edge in (1, 2):
        mv = [[masks[w] * t for t in v[w]] if v[w] is not None else None for w in range(7)]
        new = [None] * 7
        for w in range(edge, 7 - edge):
            prod = coarse_product(bx_ref, 1, w, v[w])
            resid = []
            for j in range(HALF):
                t = mv[w][j]
                total = mv[w - 1][j] + mv[w + 1][j]
                total = total + jnp.where(s > 0, down(t, 1), 0.0) + jnp.where(s < 7, up(t, 1), 0.0)
                total = total + jnp.where(inner_lane > 0, pltpu.roll(t, 1, 1), 0.0)
                total = total + jnp.where(inner_lane < 63, pltpu.roll(t, 127, 1), 0.0)
                inner = prod[j] + coeffs[j] * (6.0 * v[w][j] - total)
                resid.append(b[w][j] - (masks[w] * inner + (1.0 - masks[w]) * v[w][j]))
            step = coarse_smooth(bx_ref, masks[w], w, resid)
            new[w] = [x + y for x, y in zip(v[w], step)]
        v = new
    return v[2:5]


def prolong(sc_ref, q):
    zd = sc_ref[1]
    o, k = rows((24, 24)), lanes((24, 24))
    group, s = o // 8, o % 8
    z = s % 4
    fx = jnp.where(group == 1, jnp.where(s < 4, -1, 2), s // 4)
    fz = jnp.where(group == 2, jnp.where(z == 0, -1, 4), z) + 4 * zd
    weights = hat(fx - 2 * (k // 8 - 1)) * hat(fz - 2 * (k % 8))
    unused = jnp.logical_and(group == 2, jnp.logical_or(z == 1, z == 2))
    weights = jnp.where(unused, 0.0, weights * 0.0625).astype(BF16)
    stacked = jnp.concatenate([jnp.concatenate(row, axis=1) for row in q], axis=0)
    xz = dot_left(weights, stacked)
    tall = jnp.concatenate([xz[:, 128 * j : 128 * j + 128] for j in range(HALF)], axis=0)
    a, f = rows((128, 256)), lanes((128, 256))
    along = hat(f % 128 - 2 * (a % 64)) * 0.25
    along = jnp.where(a // 64 == f // 128, along, 0.0).astype(BF16)
    fine = dot_right(tall, along)
    groups = []
    for g in range(3):
        tiles = [fine[24 * j + 8 * g : 24 * j + 8 * g + 8] for j in range(HALF)]
        groups.append([t[:, :128] for t in tiles] + [t[:, 128:] for t in tiles])
    return groups


def outside_masks(sc_ref, win_ref):
    zd = sc_ref[1]
    s = rows()
    z = s % 4
    turn = lax.rem(8 - 2 * zd, 8)
    low_x = pltpu.roll(win_ref[CENTRE - 1, 10], turn, 0)[:1]
    high_x = pltpu.roll(win_ref[CENTRE + 1, 10], turn, 0)[:1]
    own = pltpu.roll(win_ref[CENTRE, 10], turn, 0)
    low_z, high_z = own[7:8], own[2:3]
    mask_x = jnp.where(s < 4, jnp.broadcast_to(low_x, TILE), jnp.broadcast_to(high_x, TILE))
    mask_z = jnp.where(
        jnp.logical_and(z == 0, zd > 0),
        jnp.broadcast_to(low_z, TILE),
        jnp.where(jnp.logical_and(z == 3, zd < 3), jnp.broadcast_to(high_z, TILE), 0.0),
    )
    return mask_x, mask_z


def first_kernel(sc_ref, act_ref, src_ref, smoother_ref, u_ref, face_ref, swap_ref):
    mask = fine_mask_of(act_ref)
    u = smooth(smoother_ref, mask, load(src_ref))
    for c in range(COMP):
        u_ref[c] = u[c]
    write_faces(sc_ref, mask, u, face_ref, swap_ref)


def residual(sc_ref, act_ref, diff_ref, src_ref, reaction_ref, u_ref, face_ref, swap_ref):
    mask = fine_mask_of(act_ref)
    u = load(u_ref)
    hx, hz = read_faces(sc_ref, face_ref, swap_ref)
    au = operator(reaction_ref, diff_ref, mask, u, hx, hz)
    return mask, u, [src_ref[c] - au[c] for c in range(COMP)]


def send_kernel(
    with_blocks, sc_ref, act_ref, diff_ref, src_ref, reaction_ref, u_ref, face_ref, swap_ref, *rest
):
    if with_blocks:
        smoother_ref, r_ref, out_ref, sums_ref = rest
    else:
        r_ref, out_ref = rest
    _, _, resid = residual(sc_ref, act_ref, diff_ref, src_ref, reaction_ref, u_ref, face_ref, swap_ref)
    for c in range(COMP):
        r_ref[c] = resid[c]
    tiles = contributions(resid)
    if with_blocks:
        packed = packed_blocks(smoother_ref, reaction_ref, act_ref, sums_ref)
        tiles = tiles + [packed[:8], packed[8:]]
    for n, tile in enumerate(tiles):
        for target in range(16):
            out_ref[target, n] = tile


def gather_kernel(with_blocks, sc_ref, recv_ref, own_ref, far_ref, near_ref):
    right = sc_ref[2] // 2
    s = rows()
    low_half = s < 4
    for j in range(6):
        for jj in range(3):
            parts = []
            for zd in range(4):
                total = None
                for q in range(4):
                    x = j - q
                    if 0 <= x <= 2:
                        tile = recv_ref[q * 4 + zd, jj * 3 + x]
                        total = tile if total is None else total + tile
                parts.append(total)
            m0, m1, m2, m3 = parts
            even = (jnp.where(low_half, m0, down(m2, 4)), jnp.where(low_half, down(m0, 4), m2))
            odd = (jnp.where(low_half, m1, down(m3, 4)), jnp.where(low_half, down(m1, 4), m3))
            for n in range(2):
                own_ref[j, jj + 3 * n] = jnp.where(s < 7, up(even[n], 1), 0.0) + jnp.where(
                    s > 0, down(odd[n], 1), 0.0
                )
    for f in range(4):
        for j in range(HALF):
            far_ref[f * 6 + j] = own_ref[2 * right + f, j]
    for f in range(2):
        for j in range(HALF):
            near_ref[f * 6 + j] = own_ref[4 * right + f, j]
    if with_blocks:
        for e in range(3):
            for zd in range(4):
                for t in range(2):
                    far_ref[24 + e * 8 + zd * 2 + t] = recv_ref[(e + right) * 4 + zd, 9 + t]
        for zd in range(4):
            for t in range(2):
                near_ref[12 + zd * 2 + t] = recv_ref[3 * right * 4 + zd, 9 + t]


def fill_window(sc_ref, recv_ref, far_ref, near_ref, all_ref, win_ref):
    p = sc_ref[2]
    right = p // 2
    zero = jnp.zeros(TILE, F32)
    for n in range(16):
        for r in range(CHANNELS):
            all_ref[n, r] = zero
    for q in range(4):
        for r in range(CHANNELS):
            at = pl.ds(r % 8, 1)
            all_ref[q - p + 7, r] = expand_channel(lambda zd: recv_ref[q * 4 + zd, 9 + r // 8, at, :])
    base = 4 - p + 7 * right
    for e in range(3):
        for r in range(CHANNELS):
            at = pl.ds(r % 8, 1)
            all_ref[e + base, r] = expand_channel(lambda zd: far_ref[24 + e * 8 + zd * 2 + r // 8, at, :])
    place = 11 - p - 5 * right
    for r in range(CHANNELS):
        at = pl.ds(r % 8, 1)
        all_ref[place, r] = expand_channel(lambda zd: near_ref[12 + zd * 2 + r // 8, at, :])
    for w in range(7):
        for r in range(CHANNELS):
            win_ref[w, r] = all_ref[w + 4, r]


def correct_kernel(
    with_blocks,
    sc_ref,
    act_ref,
    diff_ref,
    reaction_ref,
    smoother_ref,
    u_ref,
    r_ref,
    own_ref,
    far_ref,
    near_ref,
    *rest,
):
    if with_blocks:
        recv_ref, new_ref, face_ref, swap_ref, win_ref, rhs_ref, bx_ref, all_ref = rest
        fill_window(sc_ref, recv_ref, far_ref, near_ref, all_ref, win_ref)
    else:
        win_ref, new_ref, face_ref, swap_ref, rhs_ref, bx_ref = rest
    p, brick, bricks = sc_ref[2], sc_ref[3], sc_ref[4]
    right = p // 2
    zero = jnp.zeros(TILE, F32)
    for n in range(16):
        for j in range(HALF):
            rhs_ref[n, j] = zero
    for n in range(6):
        for j in range(HALF):
            rhs_ref[n - p + 6, j] = own_ref[n, j]
    for f in range(4):
        at = f + 4 - p + 6 * right
        for j in range(HALF):
            rhs_ref[at, j] = rhs_ref[at, j] + far_ref[f * 6 + j]
    for f in range(2):
        at = f + 10 - p - 4 * right
        for j in range(HALF):
            rhs_ref[at, j] = rhs_ref[at, j] + near_ref[f * 6 + j]

    def rhs(w):
        place = brick + (w - CENTRE)
        inside = jnp.logical_and(place >= 0, place < bricks)
        return [pick(inside, rhs_ref[w + 4, j], 0.0) for j in range(HALF)]

    expand_blocks(win_ref, bx_ref)
    q = solve_coarse(sc_ref, diff_ref, rhs, win_ref, bx_ref)
    inside, hx, hz = prolong(sc_ref, q)
    mask_x, mask_z = outside_masks(sc_ref, win_ref)
    hx = [mask_x * t for t in hx]
    hz = [mask_z * t for t in hz]
    mask = fine_mask_of(act_ref)
    change = operator(reaction_ref, diff_ref, mask, inside, hx, hz)
    resid = [r_ref[c] - change[c] for c in range(COMP)]
    step = smooth(smoother_ref, mask, resid)
    new = [u_ref[c] + inside[c] + step[c] for c in range(COMP)]
    for c in range(COMP):
        new_ref[c] = new[c]
    write_faces(sc_ref, mask, new, face_ref, swap_ref)


def sweep_kernel(
    sc_ref, act_ref, diff_ref, src_ref, reaction_ref, u_ref, face_ref, swap_ref, smoother_ref,
    new_ref, face_out, swap_out,
):
    mask, u, resid = residual(
        sc_ref, act_ref, diff_ref, src_ref, reaction_ref, u_ref, face_ref, swap_ref
    )
    step = smooth(smoother_ref, mask, resid)
    new = [a + b for a, b in zip(u, step)]
    for c in range(COMP):
        new_ref[c] = new[c]
    write_faces(sc_ref, mask, new, face_out, swap_out)


def last_kernel(
    sc_ref, act_ref, diff_ref, src_ref, reaction_ref, u_ref, face_ref, swap_ref, r_ref
):
    _, _, resid = residual(
        sc_ref, act_ref, diff_ref, src_ref, reaction_ref, u_ref, face_ref, swap_ref
    )
    for c in range(COMP):
        r_ref[c] = resid[c]


SMEM_SPEC = pl.BlockSpec(memory_space=pltpu.SMEM)
VMEM_SPEC = pl.BlockSpec(memory_space=pltpu.VMEM)


def call(kernel, name, scalars, arrays, outs, scratch=()):
    return pl.pallas_call(
        kernel,
        name=name,
        in_specs=[SMEM_SPEC] * len(scalars) + [VMEM_SPEC] * len(arrays),
        out_specs=[VMEM_SPEC] * len(outs),
        out_shape=[jax.ShapeDtypeStruct(shape, F32) for shape in outs],
        scratch_shapes=[pltpu.VMEM(shape, F32) for shape in scratch],
        compiler_params=pltpu.CompilerParams(vmem_limit_bytes=VMEM_LIMIT),
    )(*scalars, *arrays)


VEC = (COMP, 8, 128)
FACE = (8, HALF, 8, 128)
SWAP = (HALF, 8, 128)


def local(bricks, source, reaction, smoother, diffusion, active):
    core = lax.axis_index("core")
    zd = lax.axis_index("gz")
    brick = lax.axis_index(X_AXES)
    scalars = jnp.stack(
        [core, zd, brick % 4, brick, jnp.int32(bricks), core, core, core]
    ).astype(jnp.int32)
    act = active.reshape(4)
    src = source.reshape(VEC)
    react = reaction.reshape(COMP * COMP * 8, 128)
    smoo = smoother.reshape(COMP * COMP * 8, 128)
    groups = bricks // 4

    pairs = [(i, i + 1) for i in range(1, bricks - 1, 2)]
    swap_pairs = pairs + [(b, a) for a, b in pairs]
    far_pairs, near_pairs = [], []
    for i in range(bricks):
        g, p = divmod(i, 4)
        step = 1 if p >= 2 else -1
        if 0 <= g + step < groups:
            far_pairs.append((i, 4 * (g + step) + 3 - p))
            near_pairs.append((i, i + 4 * step))

    def faces(face, swap):
        swap = lax.ppermute(swap, X_AXES, swap_pairs)
        face = lax.all_to_all(face, ("core", "gz"), 0, 0)
        return face, swap

    def to_coarse(message, with_blocks):
        recv = lax.all_to_all(message, ("xc", "core", "gz"), 0, 0)
        far_rows, near_rows = (48, 20) if with_blocks else (24, 12)
        own, far, near = call(
            functools.partial(gather_kernel, with_blocks),
            "gather",
            [scalars],
            [recv],
            [(6, HALF, 8, 128), (far_rows, 8, 128), (near_rows, 8, 128)],
        )
        far = lax.ppermute(far, X_AXES, far_pairs)
        near = lax.ppermute(near, X_AXES, near_pairs)
        return recv, own, far, near

    small = [scalars, act, diffusion]
    u, face, swap = call(first_kernel, "first", [scalars, act], [src, smoo], [VEC, FACE, SWAP])
    face, swap = faces(face, swap)
    resid, message = call(
        functools.partial(send_kernel, True),
        "send",
        small,
        [src, react, u, face, swap, smoo],
        [VEC, (16, 11, 8, 128)],
        [(2, 160, 128)],
    )
    recv, own, far, near = to_coarse(message, True)
    rhs_shape, bx_shape = (16, HALF, 8, 128), (7, 72, 2, 8, 128)
    u, face, swap, window = call(
        functools.partial(correct_kernel, True),
        "correct",
        small,
        [react, smoo, u, resid, own, far, near, recv],
        [VEC, FACE, SWAP, (7, CHANNELS, 8, 128)],
        [rhs_shape, bx_shape, (16, CHANNELS, 8, 128)],
    )
    face, swap = faces(face, swap)
    u, face, swap = call(
        sweep_kernel, "sweep", small, [src, react, u, face, swap, smoo], [VEC, FACE, SWAP]
    )
    face, swap = faces(face, swap)
    resid, message = call(
        functools.partial(send_kernel, False),
        "send",
        small,
        [src, react, u, face, swap],
        [VEC, (16, 9, 8, 128)],
    )
    recv, own, far, near = to_coarse(message, False)
    u, face, swap = call(
        functools.partial(correct_kernel, False),
        "correct",
        small,
        [react, smoo, u, resid, own, far, near, window],
        [VEC, FACE, SWAP],
        [rhs_shape, bx_shape],
    )
    face, swap = faces(face, swap)
    (resid,) = call(last_kernel, "last", small, [src, react, u, face, swap], [VEC])
    return u.reshape(source.shape), resid.reshape(source.shape)


def solution(mesh):
    bricks = mesh.shape["bricks"]
    gz = mesh.shape["gz"]
    inner = Mesh(mesh.devices.reshape(bricks // 4, 2, 2, gz), X_AXES + ("gz",))
    in_specs = (
        P(None, X_AXES, "gz", None),
        P(None, None, X_AXES, "gz", None),
        P(None, None, X_AXES, "gz", None),
        P(),
        P(X_AXES, "gz", None),
    )
    out_specs = (P(None, X_AXES, "gz", None), P(None, X_AXES, "gz", None))
    return jax.shard_map(
        functools.partial(local, bricks),
        mesh=inner,
        in_specs=in_specs,
        out_specs=out_specs,
        check_vma=False,
    )
```

```python
import functools

import jax
import jax.numpy as jnp
from jax import lax
from jax.experimental import pallas as pl
from jax.experimental.pallas import tpu as pltpu
from jax.sharding import Mesh
from jax.sharding import PartitionSpec as P

COMP = 12
HALF = 6
F32 = jnp.float32
BF16 = jnp.bfloat16
X_AXES = ("xg", "xc", "core")
TILE = (8, 128)
CHANNELS = 11
BRICK_TILES = 6
CENTRE = 3
VMEM_LIMIT = 16 * 1024 * 1024


def rows(shape=TILE):
    return lax.broadcasted_iota(jnp.int32, shape, 0)


def lanes(shape=TILE):
    return lax.broadcasted_iota(jnp.int32, shape, 1)


def up(x, by):
    return pltpu.roll(x, 8 - by, 0)


def down(x, by):
    return pltpu.roll(x, by, 0)


def pick(cond, a, b):
    return jnp.where(cond, a, b)


def hat(diff):
    inner = jnp.logical_or(diff == 0, diff == 1)
    outer = jnp.logical_or(diff == -1, diff == 2)
    return jnp.where(inner, 3.0, jnp.where(outer, 1.0, 0.0)).astype(F32)


def split(x, parts):
    pieces = []
    for _ in range(parts):
        piece = x.astype(BF16)
        pieces.append(piece)
        x = x - piece.astype(F32)
    return pieces


def dot(a, b):
    return jnp.dot(a, b, preferred_element_type=F32)


def dot_right(x, weights, parts=3):
    total = None
    for piece in split(x, parts):
        term = dot(piece, weights)
        total = term if total is None else total + term
    return total


def dot_left(weights, x, parts=3):
    total = None
    for piece in split(x, parts):
        term = dot(weights, piece)
        total = term if total is None else total + term
    return total


def fine_mask_of(sc_ref):
    brick = lanes() // 32
    out = jnp.zeros(TILE, F32)
    for b in range(4):
        out = jnp.where(brick == b, sc_ref[8 + b].astype(F32), out)
    return out


def packed_mask_of(sc_ref):
    brick = (lanes() % 64) // 16
    out = jnp.zeros(TILE, F32)
    for b in range(4):
        out = jnp.where(brick == b, sc_ref[8 + b].astype(F32), out)
    return out


def load(ref):
    return [ref[c] for c in range(COMP)]


def block_product(blocks_ref, vec):
    out = []
    for c in range(COMP):
        acc = None
        for d in range(0, COMP, 2):
            pair = blocks_ref[pl.ds((c * COMP + d) * 8, 16), :].astype(F32)
            term = pair[:8] * vec[d] + pair[8:] * vec[d + 1]
            acc = term if acc is None else acc + term
        out.append(acc)
    return out


def smooth(smoother_ref, mask, resid):
    prod = block_product(smoother_ref, resid)
    return [mask * a + (1.0 - mask) * r for a, r in zip(prod, resid)]


def neighbours(mv, hx, hz):
    z = rows() % 4
    lane = lanes()
    total = down(mv, 4) + hx + hz
    total = total + jnp.where(z > 0, down(mv, 1), 0.0) + jnp.where(z < 3, up(mv, 1), 0.0)
    total = total + jnp.where(lane > 0, pltpu.roll(mv, 1, 1), 0.0)
    return total + jnp.where(lane < 127, pltpu.roll(mv, 127, 1), 0.0)


def operator(reaction_ref, diff_ref, mask, vec, hx, hz):
    prod = block_product(reaction_ref, vec)
    out = []
    for c in range(COMP):
        v = vec[c]
        inner = prod[c] + diff_ref[c] * (6.0 * v - neighbours(mask * v, hx[c], hz[c]))
        out.append(mask * inner + (1.0 - mask) * v)
    return out


def x_messages(vec):
    low_half = rows() < 4
    to_high, to_low = [], []
    for j in range(HALF):
        a, b = vec[j], vec[j + HALF]
        to_high.append(jnp.where(low_half, down(a, 4), b))
        to_low.append(jnp.where(low_half, a, down(b, 4)))
    return to_high, to_low


def x_halo(low, high):
    low_half = rows() < 4
    first = [jnp.where(low_half, a, down(b, 4)) for a, b in zip(low, high)]
    second = [jnp.where(low_half, down(a, 4), b) for a, b in zip(low, high)]
    return first + second


def z_messages(vec):
    z = rows() % 4
    to_high, to_low = [], []
    for c in range(3):
        up_tile, down_tile = up(vec[c], 3), vec[c]
        for k in range(1, 4):
            t = vec[c + 3 * k]
            up_tile = jnp.where(z == k, up(t, 3 - k) if k < 3 else t, up_tile)
            down_tile = jnp.where(z == k, down(t, k), down_tile)
        to_high.append(up_tile)
        to_low.append(down_tile)
    return to_high, to_low


def z_halo(zd, low, high):
    z = rows() % 4
    has_low = jnp.logical_and(z == 0, zd > 0)
    has_high = jnp.logical_and(z == 3, zd < 3)
    out = []
    for c in range(COMP):
        k, at = c // 3, c % 3
        a = up(low[at], k) if k else low[at]
        b = down(high[at], 3 - k) if k < 3 else high[at]
        out.append(jnp.where(has_low, a, jnp.where(has_high, b, 0.0)))
    return out


def write_faces(sc_ref, mask, vec, face_ref, swap_ref):
    core, zd = sc_ref[0], sc_ref[1]
    first = core == 0
    mv = [mask * v for v in vec]
    x_high, x_low = x_messages(mv)
    z_high, z_low = z_messages(mv)
    for j in range(HALF):
        in_chip = pick(first, x_high[j], x_low[j])
        swap_ref[j] = pick(first, x_low[j], x_high[j])
        for other in range(4):
            along = pick(other > zd, z_high[j % 3], z_low[j % 3])
            face_ref[other, j] = pick(first, along, in_chip)
            face_ref[4 + other, j] = pick(first, in_chip, along)


def read_faces(sc_ref, face_ref, swap_ref):
    core, zd = sc_ref[0], sc_ref[1]
    first = core == 0
    chip_at = (1 - core) * 4 + zd
    low_at = core * 4 + jnp.maximum(zd - 1, 0)
    high_at = core * 4 + jnp.minimum(zd + 1, 3)
    low, high = [], []
    for j in range(HALF):
        chip, cross = face_ref[chip_at, j], swap_ref[j]
        low.append(pick(first, cross, chip))
        high.append(pick(first, chip, cross))
    hz = z_halo(zd, [face_ref[low_at, c] for c in range(3)], [face_ref[high_at, c] for c in range(3)])
    return x_halo(low, high), hz


def write_layers(sc_ref, mask, vec, resid, chip_ref, cross_ref):
    first = sc_ref[0] == 0
    r_high, r_low = x_messages(resid)
    v_high, v_low = x_messages([mask * v for v in vec])
    for n, (high, low) in enumerate(zip(r_high + v_high + [mask], r_low + v_low + [mask])):
        chip_ref[n] = pick(first, high, low)
        cross_ref[n] = pick(first, low, high)


def restrict(own, beside, above):
    kinds = [own, beside] + ([above] if above is not None else [])
    depth = 8 * len(kinds)
    l, o = rows((128, 128)), lanes((128, 128))
    low = jnp.where(o < 64, hat(l - 2 * o), 0.0).astype(BF16)
    high = jnp.where(o >= 64, hat(l - 2 * (o - 64)), 0.0).astype(BF16)
    a = jnp.concatenate([kind[j] for j in range(HALF) for kind in kinds], axis=0)
    b = jnp.concatenate([kind[j + HALF] for j in range(HALF) for kind in kinds], axis=0)
    along_y = (dot_right(a, low) + dot_right(b, high)) * 0.125
    blocks = [along_y[depth * j : depth * j + depth] for j in range(HALF)]
    stacked = jnp.concatenate(
        [jnp.concatenate(blocks[:3], axis=1), jnp.concatenate(blocks[3:], axis=1)], axis=0
    )
    o, k = rows((8, 2 * depth)), lanes((8, 2 * depth))
    kind, s = (k % depth) // 8, k % 8
    z = s % 4
    outer_x = jnp.where(s < 4, -1, 2)
    in_own = jnp.logical_or(z == 0, z == 3)
    x = jnp.where(kind == 0, s // 4, jnp.where(kind == 1, outer_x, jnp.where(in_own, s // 4, outer_x)))
    fine_z = jnp.where(kind == 2, jnp.where(z < 2, -1, 4), z)
    weights = hat(x) * hat(fine_z - 2 * (o % 4 - 1))
    weights = jnp.where(o // 4 == k // depth, weights, 0.0).astype(BF16)
    result = dot_left(weights, stacked) * (1.0 / 64.0)
    return [result[:, 128 * jj : 128 * jj + 128] for jj in range(3)]


def packed_blocks(smoother_ref, reaction_ref, sc_ref, sums_ref):
    l, o = rows((128, 128)), lanes((128, 128))
    weights = jnp.where(l // 32 == o % 4, 1.0 / 256.0, 0.0).astype(BF16)
    zero = jnp.zeros((16, 128), F32)
    for a, ref in enumerate((smoother_ref, reaction_ref)):
        for n in range(0, COMP * COMP, 2):
            pair = ref[pl.ds(n * 8, 16), :].astype(F32)
            sums_ref[a, pl.ds(n, 1), :] = jnp.sum(pair[:8], axis=0, keepdims=True)
            sums_ref[a, pl.ds(n + 1, 1), :] = jnp.sum(pair[8:], axis=0, keepdims=True)
        sums_ref[a, pl.ds(144, 16), :] = zero
        sums_ref[a] = dot_right(sums_ref[a], weights)
    s, lane = rows((16, 128)), lanes((16, 128))
    out = zero
    for k in range(8):
        for a in range(2):
            for half in range(2):
                part = sums_ref[a, pl.ds(72 * half + 9 * k, 16), :]
                out = jnp.where(lane // 4 == 4 * k + 2 * a + half, part, out)
    coarse = jnp.broadcast_to(packed_mask_of(sc_ref)[:1], (16, 128))
    fine = jnp.broadcast_to(fine_mask_of(sc_ref)[:1], (16, 128))
    return jnp.where(s < 9, out, jnp.where(s == 9, coarse, jnp.where(s == 10, fine, 0.0)))


def expand_channel(get_row):
    owner = rows() // 2
    out = jnp.broadcast_to(get_row(0), TILE)
    for zd in range(1, 4):
        out = jnp.where(owner == zd, jnp.broadcast_to(get_row(zd), TILE), out)
    return out


def slots_of(p):
    right = p // 2
    out = []
    for w in range(7):
        x = p - CENTRE + w
        before = jnp.where(right == 0, x + 7, 7)
        after = jnp.where(right == 1, x, 7)
        out.append(jnp.where(x < 0, before, jnp.where(x > 3, after, x)))
    return out


def coarse_product(bx_ref, which, slot, vec):
    left = lanes() < 64
    both = [None] * COMP
    for j in range(HALF):
        turned = pltpu.roll(vec[j], 64, 1)
        both[j] = jnp.where(left, vec[j], turned)
        both[j + HALF] = jnp.where(left, turned, vec[j])
    out = []
    for j in range(HALF):
        acc = None
        for d in range(COMP):
            term = bx_ref[slot, j * COMP + d, which] * both[d]
            acc = term if acc is None else acc + term
        out.append(acc)
    return out


def coarse_smooth(bx_ref, mask, slot, resid):
    prod = coarse_product(bx_ref, 0, slot, resid)
    return [mask * a + (1.0 - mask) * r for a, r in zip(prod, resid)]


def expand_blocks(win_ref, bx_ref, slots):
    flat = jnp.concatenate([win_ref[n, r] for n in slots for r in range(9)], axis=0)
    pieces = jnp.concatenate(split(flat, 2), axis=1)
    l, o = rows((256, 256)) % 128, lanes((256, 256))
    target = (o // 128) * 8 + ((o % 128) // 64) * 4 + (o % 64) // 16
    for k in range(8):
        weights = jnp.where(l == 16 * k + target, 1.0, 0.0).astype(BF16)
        out = dot(pieces, weights)
        for i, n in enumerate(slots):
            for r in range(9):
                tile = out[(i * 9 + r) * 8 : (i * 9 + r) * 8 + 8]
                bx_ref[n, 9 * k + r, 0] = tile[:, :128]
                bx_ref[n, 9 * k + r, 1] = tile[:, 128:]


def solve_coarse(diff_ref, rhs, slots, win_ref, bx_ref):
    s, lane = rows(), lanes()
    left = lane < 64
    inner_lane = lane % 64
    coeffs = [
        0.25 * jnp.where(left, jnp.full(TILE, diff_ref[j], F32), jnp.full(TILE, diff_ref[j + HALF], F32))
        for j in range(HALF)
    ]
    masks = [win_ref[slots[w], 9] for w in range(7)]
    b = [rhs(w) for w in range(7)]
    v = [coarse_smooth(bx_ref, masks[w], slots[w], b[w]) for w in range(7)]
    for edge in (1, 2):
        mv = [[masks[w] * t for t in v[w]] if v[w] is not None else None for w in range(7)]
        new = [None] * 7
        for w in range(edge, 7 - edge):
            prod = coarse_product(bx_ref, 1, slots[w], v[w])
            resid = []
            for j in range(HALF):
                t = mv[w][j]
                total = mv[w - 1][j] + mv[w + 1][j]
                total = total + jnp.where(s > 0, down(t, 1), 0.0) + jnp.where(s < 7, up(t, 1), 0.0)
                total = total + jnp.where(inner_lane > 0, pltpu.roll(t, 1, 1), 0.0)
                total = total + jnp.where(inner_lane < 63, pltpu.roll(t, 127, 1), 0.0)
                inner = prod[j] + coeffs[j] * (6.0 * v[w][j] - total)
                resid.append(b[w][j] - (masks[w] * inner + (1.0 - masks[w]) * v[w][j]))
            step = coarse_smooth(bx_ref, masks[w], slots[w], resid)
            new[w] = [x + y for x, y in zip(v[w], step)]
        v = new
    return v[2:5]


def prolong(sc_ref, q):
    zd = sc_ref[1]
    o, k = rows((24, 24)), lanes((24, 24))
    group, s = o // 8, o % 8
    z = s % 4
    fx = jnp.where(group == 1, jnp.where(s < 4, -1, 2), s // 4)
    fz = jnp.where(group == 2, jnp.where(z == 0, -1, 4), z) + 4 * zd
    weights = hat(fx - 2 * (k // 8 - 1)) * hat(fz - 2 * (k % 8))
    unused = jnp.logical_and(group == 2, jnp.logical_or(z == 1, z == 2))
    weights = jnp.where(unused, 0.0, weights * 0.0625).astype(BF16)
    stacked = jnp.concatenate([jnp.concatenate(row, axis=1) for row in q], axis=0)
    xz = dot_left(weights, stacked)
    tall = jnp.concatenate([xz[:, 128 * j : 128 * j + 128] for j in range(HALF)], axis=0)
    a, f = rows((128, 256)), lanes((128, 256))
    along = hat(f % 128 - 2 * (a % 64)) * 0.25
    along = jnp.where(a // 64 == f // 128, along, 0.0).astype(BF16)
    fine = dot_right(tall, along)
    groups = []
    for g in range(3):
        tiles = [fine[24 * j + 8 * g : 24 * j + 8 * g + 8] for j in range(HALF)]
        groups.append([t[:, :128] for t in tiles] + [t[:, 128:] for t in tiles])
    return groups


def masks_around(zd, tile):
    own = pltpu.roll(tile, lax.rem(8 - 2 * zd, 8), 0)
    return own[7:8], own[:1], own[2:3]


def outside_masks(zd, tiles):
    s = rows()
    z = s % 4
    _, low_x, _ = masks_around(zd, tiles[0])
    low_z, _, high_z = masks_around(zd, tiles[1])
    _, high_x, _ = masks_around(zd, tiles[2])
    mask_x = jnp.where(s < 4, jnp.broadcast_to(low_x, TILE), jnp.broadcast_to(high_x, TILE))
    mask_z = jnp.where(
        jnp.logical_and(z == 0, zd > 0),
        jnp.broadcast_to(low_z, TILE),
        jnp.where(jnp.logical_and(z == 3, zd < 3), jnp.broadcast_to(high_z, TILE), 0.0),
    )
    return mask_x, mask_z


def layer_masks(zd, tiles):
    s = rows()
    z = s % 4
    around = [masks_around(zd, tile) for tile in tiles]
    below = [jnp.broadcast_to(a[0], TILE) for a in around]
    above = [jnp.broadcast_to(a[2], TILE) for a in around]
    low = jnp.where(z == 0, below[1], jnp.where(s < 4, below[0], below[2]))
    high = jnp.where(z == 3, above[1], jnp.where(s < 4, above[0], above[2]))
    low = jnp.where(zd > 0, low, 0.0)
    high = jnp.where(zd < 3, high, 0.0)
    return jnp.where(z < 2, low, high)


ZEROS = [0.0] * COMP


def first_kernel(sc_ref, src_ref, smoother_ref, u_ref, z_ref):
    mask = fine_mask_of(sc_ref)
    zd = sc_ref[1]
    u = smooth(smoother_ref, mask, load(src_ref))
    for c in range(COMP):
        u_ref[c] = u[c]
    high, low = z_messages([mask * v for v in u])
    for other in range(4):
        for n in range(3):
            z_ref[other, n] = pick(other > zd, high[n], low[n])


def blocks_kernel(sc_ref, smoother_ref, reaction_ref, out_ref, sums_ref):
    packed = packed_blocks(smoother_ref, reaction_ref, sc_ref, sums_ref)
    out_ref[0] = packed[:8]
    out_ref[1] = packed[8:]


def part_kernel(
    sc_ref, diff_ref, src_ref, reaction_ref, u_ref, z_ref, r_ref, chip_ref, cross_ref
):
    mask = fine_mask_of(sc_ref)
    zd = sc_ref[1]
    u = load(u_ref)
    below, above = jnp.maximum(zd - 1, 0), jnp.minimum(zd + 1, 3)
    hz = z_halo(zd, [z_ref[below, n] for n in range(3)], [z_ref[above, n] for n in range(3)])
    au = operator(reaction_ref, diff_ref, mask, u, ZEROS, hz)
    resid = [src_ref[c] - au[c] for c in range(COMP)]
    for c in range(COMP):
        r_ref[c] = resid[c]
    write_layers(sc_ref, mask, u, resid, chip_ref, cross_ref)


def send_kernel(
    again, sc_ref, diff_ref, u_ref, part_ref, chip_ref, cross_ref, extra_ref, r_ref, out_ref
):
    mask = fine_mask_of(sc_ref)
    zd = sc_ref[1]
    first = sc_ref[0] == 0
    low = [pick(first, cross_ref[n], chip_ref[n]) for n in range(13)]
    high = [pick(first, chip_ref[n], cross_ref[n]) for n in range(13)]
    hr = x_halo(low[:6], high[:6])
    hv = x_halo(low[6:12], high[6:12])
    mask_x = jnp.where(rows() < 4, low[12], high[12])
    mv = [mask * u_ref[c] for c in range(COMP)]
    own = [part_ref[c] + mask * (diff_ref[c] * hv[c]) for c in range(COMP)]
    beside = [hr[c] + mask_x * (diff_ref[c] * mv[c]) for c in range(COMP)]
    for c in range(COMP):
        r_ref[c] = own[c]
    above = None
    if again:
        z = rows() % 4
        inner = jnp.logical_or(z == 0, z == 3)
        edge = layer_masks(zd, [extra_ref[n] for n in range(3)])
        above = []
        for c in range(COMP):
            outer = jnp.where(z == 1, down(hv[c], 1), up(hv[c], 1))
            above.append(edge * (diff_ref[c] * jnp.where(inner, mv[c], outer)))
    tiles = restrict(own, beside, above)
    if not again:
        tiles = tiles + [extra_ref[0], extra_ref[1]]
    for n, tile in enumerate(tiles):
        for target in range(16):
            out_ref[target, n] = tile
    if again:
        z_high, z_low = z_messages(mv)
        for n in range(3):
            for other in range(4):
                tile = pick(other > zd, z_high[n], z_low[n])
                for q in range(4):
                    out_ref[q * 4 + other, 3 + n] = tile


def gather_kernel(with_blocks, sc_ref, recv_ref, own_ref, far_ref, near_ref):
    right = sc_ref[2] // 2
    s = rows()
    low_half = s < 4
    for q in range(4):
        for jj in range(3):
            m0, m1, m2, m3 = [recv_ref[q * 4 + zd, jj] for zd in range(4)]
            even = (jnp.where(low_half, m0, down(m2, 4)), jnp.where(low_half, down(m0, 4), m2))
            odd = (jnp.where(low_half, m1, down(m3, 4)), jnp.where(low_half, down(m1, 4), m3))
            for n in range(2):
                own_ref[q, jj + 3 * n] = jnp.where(s < 7, up(even[n], 1), 0.0) + jnp.where(
                    s > 0, down(odd[n], 1), 0.0
                )
    for e in range(3):
        for j in range(HALF):
            far_ref[e * 6 + j] = own_ref[right + e, j]
    for j in range(HALF):
        near_ref[j] = own_ref[3 * right, j]
    if with_blocks:
        for n in range(BRICK_TILES):
            for e in range(3):
                far_ref[18 + e * BRICK_TILES + n] = brick_tile(recv_ref, right + e, n)
            near_ref[6 + n] = brick_tile(recv_ref, 3 * right, n)


def brick_tile(recv_ref, q, n):
    s = rows()
    out = None
    for at in range(8):
        r = 2 * n + at // 4
        row = recv_ref[q * 4 + at % 4, 3 + r // 8, pl.ds(r % 8, 1), :]
        row = jnp.broadcast_to(row, TILE)
        out = row if out is None else jnp.where(s == at, row, out)
    return out


def fill_own(recv_ref, win_ref):
    for r in range(CHANNELS):
        at, tile = pl.ds(r % 8, 1), r // 8
        for q in range(4):
            win_ref[q, r] = expand_channel(lambda zd: recv_ref[q * 4 + zd, 3 + tile, at, :])


def fill_others(far_ref, near_ref, win_ref):
    for r in range(CHANNELS):
        tile, base = r // 2, 4 * (r % 2)
        for e in range(3):
            win_ref[4 + e, r] = expand_channel(
                lambda zd: far_ref[18 + e * BRICK_TILES + tile, pl.ds(base + zd, 1), :]
            )
        win_ref[7, r] = expand_channel(lambda zd: near_ref[6 + tile, pl.ds(base + zd, 1), :])


def correct_kernel(
    again,
    sc_ref,
    diff_ref,
    reaction_ref,
    smoother_ref,
    u_ref,
    r_ref,
    recv_ref,
    own_ref,
    far_ref,
    near_ref,
    *rest,
):
    zd, p, brick, bricks = sc_ref[1], sc_ref[2], sc_ref[3], sc_ref[4]
    if again:
        win_ref, new_ref, face_ref, swap_ref, rhs_ref, bx_ref = rest
    else:
        new_ref, face_ref, swap_ref, win_ref, around_ref, rhs_ref, bx_ref = rest
        fill_own(recv_ref, win_ref)
        fill_others(far_ref, near_ref, win_ref)
    expand_blocks(win_ref, bx_ref, range(8))
    slots = slots_of(p)
    for j in range(HALF):
        for q in range(4):
            rhs_ref[q, j] = own_ref[q, j]
        for e in range(3):
            rhs_ref[4 + e, j] = far_ref[e * 6 + j]
        rhs_ref[7, j] = near_ref[j]

    def rhs(w):
        place = brick + (w - CENTRE)
        inside = jnp.logical_and(place >= 0, place < bricks)
        return [pick(inside, rhs_ref[slots[w], j], 0.0) for j in range(HALF)]

    q = solve_coarse(diff_ref, rhs, slots, win_ref, bx_ref)
    inside, hx, hz = prolong(sc_ref, q)
    fine_masks = [win_ref[slots[CENTRE + n], 10] for n in (-1, 0, 1)]
    if not again:
        for n in range(3):
            around_ref[n] = fine_masks[n]
    mask_x, mask_z = outside_masks(zd, fine_masks)
    hx = [mask_x * t for t in hx]
    hz = [mask_z * t for t in hz]
    mask = fine_mask_of(sc_ref)
    change = operator(reaction_ref, diff_ref, mask, inside, hx, hz)
    resid = [r_ref[c] - change[c] for c in range(COMP)]
    if again:
        below = p * 4 + jnp.maximum(zd - 1, 0)
        above = p * 4 + jnp.minimum(zd + 1, 3)
        halo = z_halo(
            zd, [recv_ref[below, 3 + n] for n in range(3)], [recv_ref[above, 3 + n] for n in range(3)]
        )
        resid = [r + mask * (diff_ref[c] * h) for c, (r, h) in enumerate(zip(resid, halo))]
    step = smooth(smoother_ref, mask, resid)
    new = [u_ref[c] + inside[c] + step[c] for c in range(COMP)]
    for c in range(COMP):
        new_ref[c] = new[c]
    write_faces(sc_ref, mask, new, face_ref, swap_ref)


def residual(sc_ref, diff_ref, src_ref, reaction_ref, u_ref, face_ref, swap_ref):
    mask = fine_mask_of(sc_ref)
    u = load(u_ref)
    hx, hz = read_faces(sc_ref, face_ref, swap_ref)
    au = operator(reaction_ref, diff_ref, mask, u, hx, hz)
    return mask, u, [src_ref[c] - au[c] for c in range(COMP)]


def sweep_kernel(
    sc_ref, diff_ref, src_ref, reaction_ref, u_ref, face_ref, swap_ref, smoother_ref,
    new_ref, part_ref, chip_ref, cross_ref,
):
    mask, u, resid = residual(
        sc_ref, diff_ref, src_ref, reaction_ref, u_ref, face_ref, swap_ref
    )
    step = smooth(smoother_ref, mask, resid)
    new = [a + b for a, b in zip(u, step)]
    au = operator(reaction_ref, diff_ref, mask, new, ZEROS, ZEROS)
    part = [src_ref[c] - au[c] for c in range(COMP)]
    for c in range(COMP):
        new_ref[c] = new[c]
        part_ref[c] = part[c]
    write_layers(sc_ref, mask, new, part, chip_ref, cross_ref)


def last_kernel(
    sc_ref, diff_ref, src_ref, reaction_ref, u_ref, face_ref, swap_ref, r_ref
):
    _, _, resid = residual(
        sc_ref, diff_ref, src_ref, reaction_ref, u_ref, face_ref, swap_ref
    )
    for c in range(COMP):
        r_ref[c] = resid[c]


SMEM_SPEC = pl.BlockSpec(memory_space=pltpu.SMEM)
VMEM_SPEC = pl.BlockSpec(memory_space=pltpu.VMEM)


def call(kernel, name, scalars, arrays, outs, scratch=()):
    return pl.pallas_call(
        kernel,
        name=name,
        in_specs=[SMEM_SPEC] * len(scalars) + [VMEM_SPEC] * len(arrays),
        out_specs=[VMEM_SPEC] * len(outs),
        out_shape=[jax.ShapeDtypeStruct(shape, F32) for shape in outs],
        scratch_shapes=[pltpu.VMEM(shape, F32) for shape in scratch],
        compiler_params=pltpu.CompilerParams(vmem_limit_bytes=VMEM_LIMIT),
    )(*scalars, *arrays)


VEC = (COMP, 8, 128)
FACE = (8, HALF, 8, 128)
SWAP = (HALF, 8, 128)
LAYER = (13, 8, 128)


def local(bricks, source, reaction, smoother, diffusion, active):
    core = lax.axis_index("core")
    zd = lax.axis_index("gz")
    brick = lax.axis_index(X_AXES)
    scalars = jnp.stack(
        [core, zd, brick % 4, brick, jnp.int32(bricks), core, core, core]
    ).astype(jnp.int32)
    scalars = jnp.concatenate([scalars, active.reshape(4)])
    src = source.reshape(VEC)
    react = reaction.reshape(COMP * COMP * 8, 128)
    smoo = smoother.reshape(COMP * COMP * 8, 128)
    groups = bricks // 4

    chip_pairs = [(i, i ^ 1) for i in range(bricks)]
    pairs = [(i, i + 1) for i in range(1, bricks - 1, 2)]
    swap_pairs = pairs + [(b, a) for a, b in pairs]
    far_pairs, near_pairs = [], []
    for i in range(bricks):
        g, p = divmod(i, 4)
        step = 1 if p >= 2 else -1
        if 0 <= g + step < groups:
            far_pairs.append((i, 4 * (g + step) + 3 - p))
            if p in (1, 2):
                near_pairs.append((i, i + 4 * step))

    def faces(face, swap):
        swap = lax.ppermute(swap, X_AXES, swap_pairs)
        face = lax.all_to_all(face, ("core", "gz"), 0, 0)
        return face, swap

    def layers(chip, cross):
        return lax.ppermute(chip, X_AXES, chip_pairs), lax.ppermute(cross, X_AXES, swap_pairs)

    def to_coarse(message, with_blocks):
        recv = lax.all_to_all(message, ("xc", "core", "gz"), 0, 0)
        far_rows, near_rows = (18 + 3 * BRICK_TILES, 6 + BRICK_TILES) if with_blocks else (18, 6)
        own, far, near = call(
            functools.partial(gather_kernel, with_blocks),
            "gather",
            [scalars],
            [recv],
            [(4, HALF, 8, 128), (far_rows, 8, 128), (near_rows, 8, 128)],
        )
        far = lax.ppermute(far, X_AXES, far_pairs)
        near = lax.ppermute(near, X_AXES, near_pairs)
        return recv, own, far, near

    small = [scalars, diffusion]
    u, edges = call(first_kernel, "first", [scalars], [src, smoo], [VEC, (4, 3, 8, 128)])
    (packed,) = call(blocks_kernel, "blocks", [scalars], [smoo, react], [(2, 8, 128)], [(2, 160, 128)])
    edges = lax.all_to_all(edges, "gz", 0, 0)
    part, chip, cross = call(
        part_kernel, "part", small, [src, react, u, edges], [VEC, LAYER, LAYER]
    )
    chip, cross = layers(chip, cross)
    resid, message = call(
        functools.partial(send_kernel, False),
        "send",
        small,
        [u, part, chip, cross, packed],
        [VEC, (16, 5, 8, 128)],
    )
    recv, own, far, near = to_coarse(message, True)
    rhs_shape, bx_shape, win_shape = (8, HALF, 8, 128), (8, 72, 2, 8, 128), (8, CHANNELS, 8, 128)
    u, face, swap, window, around = call(
        functools.partial(correct_kernel, False),
        "correct",
        small,
        [react, smoo, u, resid, recv, own, far, near],
        [VEC, FACE, SWAP, win_shape, (3, 8, 128)],
        [rhs_shape, bx_shape],
    )
    face, swap = faces(face, swap)
    u, part, chip, cross = call(
        sweep_kernel, "sweep", small, [src, react, u, face, swap, smoo], [VEC, VEC, LAYER, LAYER]
    )
    chip, cross = layers(chip, cross)
    resid, message = call(
        functools.partial(send_kernel, True),
        "send",
        small,
        [u, part, chip, cross, around],
        [VEC, (16, 6, 8, 128)],
    )
    recv, own, far, near = to_coarse(message, False)
    u, face, swap = call(
        functools.partial(correct_kernel, True),
        "correct",
        small,
        [react, smoo, u, resid, recv, own, far, near, window],
        [VEC, FACE, SWAP],
        [rhs_shape, bx_shape],
    )
    face, swap = faces(face, swap)
    (resid,) = call(last_kernel, "last", small, [src, react, u, face, swap], [VEC])
    return u.reshape(source.shape), resid.reshape(source.shape)


def solution(mesh):
    bricks = mesh.shape["bricks"]
    gz = mesh.shape["gz"]
    inner = Mesh(mesh.devices.reshape(bricks // 4, 2, 2, gz), X_AXES + ("gz",))
    in_specs = (
        P(None, X_AXES, "gz", None),
        P(None, None, X_AXES, "gz", None),
        P(None, None, X_AXES, "gz", None),
        P(),
        P(X_AXES, "gz", None),
    )
    out_specs = (P(None, X_AXES, "gz", None), P(None, X_AXES, "gz", None))
    return jax.shard_map(
        functools.partial(local, bricks),
        mesh=inner,
        in_specs=in_specs,
        out_specs=out_specs,
        check_vma=False,
    )
```

```python
import functools

import jax
import jax.numpy as jnp
from jax import lax
from jax.experimental import pallas as pl
from jax.experimental.pallas import tpu as pltpu
from jax.sharding import Mesh
from jax.sharding import PartitionSpec as P

COMP = 12
HALF = 6
F32 = jnp.float32
BF16 = jnp.bfloat16
X_AXES = ("xg", "xc", "core")
TILE = (8, 128)
CHANNELS = 11
BRICK_TILES = 6
CENTRE = 3
VMEM_LIMIT = 16 * 1024 * 1024


def rows(shape=TILE):
    return lax.broadcasted_iota(jnp.int32, shape, 0)


def lanes(shape=TILE):
    return lax.broadcasted_iota(jnp.int32, shape, 1)


def up(x, by):
    return pltpu.roll(x, 8 - by, 0)


def down(x, by):
    return pltpu.roll(x, by, 0)


def pick(cond, a, b):
    return jnp.where(cond, a, b)


def hat(diff):
    inner = jnp.logical_or(diff == 0, diff == 1)
    outer = jnp.logical_or(diff == -1, diff == 2)
    return jnp.where(inner, 3.0, jnp.where(outer, 1.0, 0.0)).astype(F32)


def split(x, parts):
    pieces = []
    for _ in range(parts):
        piece = x.astype(BF16)
        pieces.append(piece)
        x = x - piece.astype(F32)
    return pieces


def dot(a, b):
    return jnp.dot(a, b, preferred_element_type=F32)


def dot_right(x, weights, parts=3):
    total = None
    for piece in split(x, parts):
        term = dot(piece, weights)
        total = term if total is None else total + term
    return total


def dot_left(weights, x, parts=3):
    total = None
    for piece in split(x, parts):
        term = dot(weights, piece)
        total = term if total is None else total + term
    return total


def fine_mask_of(here):
    brick = lanes() // 32
    out = jnp.zeros(TILE, F32)
    for b in range(4):
        out = jnp.where(brick == b, here[5 + b], out)
    return out


def packed_mask_of(here):
    brick = (lanes() % 64) // 16
    out = jnp.zeros(TILE, F32)
    for b in range(4):
        out = jnp.where(brick == b, here[5 + b], out)
    return out


def load(ref):
    return [ref[c] for c in range(COMP)]


def block_product(blocks_ref, vec):
    out = []
    for c in range(COMP):
        acc = None
        for d in range(0, COMP, 2):
            pair = blocks_ref[pl.ds((c * COMP + d) * 8, 16), :].astype(F32)
            term = pair[:8] * vec[d] + pair[8:] * vec[d + 1]
            acc = term if acc is None else acc + term
        out.append(acc)
    return out


def smooth(smoother_ref, mask, resid):
    prod = block_product(smoother_ref, resid)
    return [mask * a + (1.0 - mask) * r for a, r in zip(prod, resid)]


def neighbours(mv, hx, hz):
    z = rows() % 4
    lane = lanes()
    total = down(mv, 4) + hx + hz
    total = total + jnp.where(z > 0, down(mv, 1), 0.0) + jnp.where(z < 3, up(mv, 1), 0.0)
    total = total + jnp.where(lane > 0, pltpu.roll(mv, 1, 1), 0.0)
    return total + jnp.where(lane < 127, pltpu.roll(mv, 127, 1), 0.0)


def operator(reaction_ref, diff_ref, mask, vec, hx, hz):
    prod = block_product(reaction_ref, vec)
    out = []
    for c in range(COMP):
        v = vec[c]
        inner = prod[c] + diff_ref[c] * (6.0 * v - neighbours(mask * v, hx[c], hz[c]))
        out.append(mask * inner + (1.0 - mask) * v)
    return out


def x_messages(vec):
    low_half = rows() < 4
    to_high, to_low = [], []
    for j in range(HALF):
        a, b = vec[j], vec[j + HALF]
        to_high.append(jnp.where(low_half, down(a, 4), b))
        to_low.append(jnp.where(low_half, a, down(b, 4)))
    return to_high, to_low


def x_halo(low, high):
    low_half = rows() < 4
    first = [jnp.where(low_half, a, down(b, 4)) for a, b in zip(low, high)]
    second = [jnp.where(low_half, down(a, 4), b) for a, b in zip(low, high)]
    return first + second


def z_messages(vec):
    z = rows() % 4
    to_high, to_low = [], []
    for c in range(3):
        up_tile, down_tile = up(vec[c], 3), vec[c]
        for k in range(1, 4):
            t = vec[c + 3 * k]
            up_tile = jnp.where(z == k, up(t, 3 - k) if k < 3 else t, up_tile)
            down_tile = jnp.where(z == k, down(t, k), down_tile)
        to_high.append(up_tile)
        to_low.append(down_tile)
    return to_high, to_low


def z_halo(zd, low, high):
    z = rows() % 4
    has_low = jnp.logical_and(z == 0, zd > 0)
    has_high = jnp.logical_and(z == 3, zd < 3)
    out = []
    for c in range(COMP):
        k, at = c // 3, c % 3
        a = up(low[at], k) if k else low[at]
        b = down(high[at], 3 - k) if k < 3 else high[at]
        out.append(jnp.where(has_low, a, jnp.where(has_high, b, 0.0)))
    return out


def write_faces(here, mask, vec, face_ref, swap_ref):
    core, zd = here[0], here[1]
    first = core == 0
    mv = [mask * v for v in vec]
    x_high, x_low = x_messages(mv)
    z_high, z_low = z_messages(mv)
    for j in range(HALF):
        in_chip = pick(first, x_high[j], x_low[j])
        swap_ref[j] = pick(first, x_low[j], x_high[j])
        for other in range(4):
            along = pick(other > zd, z_high[j % 3], z_low[j % 3])
            face_ref[other, j] = pick(first, along, in_chip)
            face_ref[4 + other, j] = pick(first, in_chip, along)


def read_faces(here, face_ref, swap_ref):
    core, zd = here[0], here[1]
    first = core == 0
    chip_at = (1 - core) * 4 + zd
    low_at = core * 4 + jnp.maximum(zd - 1, 0)
    high_at = core * 4 + jnp.minimum(zd + 1, 3)
    low, high = [], []
    for j in range(HALF):
        chip, cross = face_ref[chip_at, j], swap_ref[j]
        low.append(pick(first, cross, chip))
        high.append(pick(first, chip, cross))
    hz = z_halo(zd, [face_ref[low_at, c] for c in range(3)], [face_ref[high_at, c] for c in range(3)])
    return x_halo(low, high), hz


def write_layers(here, mask, vec, resid, chip_ref, cross_ref):
    first = here[0] == 0
    r_high, r_low = x_messages(resid)
    v_high, v_low = x_messages([mask * v for v in vec])
    for n, (high, low) in enumerate(zip(r_high + v_high + [mask], r_low + v_low + [mask])):
        chip_ref[n] = pick(first, high, low)
        cross_ref[n] = pick(first, low, high)


def restrict(own, beside, above):
    kinds = [own, beside] + ([above] if above is not None else [])
    depth = 8 * len(kinds)
    l, o = rows((128, 128)), lanes((128, 128))
    low = jnp.where(o < 64, hat(l - 2 * o), 0.0).astype(BF16)
    high = jnp.where(o >= 64, hat(l - 2 * (o - 64)), 0.0).astype(BF16)
    a = jnp.concatenate([kind[j] for j in range(HALF) for kind in kinds], axis=0)
    b = jnp.concatenate([kind[j + HALF] for j in range(HALF) for kind in kinds], axis=0)
    along_y = (dot_right(a, low) + dot_right(b, high)) * 0.125
    blocks = [along_y[depth * j : depth * j + depth] for j in range(HALF)]
    stacked = jnp.concatenate(
        [jnp.concatenate(blocks[:3], axis=1), jnp.concatenate(blocks[3:], axis=1)], axis=0
    )
    o, k = rows((8, 2 * depth)), lanes((8, 2 * depth))
    kind, s = (k % depth) // 8, k % 8
    z = s % 4
    outer_x = jnp.where(s < 4, -1, 2)
    in_own = jnp.logical_or(z == 0, z == 3)
    x = jnp.where(kind == 0, s // 4, jnp.where(kind == 1, outer_x, jnp.where(in_own, s // 4, outer_x)))
    fine_z = jnp.where(kind == 2, jnp.where(z < 2, -1, 4), z)
    weights = hat(x) * hat(fine_z - 2 * (o % 4 - 1))
    weights = jnp.where(o // 4 == k // depth, weights, 0.0).astype(BF16)
    result = dot_left(weights, stacked) * (1.0 / 64.0)
    return [result[:, 128 * jj : 128 * jj + 128] for jj in range(3)]


def packed_blocks(smoother_ref, reaction_ref, here, sums_ref):
    l, o = rows((128, 128)), lanes((128, 128))
    weights = jnp.where(l // 32 == o % 4, 1.0 / 256.0, 0.0).astype(BF16)
    zero = jnp.zeros((16, 128), F32)
    for a, ref in enumerate((smoother_ref, reaction_ref)):
        for n in range(0, COMP * COMP, 2):
            pair = ref[pl.ds(n * 8, 16), :].astype(F32)
            sums_ref[a, pl.ds(n, 1), :] = jnp.sum(pair[:8], axis=0, keepdims=True)
            sums_ref[a, pl.ds(n + 1, 1), :] = jnp.sum(pair[8:], axis=0, keepdims=True)
        sums_ref[a, pl.ds(144, 16), :] = zero
        sums_ref[a] = dot_right(sums_ref[a], weights)
    s, lane = rows((16, 128)), lanes((16, 128))
    out = zero
    for k in range(8):
        for a in range(2):
            for half in range(2):
                part = sums_ref[a, pl.ds(72 * half + 9 * k, 16), :]
                out = jnp.where(lane // 4 == 4 * k + 2 * a + half, part, out)
    coarse = jnp.broadcast_to(packed_mask_of(here)[:1], (16, 128))
    fine = jnp.broadcast_to(fine_mask_of(here)[:1], (16, 128))
    return jnp.where(s < 9, out, jnp.where(s == 9, coarse, jnp.where(s == 10, fine, 0.0)))


def expand_channel(get_row):
    owner = rows() // 2
    out = jnp.broadcast_to(get_row(0), TILE)
    for zd in range(1, 4):
        out = jnp.where(owner == zd, jnp.broadcast_to(get_row(zd), TILE), out)
    return out


def slots_of(p):
    right = p // 2
    out = []
    for w in range(7):
        x = p - CENTRE + w
        before = jnp.where(right == 0, x + 7, 7)
        after = jnp.where(right == 1, x, 7)
        out.append(jnp.where(x < 0, before, jnp.where(x > 3, after, x)))
    return out


def coarse_product(bx_ref, which, slot, vec):
    left = lanes() < 64
    both = [None] * COMP
    for j in range(HALF):
        turned = pltpu.roll(vec[j], 64, 1)
        both[j] = jnp.where(left, vec[j], turned)
        both[j + HALF] = jnp.where(left, turned, vec[j])
    out = []
    for j in range(HALF):
        acc = None
        for d in range(COMP):
            term = bx_ref[slot, j * COMP + d, which] * both[d]
            acc = term if acc is None else acc + term
        out.append(acc)
    return out


def coarse_smooth(bx_ref, mask, slot, resid):
    prod = coarse_product(bx_ref, 0, slot, resid)
    return [mask * a + (1.0 - mask) * r for a, r in zip(prod, resid)]


def expand_blocks(win_ref, bx_ref, slots):
    flat = jnp.concatenate([win_ref[n, r] for n in slots for r in range(9)], axis=0)
    pieces = jnp.concatenate(split(flat, 2), axis=1)
    l, o = rows((256, 256)) % 128, lanes((256, 256))
    target = (o // 128) * 8 + ((o % 128) // 64) * 4 + (o % 64) // 16
    for k in range(8):
        weights = jnp.where(l == 16 * k + target, 1.0, 0.0).astype(BF16)
        out = dot(pieces, weights)
        for i, n in enumerate(slots):
            for r in range(9):
                tile = out[(i * 9 + r) * 8 : (i * 9 + r) * 8 + 8]
                bx_ref[n, 9 * k + r, 0] = tile[:, :128]
                bx_ref[n, 9 * k + r, 1] = tile[:, 128:]


def solve_coarse(diff_ref, rhs, slots, win_ref, bx_ref):
    s, lane = rows(), lanes()
    left = lane < 64
    inner_lane = lane % 64
    coeffs = [
        0.25 * jnp.where(left, diff_ref[j], diff_ref[j + HALF])
        for j in range(HALF)
    ]
    masks = [win_ref[slots[w], 9] for w in range(7)]
    b = [rhs(w) for w in range(7)]
    v = [coarse_smooth(bx_ref, masks[w], slots[w], b[w]) for w in range(7)]
    for edge in (1, 2):
        mv = [[masks[w] * t for t in v[w]] if v[w] is not None else None for w in range(7)]
        new = [None] * 7
        for w in range(edge, 7 - edge):
            prod = coarse_product(bx_ref, 1, slots[w], v[w])
            resid = []
            for j in range(HALF):
                t = mv[w][j]
                total = mv[w - 1][j] + mv[w + 1][j]
                total = total + jnp.where(s > 0, down(t, 1), 0.0) + jnp.where(s < 7, up(t, 1), 0.0)
                total = total + jnp.where(inner_lane > 0, pltpu.roll(t, 1, 1), 0.0)
                total = total + jnp.where(inner_lane < 63, pltpu.roll(t, 127, 1), 0.0)
                inner = prod[j] + coeffs[j] * (6.0 * v[w][j] - total)
                resid.append(b[w][j] - (masks[w] * inner + (1.0 - masks[w]) * v[w][j]))
            step = coarse_smooth(bx_ref, masks[w], slots[w], resid)
            new[w] = [x + y for x, y in zip(v[w], step)]
        v = new
    return v[2:5]


def prolong(here, q):
    zd = here[1]
    o, k = rows((24, 24)), lanes((24, 24))
    group, s = o // 8, o % 8
    z = s % 4
    fx = jnp.where(group == 1, jnp.where(s < 4, -1, 2), s // 4)
    fz = jnp.where(group == 2, jnp.where(z == 0, -1, 4), z) + 4 * zd
    weights = hat(fx - 2 * (k // 8 - 1)) * hat(fz - 2 * (k % 8))
    unused = jnp.logical_and(group == 2, jnp.logical_or(z == 1, z == 2))
    weights = jnp.where(unused, 0.0, weights * 0.0625).astype(BF16)
    stacked = jnp.concatenate([jnp.concatenate(row, axis=1) for row in q], axis=0)
    xz = dot_left(weights, stacked)
    tall = jnp.concatenate([xz[:, 128 * j : 128 * j + 128] for j in range(HALF)], axis=0)
    a, f = rows((128, 256)), lanes((128, 256))
    along = hat(f % 128 - 2 * (a % 64)) * 0.25
    along = jnp.where(a // 64 == f // 128, along, 0.0).astype(BF16)
    fine = dot_right(tall, along)
    groups = []
    for g in range(3):
        tiles = [fine[24 * j + 8 * g : 24 * j + 8 * g + 8] for j in range(HALF)]
        groups.append([t[:, :128] for t in tiles] + [t[:, 128:] for t in tiles])
    return groups


def masks_around(zd, tile):
    own = pltpu.roll(tile, lax.rem(8 - 2 * zd, 8), 0)
    return own[7:8], own[:1], own[2:3]


def outside_masks(zd, tiles):
    s = rows()
    z = s % 4
    _, low_x, _ = masks_around(zd, tiles[0])
    low_z, _, high_z = masks_around(zd, tiles[1])
    _, high_x, _ = masks_around(zd, tiles[2])
    mask_x = jnp.where(s < 4, jnp.broadcast_to(low_x, TILE), jnp.broadcast_to(high_x, TILE))
    mask_z = jnp.where(
        jnp.logical_and(z == 0, zd > 0),
        jnp.broadcast_to(low_z, TILE),
        jnp.where(jnp.logical_and(z == 3, zd < 3), jnp.broadcast_to(high_z, TILE), 0.0),
    )
    return mask_x, mask_z


def layer_masks(zd, tiles):
    s = rows()
    z = s % 4
    around = [masks_around(zd, tile) for tile in tiles]
    below = [jnp.broadcast_to(a[0], TILE) for a in around]
    above = [jnp.broadcast_to(a[2], TILE) for a in around]
    low = jnp.where(z == 0, below[1], jnp.where(s < 4, below[0], below[2]))
    high = jnp.where(z == 3, above[1], jnp.where(s < 4, above[0], above[2]))
    low = jnp.where(zd > 0, low, 0.0)
    high = jnp.where(zd < 3, high, 0.0)
    return jnp.where(z < 2, low, high)


ZEROS = [0.0] * COMP


def first_kernel(here, src_ref, smoother_ref, u_ref, z_ref):
    mask = fine_mask_of(here)
    zd = here[1]
    u = smooth(smoother_ref, mask, load(src_ref))
    for c in range(COMP):
        u_ref[c] = u[c]
    high, low = z_messages([mask * v for v in u])
    for other in range(4):
        for n in range(3):
            z_ref[other, n] = pick(other > zd, high[n], low[n])


def blocks_kernel(here, smoother_ref, reaction_ref, out_ref, sums_ref):
    packed = packed_blocks(smoother_ref, reaction_ref, here, sums_ref)
    out_ref[0] = packed[:8]
    out_ref[1] = packed[8:]


def part_kernel(
    here, diff_ref, src_ref, reaction_ref, u_ref, z_ref, r_ref, chip_ref, cross_ref
):
    mask = fine_mask_of(here)
    zd = here[1]
    u = load(u_ref)
    below, above = jnp.maximum(zd - 1, 0), jnp.minimum(zd + 1, 3)
    hz = z_halo(zd, [z_ref[below, n] for n in range(3)], [z_ref[above, n] for n in range(3)])
    au = operator(reaction_ref, diff_ref, mask, u, ZEROS, hz)
    resid = [src_ref[c] - au[c] for c in range(COMP)]
    for c in range(COMP):
        r_ref[c] = resid[c]
    write_layers(here, mask, u, resid, chip_ref, cross_ref)


def send_kernel(
    again, here, diff_ref, u_ref, part_ref, chip_ref, cross_ref, extra_ref, r_ref, out_ref
):
    mask = fine_mask_of(here)
    zd = here[1]
    first = here[0] == 0
    low = [pick(first, cross_ref[n], chip_ref[n]) for n in range(13)]
    high = [pick(first, chip_ref[n], cross_ref[n]) for n in range(13)]
    hr = x_halo(low[:6], high[:6])
    hv = x_halo(low[6:12], high[6:12])
    mask_x = jnp.where(rows() < 4, low[12], high[12])
    mv = [mask * u_ref[c] for c in range(COMP)]
    own = [part_ref[c] + mask * (diff_ref[c] * hv[c]) for c in range(COMP)]
    beside = [hr[c] + mask_x * (diff_ref[c] * mv[c]) for c in range(COMP)]
    for c in range(COMP):
        r_ref[c] = own[c]
    above = None
    if again:
        z = rows() % 4
        inner = jnp.logical_or(z == 0, z == 3)
        edge = layer_masks(zd, [extra_ref[n] for n in range(3)])
        above = []
        for c in range(COMP):
            outer = jnp.where(z == 1, down(hv[c], 1), up(hv[c], 1))
            above.append(edge * (diff_ref[c] * jnp.where(inner, mv[c], outer)))
    tiles = restrict(own, beside, above)
    if not again:
        tiles = tiles + [extra_ref[0], extra_ref[1]]
    for n, tile in enumerate(tiles):
        for target in range(16):
            out_ref[target, n] = tile
    if again:
        z_high, z_low = z_messages(mv)
        for n in range(3):
            for other in range(4):
                tile = pick(other > zd, z_high[n], z_low[n])
                for q in range(4):
                    out_ref[q * 4 + other, 3 + n] = tile


def gather_kernel(with_blocks, here, recv_ref, own_ref, far_ref, near_ref):
    right = here[2] // 2
    s = rows()
    low_half = s < 4
    for q in range(4):
        for jj in range(3):
            m0, m1, m2, m3 = [recv_ref[q * 4 + zd, jj] for zd in range(4)]
            even = (jnp.where(low_half, m0, down(m2, 4)), jnp.where(low_half, down(m0, 4), m2))
            odd = (jnp.where(low_half, m1, down(m3, 4)), jnp.where(low_half, down(m1, 4), m3))
            for n in range(2):
                own_ref[q, jj + 3 * n] = jnp.where(s < 7, up(even[n], 1), 0.0) + jnp.where(
                    s > 0, down(odd[n], 1), 0.0
                )
    for e in range(3):
        for j in range(HALF):
            far_ref[e * 6 + j] = own_ref[right + e, j]
    for j in range(HALF):
        near_ref[j] = own_ref[3 * right, j]
    if with_blocks:
        for n in range(BRICK_TILES):
            for e in range(3):
                far_ref[18 + e * BRICK_TILES + n] = brick_tile(recv_ref, right + e, n)
            near_ref[6 + n] = brick_tile(recv_ref, 3 * right, n)


def brick_tile(recv_ref, q, n):
    s = rows()
    out = None
    for at in range(8):
        r = 2 * n + at // 4
        row = recv_ref[q * 4 + at % 4, 3 + r // 8, pl.ds(r % 8, 1), :]
        row = jnp.broadcast_to(row, TILE)
        out = row if out is None else jnp.where(s == at, row, out)
    return out


def fill_own(recv_ref, win_ref):
    for r in range(CHANNELS):
        at, tile = pl.ds(r % 8, 1), r // 8
        for q in range(4):
            win_ref[q, r] = expand_channel(lambda zd: recv_ref[q * 4 + zd, 3 + tile, at, :])


def fill_others(far_ref, near_ref, win_ref):
    for r in range(CHANNELS):
        tile, base = r // 2, 4 * (r % 2)
        for e in range(3):
            win_ref[4 + e, r] = expand_channel(
                lambda zd: far_ref[18 + e * BRICK_TILES + tile, pl.ds(base + zd, 1), :]
            )
        win_ref[7, r] = expand_channel(lambda zd: near_ref[6 + tile, pl.ds(base + zd, 1), :])


def correct_kernel(
    again,
    here,
    diff_ref,
    reaction_ref,
    smoother_ref,
    u_ref,
    r_ref,
    recv_ref,
    own_ref,
    far_ref,
    near_ref,
    *rest,
):
    zd, p, brick, bricks = here[1], here[2], here[3], here[4]
    if again:
        win_ref, new_ref, face_ref, swap_ref, rhs_ref, bx_ref = rest
    else:
        new_ref, face_ref, swap_ref, win_ref, around_ref, rhs_ref, bx_ref = rest
        fill_own(recv_ref, win_ref)
        fill_others(far_ref, near_ref, win_ref)
    expand_blocks(win_ref, bx_ref, range(8))
    slots = slots_of(p)
    for j in range(HALF):
        for q in range(4):
            rhs_ref[q, j] = own_ref[q, j]
        for e in range(3):
            rhs_ref[4 + e, j] = far_ref[e * 6 + j]
        rhs_ref[7, j] = near_ref[j]

    def rhs(w):
        place = brick + (w - CENTRE)
        inside = jnp.logical_and(place >= 0, place < bricks)
        return [pick(inside, rhs_ref[slots[w], j], 0.0) for j in range(HALF)]

    q = solve_coarse(diff_ref, rhs, slots, win_ref, bx_ref)
    inside, hx, hz = prolong(here, q)
    fine_masks = [win_ref[slots[CENTRE + n], 10] for n in (-1, 0, 1)]
    if not again:
        for n in range(3):
            around_ref[n] = fine_masks[n]
    mask_x, mask_z = outside_masks(zd, fine_masks)
    hx = [mask_x * t for t in hx]
    hz = [mask_z * t for t in hz]
    mask = fine_mask_of(here)
    change = operator(reaction_ref, diff_ref, mask, inside, hx, hz)
    resid = [r_ref[c] - change[c] for c in range(COMP)]
    if again:
        below = p * 4 + jnp.maximum(zd - 1, 0)
        above = p * 4 + jnp.minimum(zd + 1, 3)
        halo = z_halo(
            zd, [recv_ref[below, 3 + n] for n in range(3)], [recv_ref[above, 3 + n] for n in range(3)]
        )
        resid = [r + mask * (diff_ref[c] * h) for c, (r, h) in enumerate(zip(resid, halo))]
    step = smooth(smoother_ref, mask, resid)
    new = [u_ref[c] + inside[c] + step[c] for c in range(COMP)]
    for c in range(COMP):
        new_ref[c] = new[c]
    write_faces(here, mask, new, face_ref, swap_ref)


def residual(here, diff_ref, src_ref, reaction_ref, u_ref, face_ref, swap_ref):
    mask = fine_mask_of(here)
    u = load(u_ref)
    hx, hz = read_faces(here, face_ref, swap_ref)
    au = operator(reaction_ref, diff_ref, mask, u, hx, hz)
    return mask, u, [src_ref[c] - au[c] for c in range(COMP)]


def sweep_kernel(
    here, diff_ref, src_ref, reaction_ref, u_ref, face_ref, swap_ref, smoother_ref,
    new_ref, part_ref, chip_ref, cross_ref,
):
    mask, u, resid = residual(
        here, diff_ref, src_ref, reaction_ref, u_ref, face_ref, swap_ref
    )
    step = smooth(smoother_ref, mask, resid)
    new = [a + b for a, b in zip(u, step)]
    au = operator(reaction_ref, diff_ref, mask, new, ZEROS, ZEROS)
    part = [src_ref[c] - au[c] for c in range(COMP)]
    for c in range(COMP):
        new_ref[c] = new[c]
        part_ref[c] = part[c]
    write_layers(here, mask, new, part, chip_ref, cross_ref)


def last_kernel(
    here, diff_ref, src_ref, reaction_ref, u_ref, face_ref, swap_ref, r_ref
):
    _, _, resid = residual(
        here, diff_ref, src_ref, reaction_ref, u_ref, face_ref, swap_ref
    )
    for c in range(COMP):
        r_ref[c] = resid[c]


VMEM_SPEC = pl.BlockSpec(memory_space=pltpu.VMEM)


def place():
    core = lax.axis_index("core")
    p = lax.axis_index("xc") * 2 + core
    brick = lax.axis_index("xg") * 4 + p
    return [core, lax.axis_index("gz"), p, brick, lax.axis_size("xg") * 4]


def spread(row_ref):
    return [
        jnp.broadcast_to(row_ref[:, n : n + 1], TILE).astype(F32) for n in range(row_ref.shape[1])
    ]


def call(kernel, name, small, arrays, outs, scratch=()):
    def body(*refs):
        tiles = [spread(ref) for ref in refs[: len(small)]]
        position = place() + (tiles[0] if tiles else [])
        kernel(position, *tiles[1:], *refs[len(small) :])

    return pl.pallas_call(
        body,
        name=name,
        in_specs=[VMEM_SPEC] * (len(small) + len(arrays)),
        out_specs=[VMEM_SPEC] * len(outs),
        out_shape=[jax.ShapeDtypeStruct(shape, F32) for shape in outs],
        scratch_shapes=[pltpu.VMEM(shape, F32) for shape in scratch],
        compiler_params=pltpu.CompilerParams(vmem_limit_bytes=VMEM_LIMIT),
    )(*small, *arrays)


VEC = (COMP, 8, 128)
FACE = (8, HALF, 8, 128)
SWAP = (HALF, 8, 128)
LAYER = (13, 8, 128)


def local(bricks, source, reaction, smoother, diffusion, active):
    act = active.reshape(1, 4)
    small = [act, diffusion.reshape(1, COMP)]
    src = source.reshape(VEC)
    react = reaction.reshape(COMP * COMP * 8, 128)
    smoo = smoother.reshape(COMP * COMP * 8, 128)
    groups = bricks // 4

    chip_pairs = [(i, i ^ 1) for i in range(bricks)]
    pairs = [(i, i + 1) for i in range(1, bricks - 1, 2)]
    swap_pairs = pairs + [(b, a) for a, b in pairs]
    far_pairs, near_pairs = [], []
    for i in range(bricks):
        g, p = divmod(i, 4)
        step = 1 if p >= 2 else -1
        if 0 <= g + step < groups:
            far_pairs.append((i, 4 * (g + step) + 3 - p))
            if p in (1, 2):
                near_pairs.append((i, i + 4 * step))

    def faces(face, swap):
        swap = lax.ppermute(swap, X_AXES, swap_pairs)
        face = lax.all_to_all(face, ("core", "gz"), 0, 0)
        return face, swap

    def layers(chip, cross):
        return lax.ppermute(chip, X_AXES, chip_pairs), lax.ppermute(cross, X_AXES, swap_pairs)

    def to_coarse(message, with_blocks):
        recv = lax.all_to_all(message, ("xc", "core", "gz"), 0, 0)
        far_rows, near_rows = (18 + 3 * BRICK_TILES, 6 + BRICK_TILES) if with_blocks else (18, 6)
        own, far, near = call(
            functools.partial(gather_kernel, with_blocks),
            "gather",
            [],
            [recv],
            [(4, HALF, 8, 128), (far_rows, 8, 128), (near_rows, 8, 128)],
        )
        far = lax.ppermute(far, X_AXES, far_pairs)
        near = lax.ppermute(near, X_AXES, near_pairs)
        return recv, own, far, near

    u, edges = call(first_kernel, "first", [act], [src, smoo], [VEC, (4, 3, 8, 128)])
    (packed,) = call(blocks_kernel, "blocks", [act], [smoo, react], [(2, 8, 128)], [(2, 160, 128)])
    edges = lax.all_to_all(edges, "gz", 0, 0)
    part, chip, cross = call(
        part_kernel, "part", small, [src, react, u, edges], [VEC, LAYER, LAYER]
    )
    chip, cross = layers(chip, cross)
    resid, message = call(
        functools.partial(send_kernel, False),
        "send",
        small,
        [u, part, chip, cross, packed],
        [VEC, (16, 5, 8, 128)],
    )
    recv, own, far, near = to_coarse(message, True)
    rhs_shape, bx_shape, win_shape = (8, HALF, 8, 128), (8, 72, 2, 8, 128), (8, CHANNELS, 8, 128)
    u, face, swap, window, around = call(
        functools.partial(correct_kernel, False),
        "correct",
        small,
        [react, smoo, u, resid, recv, own, far, near],
        [VEC, FACE, SWAP, win_shape, (3, 8, 128)],
        [rhs_shape, bx_shape],
    )
    face, swap = faces(face, swap)
    u, part, chip, cross = call(
        sweep_kernel, "sweep", small, [src, react, u, face, swap, smoo], [VEC, VEC, LAYER, LAYER]
    )
    chip, cross = layers(chip, cross)
    resid, message = call(
        functools.partial(send_kernel, True),
        "send",
        small,
        [u, part, chip, cross, around],
        [VEC, (16, 6, 8, 128)],
    )
    recv, own, far, near = to_coarse(message, False)
    u, face, swap = call(
        functools.partial(correct_kernel, True),
        "correct",
        small,
        [react, smoo, u, resid, recv, own, far, near, window],
        [VEC, FACE, SWAP],
        [rhs_shape, bx_shape],
    )
    face, swap = faces(face, swap)
    (resid,) = call(last_kernel, "last", small, [src, react, u, face, swap], [VEC])
    return u.reshape(source.shape), resid.reshape(source.shape)


def solution(mesh):
    bricks = mesh.shape["bricks"]
    gz = mesh.shape["gz"]
    inner = Mesh(mesh.devices.reshape(bricks // 4, 2, 2, gz), X_AXES + ("gz",))
    in_specs = (
        P(None, X_AXES, "gz", None),
        P(None, None, X_AXES, "gz", None),
        P(None, None, X_AXES, "gz", None),
        P(),
        P(X_AXES, "gz", None),
    )
    out_specs = (P(None, X_AXES, "gz", None), P(None, X_AXES, "gz", None))
    return jax.shard_map(
        functools.partial(local, bricks),
        mesh=inner,
        in_specs=in_specs,
        out_specs=out_specs,
        check_vma=False,
    )
```

```python
import functools

import jax
import jax.numpy as jnp
from jax import lax
from jax.experimental import pallas as pl
from jax.experimental.pallas import tpu as pltpu
from jax.sharding import Mesh
from jax.sharding import PartitionSpec as P

COMP = 12
HALF = 6
F32 = jnp.float32
BF16 = jnp.bfloat16
X_AXES = ("xg", "xc", "core")
TILE = (8, 128)
CHANNELS = 11
BRICK_TILES = 6
CENTRE = 3
VMEM_LIMIT = 16 * 1024 * 1024


def rows(shape=TILE):
    return lax.broadcasted_iota(jnp.int32, shape, 0)


def lanes(shape=TILE):
    return lax.broadcasted_iota(jnp.int32, shape, 1)


def up(x, by):
    return pltpu.roll(x, 8 - by, 0)


def down(x, by):
    return pltpu.roll(x, by, 0)


def pick(cond, a, b):
    return jnp.where(cond, a, b)


def hat(diff):
    inner = jnp.logical_or(diff == 0, diff == 1)
    outer = jnp.logical_or(diff == -1, diff == 2)
    return jnp.where(inner, 3.0, jnp.where(outer, 1.0, 0.0)).astype(F32)


def split(x, parts):
    pieces = []
    for _ in range(parts):
        piece = x.astype(BF16)
        pieces.append(piece)
        x = x - piece.astype(F32)
    return pieces


def dot(a, b):
    return jnp.dot(a, b, preferred_element_type=F32)


def dot_right(x, weights, parts=3):
    return dot(jnp.concatenate(split(x, parts), axis=1), jnp.concatenate([weights] * parts, axis=0))


def dot_left(weights, x, parts=3):
    return dot(jnp.concatenate([weights] * parts, axis=1), jnp.concatenate(split(x, parts), axis=0))


def fine_mask_of(here):
    brick = lanes() // 32
    out = jnp.zeros(TILE, F32)
    for b in range(4):
        out = jnp.where(brick == b, here[5 + b], out)
    return out


def packed_mask_of(here):
    brick = (lanes() % 64) // 16
    out = jnp.zeros(TILE, F32)
    for b in range(4):
        out = jnp.where(brick == b, here[5 + b], out)
    return out


def load(ref):
    return [ref[c] for c in range(COMP)]


def block_product(blocks_ref, vec):
    out = []
    for c in range(COMP):
        acc = None
        for d in range(0, COMP, 2):
            pair = blocks_ref[pl.ds((c * COMP + d) * 8, 16), :].astype(F32)
            term = pair[:8] * vec[d] + pair[8:] * vec[d + 1]
            acc = term if acc is None else acc + term
        out.append(acc)
    return out


def smooth(smoother_ref, mask, resid):
    prod = block_product(smoother_ref, resid)
    return [mask * a + (1.0 - mask) * r for a, r in zip(prod, resid)]


def neighbours(mv, hx, hz):
    z = rows() % 4
    lane = lanes()
    total = down(mv, 4) + hx + hz
    total = total + jnp.where(z > 0, down(mv, 1), 0.0) + jnp.where(z < 3, up(mv, 1), 0.0)
    total = total + jnp.where(lane > 0, pltpu.roll(mv, 1, 1), 0.0)
    return total + jnp.where(lane < 127, pltpu.roll(mv, 127, 1), 0.0)


def operator(reaction_ref, diff_ref, mask, vec, hx, hz):
    prod = block_product(reaction_ref, vec)
    out = []
    for c in range(COMP):
        v = vec[c]
        inner = prod[c] + diff_ref[c] * (6.0 * v - neighbours(mask * v, hx[c], hz[c]))
        out.append(mask * inner + (1.0 - mask) * v)
    return out


def x_messages(vec):
    low_half = rows() < 4
    to_high, to_low = [], []
    for j in range(HALF):
        a, b = vec[j], vec[j + HALF]
        to_high.append(jnp.where(low_half, down(a, 4), b))
        to_low.append(jnp.where(low_half, a, down(b, 4)))
    return to_high, to_low


def x_halo(low, high):
    low_half = rows() < 4
    first = [jnp.where(low_half, a, down(b, 4)) for a, b in zip(low, high)]
    second = [jnp.where(low_half, down(a, 4), b) for a, b in zip(low, high)]
    return first + second


def z_messages(vec):
    z = rows() % 4
    to_high, to_low = [], []
    for c in range(3):
        up_tile, down_tile = up(vec[c], 3), vec[c]
        for k in range(1, 4):
            t = vec[c + 3 * k]
            up_tile = jnp.where(z == k, up(t, 3 - k) if k < 3 else t, up_tile)
            down_tile = jnp.where(z == k, down(t, k), down_tile)
        to_high.append(up_tile)
        to_low.append(down_tile)
    return to_high, to_low


def z_halo(zd, low, high):
    z = rows() % 4
    has_low = jnp.logical_and(z == 0, zd > 0)
    has_high = jnp.logical_and(z == 3, zd < 3)
    out = []
    for c in range(COMP):
        k, at = c // 3, c % 3
        a = up(low[at], k) if k else low[at]
        b = down(high[at], 3 - k) if k < 3 else high[at]
        out.append(jnp.where(has_low, a, jnp.where(has_high, b, 0.0)))
    return out


def write_faces(here, mask, vec, face_ref, swap_ref):
    core, zd = here[0], here[1]
    first = core == 0
    mv = [mask * v for v in vec]
    x_high, x_low = x_messages(mv)
    z_high, z_low = z_messages(mv)
    for j in range(HALF):
        in_chip = pick(first, x_high[j], x_low[j])
        swap_ref[j] = pick(first, x_low[j], x_high[j])
        for other in range(4):
            along = pick(other > zd, z_high[j % 3], z_low[j % 3])
            face_ref[other, j] = pick(first, along, in_chip)
            face_ref[4 + other, j] = pick(first, in_chip, along)


def read_faces(here, face_ref, swap_ref):
    core, zd = here[0], here[1]
    first = core == 0
    chip_at = (1 - core) * 4 + zd
    low_at = core * 4 + jnp.maximum(zd - 1, 0)
    high_at = core * 4 + jnp.minimum(zd + 1, 3)
    low, high = [], []
    for j in range(HALF):
        chip, cross = face_ref[chip_at, j], swap_ref[j]
        low.append(pick(first, cross, chip))
        high.append(pick(first, chip, cross))
    hz = z_halo(zd, [face_ref[low_at, c] for c in range(3)], [face_ref[high_at, c] for c in range(3)])
    return x_halo(low, high), hz


def write_layers(here, mask, vec, resid, chip_ref, cross_ref):
    first = here[0] == 0
    r_high, r_low = x_messages(resid)
    v_high, v_low = x_messages([mask * v for v in vec])
    for n, (high, low) in enumerate(zip(r_high + v_high + [mask], r_low + v_low + [mask])):
        chip_ref[n] = pick(first, high, low)
        cross_ref[n] = pick(first, low, high)


def restrict(own, beside, above):
    kinds = [own, beside] + ([above] if above is not None else [])
    depth = 8 * len(kinds)
    l, o = rows((128, 128)), lanes((128, 128))
    low = jnp.where(o < 64, hat(l - 2 * o), 0.0).astype(BF16)
    high = jnp.where(o >= 64, hat(l - 2 * (o - 64)), 0.0).astype(BF16)
    a = jnp.concatenate([kind[j] for j in range(HALF) for kind in kinds], axis=0)
    b = jnp.concatenate([kind[j + HALF] for j in range(HALF) for kind in kinds], axis=0)
    along_y = (dot_right(a, low) + dot_right(b, high)) * 0.125
    blocks = [along_y[depth * j : depth * j + depth] for j in range(HALF)]
    stacked = jnp.concatenate(
        [jnp.concatenate(blocks[:3], axis=1), jnp.concatenate(blocks[3:], axis=1)], axis=0
    )
    o, k = rows((8, 2 * depth)), lanes((8, 2 * depth))
    kind, s = (k % depth) // 8, k % 8
    z = s % 4
    outer_x = jnp.where(s < 4, -1, 2)
    in_own = jnp.logical_or(z == 0, z == 3)
    x = jnp.where(kind == 0, s // 4, jnp.where(kind == 1, outer_x, jnp.where(in_own, s // 4, outer_x)))
    fine_z = jnp.where(kind == 2, jnp.where(z < 2, -1, 4), z)
    weights = hat(x) * hat(fine_z - 2 * (o % 4 - 1))
    weights = jnp.where(o // 4 == k // depth, weights, 0.0).astype(BF16)
    result = dot_left(weights, stacked) * (1.0 / 64.0)
    return [result[:, 128 * jj : 128 * jj + 128] for jj in range(3)]


def packed_blocks(smoother_ref, reaction_ref, here, sums_ref):
    l, o = rows((128, 128)), lanes((128, 128))
    weights = jnp.where(l // 32 == o % 4, 1.0 / 256.0, 0.0).astype(BF16)
    zero = jnp.zeros((16, 128), F32)
    for a, ref in enumerate((smoother_ref, reaction_ref)):
        for n in range(0, COMP * COMP, 2):
            pair = ref[pl.ds(n * 8, 16), :].astype(F32)
            sums_ref[a, pl.ds(n, 1), :] = jnp.sum(pair[:8], axis=0, keepdims=True)
            sums_ref[a, pl.ds(n + 1, 1), :] = jnp.sum(pair[8:], axis=0, keepdims=True)
        sums_ref[a, pl.ds(144, 16), :] = zero
        sums_ref[a] = dot_right(sums_ref[a], weights)
    s, lane = rows((16, 128)), lanes((16, 128))
    out = zero
    for k in range(8):
        for a in range(2):
            for half in range(2):
                part = sums_ref[a, pl.ds(72 * half + 9 * k, 16), :]
                out = jnp.where(lane // 4 == 4 * k + 2 * a + half, part, out)
    coarse = jnp.broadcast_to(packed_mask_of(here)[:1], (16, 128))
    fine = jnp.broadcast_to(fine_mask_of(here)[:1], (16, 128))
    return jnp.where(s < 9, out, jnp.where(s == 9, coarse, jnp.where(s == 10, fine, 0.0)))


def expand_channel(get_row):
    owner = rows() // 2
    out = jnp.broadcast_to(get_row(0), TILE)
    for zd in range(1, 4):
        out = jnp.where(owner == zd, jnp.broadcast_to(get_row(zd), TILE), out)
    return out


def slots_of(p):
    right = p // 2
    out = []
    for w in range(7):
        x = p - CENTRE + w
        before = jnp.where(right == 0, x + 7, 7)
        after = jnp.where(right == 1, x, 7)
        out.append(jnp.where(x < 0, before, jnp.where(x > 3, after, x)))
    return out


def coarse_product(bx_ref, which, slot, vec):
    left = lanes() < 64
    both = [None] * COMP
    for j in range(HALF):
        turned = pltpu.roll(vec[j], 64, 1)
        both[j] = jnp.where(left, vec[j], turned)
        both[j + HALF] = jnp.where(left, turned, vec[j])
    out = []
    for j in range(HALF):
        acc = None
        for d in range(COMP):
            term = bx_ref[slot, j * COMP + d, which] * both[d]
            acc = term if acc is None else acc + term
        out.append(acc)
    return out


def coarse_smooth(bx_ref, mask, slot, resid):
    prod = coarse_product(bx_ref, 0, slot, resid)
    return [mask * a + (1.0 - mask) * r for a, r in zip(prod, resid)]


def expand_blocks(win_ref, bx_ref, slots):
    flat = jnp.concatenate([win_ref[n, r] for n in slots for r in range(9)], axis=0)
    pieces = jnp.concatenate(split(flat, 2), axis=1)
    l, o = rows((256, 256)) % 128, lanes((256, 256))
    target = (o // 128) * 8 + ((o % 128) // 64) * 4 + (o % 64) // 16
    for k in range(8):
        weights = jnp.where(l == 16 * k + target, 1.0, 0.0).astype(BF16)
        out = dot(pieces, weights)
        for i, n in enumerate(slots):
            for r in range(9):
                tile = out[(i * 9 + r) * 8 : (i * 9 + r) * 8 + 8]
                bx_ref[n, 9 * k + r, 0] = tile[:, :128]
                bx_ref[n, 9 * k + r, 1] = tile[:, 128:]


def solve_coarse(diff_ref, rhs, slots, win_ref, bx_ref):
    s, lane = rows(), lanes()
    left = lane < 64
    inner_lane = lane % 64
    coeffs = [
        0.25 * jnp.where(left, diff_ref[j], diff_ref[j + HALF])
        for j in range(HALF)
    ]
    masks = [win_ref[slots[w], 9] for w in range(7)]
    b = [rhs(w) for w in range(7)]
    v = [coarse_smooth(bx_ref, masks[w], slots[w], b[w]) for w in range(7)]
    for edge in (1, 2):
        mv = [[masks[w] * t for t in v[w]] if v[w] is not None else None for w in range(7)]
        new = [None] * 7
        for w in range(edge, 7 - edge):
            prod = coarse_product(bx_ref, 1, slots[w], v[w])
            resid = []
            for j in range(HALF):
                t = mv[w][j]
                total = mv[w - 1][j] + mv[w + 1][j]
                total = total + jnp.where(s > 0, down(t, 1), 0.0) + jnp.where(s < 7, up(t, 1), 0.0)
                total = total + jnp.where(inner_lane > 0, pltpu.roll(t, 1, 1), 0.0)
                total = total + jnp.where(inner_lane < 63, pltpu.roll(t, 127, 1), 0.0)
                inner = prod[j] + coeffs[j] * (6.0 * v[w][j] - total)
                resid.append(b[w][j] - (masks[w] * inner + (1.0 - masks[w]) * v[w][j]))
            step = coarse_smooth(bx_ref, masks[w], slots[w], resid)
            new[w] = [x + y for x, y in zip(v[w], step)]
        v = new
    return v[2:5]


def prolong(here, q):
    zd = here[1]
    o, k = rows((24, 24)), lanes((24, 24))
    group, s = o // 8, o % 8
    z = s % 4
    fx = jnp.where(group == 1, jnp.where(s < 4, -1, 2), s // 4)
    fz = jnp.where(group == 2, jnp.where(z == 0, -1, 4), z) + 4 * zd
    weights = hat(fx - 2 * (k // 8 - 1)) * hat(fz - 2 * (k % 8))
    unused = jnp.logical_and(group == 2, jnp.logical_or(z == 1, z == 2))
    weights = jnp.where(unused, 0.0, weights * 0.0625).astype(BF16)
    stacked = jnp.concatenate([jnp.concatenate(row, axis=1) for row in q], axis=0)
    xz = dot_left(weights, stacked)
    tall = jnp.concatenate([xz[:, 128 * j : 128 * j + 128] for j in range(HALF)], axis=0)
    a, f = rows((128, 256)), lanes((128, 256))
    along = hat(f % 128 - 2 * (a % 64)) * 0.25
    along = jnp.where(a // 64 == f // 128, along, 0.0).astype(BF16)
    fine = dot_right(tall, along)
    groups = []
    for g in range(3):
        tiles = [fine[24 * j + 8 * g : 24 * j + 8 * g + 8] for j in range(HALF)]
        groups.append([t[:, :128] for t in tiles] + [t[:, 128:] for t in tiles])
    return groups


def masks_around(zd, tile):
    own = pltpu.roll(tile, lax.rem(8 - 2 * zd, 8), 0)
    return own[7:8], own[:1], own[2:3]


def outside_masks(zd, tiles):
    s = rows()
    z = s % 4
    _, low_x, _ = masks_around(zd, tiles[0])
    low_z, _, high_z = masks_around(zd, tiles[1])
    _, high_x, _ = masks_around(zd, tiles[2])
    mask_x = jnp.where(s < 4, jnp.broadcast_to(low_x, TILE), jnp.broadcast_to(high_x, TILE))
    mask_z = jnp.where(
        jnp.logical_and(z == 0, zd > 0),
        jnp.broadcast_to(low_z, TILE),
        jnp.where(jnp.logical_and(z == 3, zd < 3), jnp.broadcast_to(high_z, TILE), 0.0),
    )
    return mask_x, mask_z


def layer_masks(zd, tiles):
    s = rows()
    z = s % 4
    around = [masks_around(zd, tile) for tile in tiles]
    below = [jnp.broadcast_to(a[0], TILE) for a in around]
    above = [jnp.broadcast_to(a[2], TILE) for a in around]
    low = jnp.where(z == 0, below[1], jnp.where(s < 4, below[0], below[2]))
    high = jnp.where(z == 3, above[1], jnp.where(s < 4, above[0], above[2]))
    low = jnp.where(zd > 0, low, 0.0)
    high = jnp.where(zd < 3, high, 0.0)
    return jnp.where(z < 2, low, high)


ZEROS = [0.0] * COMP


def first_kernel(here, src_ref, smoother_ref, u_ref, z_ref):
    mask = fine_mask_of(here)
    zd = here[1]
    u = smooth(smoother_ref, mask, load(src_ref))
    for c in range(COMP):
        u_ref[c] = u[c]
    high, low = z_messages([mask * v for v in u])
    for other in range(4):
        for n in range(3):
            z_ref[other, n] = pick(other > zd, high[n], low[n])


def blocks_kernel(here, smoother_ref, reaction_ref, out_ref, sums_ref):
    packed = packed_blocks(smoother_ref, reaction_ref, here, sums_ref)
    out_ref[0] = packed[:8]
    out_ref[1] = packed[8:]


def part_kernel(
    here, diff_ref, src_ref, reaction_ref, u_ref, z_ref, r_ref, chip_ref, cross_ref
):
    mask = fine_mask_of(here)
    zd = here[1]
    u = load(u_ref)
    below, above = jnp.maximum(zd - 1, 0), jnp.minimum(zd + 1, 3)
    hz = z_halo(zd, [z_ref[below, n] for n in range(3)], [z_ref[above, n] for n in range(3)])
    au = operator(reaction_ref, diff_ref, mask, u, ZEROS, hz)
    resid = [src_ref[c] - au[c] for c in range(COMP)]
    for c in range(COMP):
        r_ref[c] = resid[c]
    write_layers(here, mask, u, resid, chip_ref, cross_ref)


def send_kernel(
    again, here, diff_ref, u_ref, part_ref, chip_ref, cross_ref, extra_ref, r_ref, out_ref
):
    mask = fine_mask_of(here)
    zd = here[1]
    first = here[0] == 0
    low = [pick(first, cross_ref[n], chip_ref[n]) for n in range(13)]
    high = [pick(first, chip_ref[n], cross_ref[n]) for n in range(13)]
    hr = x_halo(low[:6], high[:6])
    hv = x_halo(low[6:12], high[6:12])
    mask_x = jnp.where(rows() < 4, low[12], high[12])
    mv = [mask * u_ref[c] for c in range(COMP)]
    own = [part_ref[c] + mask * (diff_ref[c] * hv[c]) for c in range(COMP)]
    beside = [hr[c] + mask_x * (diff_ref[c] * mv[c]) for c in range(COMP)]
    for c in range(COMP):
        r_ref[c] = own[c]
    above = None
    if again:
        z = rows() % 4
        inner = jnp.logical_or(z == 0, z == 3)
        edge = layer_masks(zd, [extra_ref[n] for n in range(3)])
        above = []
        for c in range(COMP):
            outer = jnp.where(z == 1, down(hv[c], 1), up(hv[c], 1))
            above.append(edge * (diff_ref[c] * jnp.where(inner, mv[c], outer)))
    tiles = restrict(own, beside, above)
    if not again:
        tiles = tiles + [extra_ref[0], extra_ref[1]]
    for n, tile in enumerate(tiles):
        for target in range(16):
            out_ref[target, n] = tile
    if again:
        z_high, z_low = z_messages(mv)
        for n in range(3):
            for other in range(4):
                tile = pick(other > zd, z_high[n], z_low[n])
                for q in range(4):
                    out_ref[q * 4 + other, 3 + n] = tile


def gather_kernel(with_blocks, here, recv_ref, own_ref, far_ref, near_ref):
    right = here[2] // 2
    s = rows()
    low_half = s < 4
    for q in range(4):
        for jj in range(3):
            m0, m1, m2, m3 = [recv_ref[q * 4 + zd, jj] for zd in range(4)]
            even = (jnp.where(low_half, m0, down(m2, 4)), jnp.where(low_half, down(m0, 4), m2))
            odd = (jnp.where(low_half, m1, down(m3, 4)), jnp.where(low_half, down(m1, 4), m3))
            for n in range(2):
                own_ref[q, jj + 3 * n] = jnp.where(s < 7, up(even[n], 1), 0.0) + jnp.where(
                    s > 0, down(odd[n], 1), 0.0
                )
    for e in range(3):
        for j in range(HALF):
            far_ref[e * 6 + j] = own_ref[right + e, j]
    for j in range(HALF):
        near_ref[j] = own_ref[3 * right, j]
    if with_blocks:
        for n in range(BRICK_TILES):
            for e in range(3):
                far_ref[18 + e * BRICK_TILES + n] = brick_tile(recv_ref, right + e, n)
            near_ref[6 + n] = brick_tile(recv_ref, 3 * right, n)


def brick_tile(recv_ref, q, n):
    s = rows()
    out = None
    for at in range(8):
        r = 2 * n + at // 4
        row = recv_ref[q * 4 + at % 4, 3 + r // 8, pl.ds(r % 8, 1), :]
        row = jnp.broadcast_to(row, TILE)
        out = row if out is None else jnp.where(s == at, row, out)
    return out


def fill_own(recv_ref, win_ref):
    for r in range(CHANNELS):
        at, tile = pl.ds(r % 8, 1), r // 8
        for q in range(4):
            win_ref[q, r] = expand_channel(lambda zd: recv_ref[q * 4 + zd, 3 + tile, at, :])


def fill_others(far_ref, near_ref, win_ref):
    for r in range(CHANNELS):
        tile, base = r // 2, 4 * (r % 2)
        for e in range(3):
            win_ref[4 + e, r] = expand_channel(
                lambda zd: far_ref[18 + e * BRICK_TILES + tile, pl.ds(base + zd, 1), :]
            )
        win_ref[7, r] = expand_channel(lambda zd: near_ref[6 + tile, pl.ds(base + zd, 1), :])


def correct_kernel(
    again,
    here,
    diff_ref,
    reaction_ref,
    smoother_ref,
    u_ref,
    r_ref,
    recv_ref,
    own_ref,
    far_ref,
    near_ref,
    *rest,
):
    zd, p, brick, bricks = here[1], here[2], here[3], here[4]
    if again:
        win_ref, new_ref, face_ref, swap_ref, rhs_ref, bx_ref = rest
    else:
        new_ref, face_ref, swap_ref, win_ref, around_ref, rhs_ref, bx_ref = rest
        fill_own(recv_ref, win_ref)
        fill_others(far_ref, near_ref, win_ref)
    expand_blocks(win_ref, bx_ref, range(8))
    slots = slots_of(p)
    for j in range(HALF):
        for q in range(4):
            rhs_ref[q, j] = own_ref[q, j]
        for e in range(3):
            rhs_ref[4 + e, j] = far_ref[e * 6 + j]
        rhs_ref[7, j] = near_ref[j]

    def rhs(w):
        place = brick + (w - CENTRE)
        inside = jnp.logical_and(place >= 0, place < bricks)
        return [pick(inside, rhs_ref[slots[w], j], 0.0) for j in range(HALF)]

    q = solve_coarse(diff_ref, rhs, slots, win_ref, bx_ref)
    inside, hx, hz = prolong(here, q)
    fine_masks = [win_ref[slots[CENTRE + n], 10] for n in (-1, 0, 1)]
    if not again:
        for n in range(3):
            around_ref[n] = fine_masks[n]
    mask_x, mask_z = outside_masks(zd, fine_masks)
    hx = [mask_x * t for t in hx]
    hz = [mask_z * t for t in hz]
    mask = fine_mask_of(here)
    change = operator(reaction_ref, diff_ref, mask, inside, hx, hz)
    resid = [r_ref[c] - change[c] for c in range(COMP)]
    if again:
        below = p * 4 + jnp.maximum(zd - 1, 0)
        above = p * 4 + jnp.minimum(zd + 1, 3)
        halo = z_halo(
            zd, [recv_ref[below, 3 + n] for n in range(3)], [recv_ref[above, 3 + n] for n in range(3)]
        )
        resid = [r + mask * (diff_ref[c] * h) for c, (r, h) in enumerate(zip(resid, halo))]
    step = smooth(smoother_ref, mask, resid)
    new = [u_ref[c] + inside[c] + step[c] for c in range(COMP)]
    for c in range(COMP):
        new_ref[c] = new[c]
    write_faces(here, mask, new, face_ref, swap_ref)


def residual(here, diff_ref, src_ref, reaction_ref, u_ref, face_ref, swap_ref):
    mask = fine_mask_of(here)
    u = load(u_ref)
    hx, hz = read_faces(here, face_ref, swap_ref)
    au = operator(reaction_ref, diff_ref, mask, u, hx, hz)
    return mask, u, [src_ref[c] - au[c] for c in range(COMP)]


def sweep_kernel(
    here, diff_ref, src_ref, reaction_ref, u_ref, face_ref, swap_ref, smoother_ref,
    new_ref, part_ref, chip_ref, cross_ref,
):
    mask, u, resid = residual(
        here, diff_ref, src_ref, reaction_ref, u_ref, face_ref, swap_ref
    )
    step = smooth(smoother_ref, mask, resid)
    new = [a + b for a, b in zip(u, step)]
    au = operator(reaction_ref, diff_ref, mask, new, ZEROS, ZEROS)
    part = [src_ref[c] - au[c] for c in range(COMP)]
    for c in range(COMP):
        new_ref[c] = new[c]
        part_ref[c] = part[c]
    write_layers(here, mask, new, part, chip_ref, cross_ref)


def last_kernel(
    here, diff_ref, src_ref, reaction_ref, u_ref, face_ref, swap_ref, r_ref
):
    _, _, resid = residual(
        here, diff_ref, src_ref, reaction_ref, u_ref, face_ref, swap_ref
    )
    for c in range(COMP):
        r_ref[c] = resid[c]


VMEM_SPEC = pl.BlockSpec(memory_space=pltpu.VMEM)


def place():
    core = lax.axis_index("core")
    p = lax.axis_index("xc") * 2 + core
    brick = lax.axis_index("xg") * 4 + p
    return [core, lax.axis_index("gz"), p, brick, lax.axis_size("xg") * 4]


def spread(row_ref):
    return [
        jnp.broadcast_to(row_ref[:, n : n + 1], TILE).astype(F32) for n in range(row_ref.shape[1])
    ]


def call(kernel, name, small, arrays, outs, scratch=()):
    def body(*refs):
        tiles = [spread(ref) for ref in refs[: len(small)]]
        position = place() + (tiles[0] if tiles else [])
        kernel(position, *tiles[1:], *refs[len(small) :])

    return pl.pallas_call(
        body,
        name=name,
        in_specs=[VMEM_SPEC] * (len(small) + len(arrays)),
        out_specs=[VMEM_SPEC] * len(outs),
        out_shape=[jax.ShapeDtypeStruct(shape, F32) for shape in outs],
        scratch_shapes=[pltpu.VMEM(shape, F32) for shape in scratch],
        compiler_params=pltpu.CompilerParams(vmem_limit_bytes=VMEM_LIMIT),
    )(*small, *arrays)


VEC = (COMP, 8, 128)
FACE = (8, HALF, 8, 128)
SWAP = (HALF, 8, 128)
LAYER = (13, 8, 128)


def local(bricks, source, reaction, smoother, diffusion, active):
    act = active.reshape(1, 4)
    small = [act, diffusion.reshape(1, COMP)]
    src = source.reshape(VEC)
    react = reaction.reshape(COMP * COMP * 8, 128)
    smoo = smoother.reshape(COMP * COMP * 8, 128)
    groups = bricks // 4

    chip_pairs = [(i, i ^ 1) for i in range(bricks)]
    pairs = [(i, i + 1) for i in range(1, bricks - 1, 2)]
    swap_pairs = pairs + [(b, a) for a, b in pairs]
    far_pairs, near_pairs = [], []
    for i in range(bricks):
        g, p = divmod(i, 4)
        step = 1 if p >= 2 else -1
        if 0 <= g + step < groups:
            far_pairs.append((i, 4 * (g + step) + 3 - p))
            if p in (0, 3):
                near_pairs.append((i, i + 3 * step))

    def faces(face, swap):
        swap = lax.ppermute(swap, X_AXES, swap_pairs)
        face = lax.all_to_all(face, ("core", "gz"), 0, 0)
        return face, swap

    def layers(chip, cross):
        return lax.ppermute(chip, X_AXES, chip_pairs), lax.ppermute(cross, X_AXES, swap_pairs)

    def to_coarse(message, with_blocks):
        recv = lax.all_to_all(message, ("xc", "core", "gz"), 0, 0)
        far_rows, near_rows = (18 + 3 * BRICK_TILES, 6 + BRICK_TILES) if with_blocks else (18, 6)
        own, far, near = call(
            functools.partial(gather_kernel, with_blocks),
            "gather",
            [],
            [recv],
            [(4, HALF, 8, 128), (far_rows, 8, 128), (near_rows, 8, 128)],
        )
        far = lax.ppermute(far, X_AXES, far_pairs)
        near = lax.ppermute(near, X_AXES, near_pairs)
        return recv, own, far, near

    u, edges = call(first_kernel, "first", [act], [src, smoo], [VEC, (4, 3, 8, 128)])
    (packed,) = call(blocks_kernel, "blocks", [act], [smoo, react], [(2, 8, 128)], [(2, 160, 128)])
    edges = lax.all_to_all(edges, "gz", 0, 0)
    part, chip, cross = call(
        part_kernel, "part", small, [src, react, u, edges], [VEC, LAYER, LAYER]
    )
    chip, cross = layers(chip, cross)
    resid, message = call(
        functools.partial(send_kernel, False),
        "send",
        small,
        [u, part, chip, cross, packed],
        [VEC, (16, 5, 8, 128)],
    )
    recv, own, far, near = to_coarse(message, True)
    rhs_shape, bx_shape, win_shape = (8, HALF, 8, 128), (8, 72, 2, 8, 128), (8, CHANNELS, 8, 128)
    u, face, swap, window, around = call(
        functools.partial(correct_kernel, False),
        "correct",
        small,
        [react, smoo, u, resid, recv, own, far, near],
        [VEC, FACE, SWAP, win_shape, (3, 8, 128)],
        [rhs_shape, bx_shape],
    )
    face, swap = faces(face, swap)
    u, part, chip, cross = call(
        sweep_kernel, "sweep", small, [src, react, u, face, swap, smoo], [VEC, VEC, LAYER, LAYER]
    )
    chip, cross = layers(chip, cross)
    resid, message = call(
        functools.partial(send_kernel, True),
        "send",
        small,
        [u, part, chip, cross, around],
        [VEC, (16, 6, 8, 128)],
    )
    recv, own, far, near = to_coarse(message, False)
    u, face, swap = call(
        functools.partial(correct_kernel, True),
        "correct",
        small,
        [react, smoo, u, resid, recv, own, far, near, window],
        [VEC, FACE, SWAP],
        [rhs_shape, bx_shape],
    )
    face, swap = faces(face, swap)
    (resid,) = call(last_kernel, "last", small, [src, react, u, face, swap], [VEC])
    return u.reshape(source.shape), resid.reshape(source.shape)


def solution(mesh):
    bricks = mesh.shape["bricks"]
    gz = mesh.shape["gz"]
    inner = Mesh(mesh.devices.reshape(bricks // 4, 2, 2, gz), X_AXES + ("gz",))
    in_specs = (
        P(None, X_AXES, "gz", None),
        P(None, None, X_AXES, "gz", None),
        P(None, None, X_AXES, "gz", None),
        P(),
        P(X_AXES, "gz", None),
    )
    out_specs = (P(None, X_AXES, "gz", None), P(None, X_AXES, "gz", None))
    return jax.shard_map(
        functools.partial(local, bricks),
        mesh=inner,
        in_specs=in_specs,
        out_specs=out_specs,
        check_vma=False,
    )
```

```python
import functools

import jax
import jax.numpy as jnp
from jax import lax
from jax.experimental import pallas as pl
from jax.experimental.pallas import tpu as pltpu
from jax.sharding import Mesh
from jax.sharding import PartitionSpec as P

COMP = 12
HALF = 6
F32 = jnp.float32
BF16 = jnp.bfloat16
X_AXES = ("xg", "xc", "core")
TILE = (8, 128)
CHANNELS = 11
BRICK_TILES = 6
CENTRE = 3
VMEM_LIMIT = 16 * 1024 * 1024


def rows(shape=TILE):
    return lax.broadcasted_iota(jnp.int32, shape, 0)


def lanes(shape=TILE):
    return lax.broadcasted_iota(jnp.int32, shape, 1)


def up(x, by):
    return pltpu.roll(x, 8 - by, 0)


def down(x, by):
    return pltpu.roll(x, by, 0)


def pick(cond, a, b):
    return jnp.where(cond, a, b)


def hat(diff):
    inner = jnp.logical_or(diff == 0, diff == 1)
    outer = jnp.logical_or(diff == -1, diff == 2)
    return jnp.where(inner, 3.0, jnp.where(outer, 1.0, 0.0)).astype(F32)


def split(x, parts):
    pieces = []
    for _ in range(parts):
        piece = x.astype(BF16)
        pieces.append(piece)
        x = x - piece.astype(F32)
    return pieces


def dot(a, b):
    return jnp.dot(a, b, preferred_element_type=F32)


def dot_right(x, weights, parts=3):
    return dot(jnp.concatenate(split(x, parts), axis=1), jnp.concatenate([weights] * parts, axis=0))


def dot_left(weights, x, parts=3):
    return dot(jnp.concatenate([weights] * parts, axis=1), jnp.concatenate(split(x, parts), axis=0))


def fine_mask_of(here):
    brick = lanes() // 32
    out = jnp.zeros(TILE, F32)
    for b in range(4):
        out = jnp.where(brick == b, here[5 + b], out)
    return out


def packed_mask_of(here):
    brick = (lanes() % 64) // 16
    out = jnp.zeros(TILE, F32)
    for b in range(4):
        out = jnp.where(brick == b, here[5 + b], out)
    return out


def load(ref):
    return [ref[c] for c in range(COMP)]


def block_product(blocks_ref, vec):
    out = []
    for c in range(COMP):
        acc = None
        for d in range(0, COMP, 2):
            pair = blocks_ref[pl.ds((c * COMP + d) * 8, 16), :].astype(F32)
            term = pair[:8] * vec[d] + pair[8:] * vec[d + 1]
            acc = term if acc is None else acc + term
        out.append(acc)
    return out


def smooth(smoother_ref, mask, resid):
    prod = block_product(smoother_ref, resid)
    return [mask * a + (1.0 - mask) * r for a, r in zip(prod, resid)]


def neighbours(mv, hx, hz):
    z = rows() % 4
    lane = lanes()
    total = down(mv, 4) + hx + hz
    total = total + jnp.where(z > 0, down(mv, 1), 0.0) + jnp.where(z < 3, up(mv, 1), 0.0)
    total = total + jnp.where(lane > 0, pltpu.roll(mv, 1, 1), 0.0)
    return total + jnp.where(lane < 127, pltpu.roll(mv, 127, 1), 0.0)


def operator(reaction_ref, diff_ref, mask, vec, hx, hz):
    prod = block_product(reaction_ref, vec)
    out = []
    for c in range(COMP):
        v = vec[c]
        inner = prod[c] + diff_ref[c] * (6.0 * v - neighbours(mask * v, hx[c], hz[c]))
        out.append(mask * inner + (1.0 - mask) * v)
    return out


def x_messages(vec):
    low_half = rows() < 4
    to_high, to_low = [], []
    for j in range(HALF):
        a, b = vec[j], vec[j + HALF]
        to_high.append(jnp.where(low_half, down(a, 4), b))
        to_low.append(jnp.where(low_half, a, down(b, 4)))
    return to_high, to_low


def x_halo(low, high):
    low_half = rows() < 4
    first = [jnp.where(low_half, a, down(b, 4)) for a, b in zip(low, high)]
    second = [jnp.where(low_half, down(a, 4), b) for a, b in zip(low, high)]
    return first + second


def z_messages(vec):
    z = rows() % 4
    to_high, to_low = [], []
    for c in range(3):
        up_tile, down_tile = up(vec[c], 3), vec[c]
        for k in range(1, 4):
            t = vec[c + 3 * k]
            up_tile = jnp.where(z == k, up(t, 3 - k) if k < 3 else t, up_tile)
            down_tile = jnp.where(z == k, down(t, k), down_tile)
        to_high.append(up_tile)
        to_low.append(down_tile)
    return to_high, to_low


def z_halo(zd, low, high):
    z = rows() % 4
    has_low = jnp.logical_and(z == 0, zd > 0)
    has_high = jnp.logical_and(z == 3, zd < 3)
    out = []
    for c in range(COMP):
        k, at = c // 3, c % 3
        a = up(low[at], k) if k else low[at]
        b = down(high[at], 3 - k) if k < 3 else high[at]
        out.append(jnp.where(has_low, a, jnp.where(has_high, b, 0.0)))
    return out


def write_faces(here, mask, vec, face_ref, swap_ref):
    core, zd = here[0], here[1]
    first = core == 0
    mv = [mask * v for v in vec]
    x_high, x_low = x_messages(mv)
    z_high, z_low = z_messages(mv)
    for j in range(HALF):
        in_chip = pick(first, x_high[j], x_low[j])
        swap_ref[j] = pick(first, x_low[j], x_high[j])
        for other in range(4):
            along = pick(other > zd, z_high[j % 3], z_low[j % 3])
            face_ref[other, j] = pick(first, along, in_chip)
            face_ref[4 + other, j] = pick(first, in_chip, along)


def read_faces(here, face_ref, swap_ref):
    core, zd = here[0], here[1]
    first = core == 0
    chip_at = (1 - core) * 4 + zd
    low_at = core * 4 + jnp.maximum(zd - 1, 0)
    high_at = core * 4 + jnp.minimum(zd + 1, 3)
    low, high = [], []
    for j in range(HALF):
        chip, cross = face_ref[chip_at, j], swap_ref[j]
        low.append(pick(first, cross, chip))
        high.append(pick(first, chip, cross))
    hz = z_halo(zd, [face_ref[low_at, c] for c in range(3)], [face_ref[high_at, c] for c in range(3)])
    return x_halo(low, high), hz


def write_layers(here, mask, vec, resid, chip_ref, cross_ref):
    first = here[0] == 0
    r_high, r_low = x_messages(resid)
    v_high, v_low = x_messages([mask * v for v in vec])
    for n, (high, low) in enumerate(zip(r_high + v_high + [mask], r_low + v_low + [mask])):
        chip_ref[n] = pick(first, high, low)
        cross_ref[n] = pick(first, low, high)


def restrict(own, beside, above):
    kinds = [own, beside] + ([above] if above is not None else [])
    depth = 8 * len(kinds)
    l, o = rows((128, 128)), lanes((128, 128))
    low = jnp.where(o < 64, hat(l - 2 * o), 0.0).astype(BF16)
    high = jnp.where(o >= 64, hat(l - 2 * (o - 64)), 0.0).astype(BF16)
    a = jnp.concatenate([kind[j] for j in range(HALF) for kind in kinds], axis=0)
    b = jnp.concatenate([kind[j + HALF] for j in range(HALF) for kind in kinds], axis=0)
    along_y = (dot_right(a, low) + dot_right(b, high)) * 0.125
    blocks = [along_y[depth * j : depth * j + depth] for j in range(HALF)]
    stacked = jnp.concatenate(
        [jnp.concatenate(blocks[:3], axis=1), jnp.concatenate(blocks[3:], axis=1)], axis=0
    )
    o, k = rows((8, 2 * depth)), lanes((8, 2 * depth))
    kind, s = (k % depth) // 8, k % 8
    z = s % 4
    outer_x = jnp.where(s < 4, -1, 2)
    in_own = jnp.logical_or(z == 0, z == 3)
    x = jnp.where(kind == 0, s // 4, jnp.where(kind == 1, outer_x, jnp.where(in_own, s // 4, outer_x)))
    fine_z = jnp.where(kind == 2, jnp.where(z < 2, -1, 4), z)
    weights = hat(x) * hat(fine_z - 2 * (o % 4 - 1))
    weights = jnp.where(o // 4 == k // depth, weights, 0.0).astype(BF16)
    result = dot_left(weights, stacked) * (1.0 / 64.0)
    return [result[:, 128 * jj : 128 * jj + 128] for jj in range(3)]


def packed_blocks(smoother_ref, reaction_ref, here, sums_ref):
    l, o = rows((128, 128)), lanes((128, 128))
    weights = jnp.where(l // 32 == o % 4, 1.0 / 256.0, 0.0).astype(BF16)
    zero = jnp.zeros((16, 128), F32)
    for a, ref in enumerate((smoother_ref, reaction_ref)):
        for n in range(0, COMP * COMP, 2):
            pair = ref[pl.ds(n * 8, 16), :].astype(F32)
            sums_ref[a, pl.ds(n, 1), :] = jnp.sum(pair[:8], axis=0, keepdims=True)
            sums_ref[a, pl.ds(n + 1, 1), :] = jnp.sum(pair[8:], axis=0, keepdims=True)
        sums_ref[a, pl.ds(144, 16), :] = zero
        sums_ref[a] = dot_right(sums_ref[a], weights)
    s, lane = rows((16, 128)), lanes((16, 128))
    out = zero
    for k in range(8):
        for a in range(2):
            for half in range(2):
                part = sums_ref[a, pl.ds(72 * half + 9 * k, 16), :]
                out = jnp.where(lane // 4 == 4 * k + 2 * a + half, part, out)
    coarse = jnp.broadcast_to(packed_mask_of(here)[:1], (16, 128))
    fine = jnp.broadcast_to(fine_mask_of(here)[:1], (16, 128))
    return jnp.where(s < 9, out, jnp.where(s == 9, coarse, jnp.where(s == 10, fine, 0.0)))


def expand_channel(get_row):
    owner = rows() // 2
    out = jnp.broadcast_to(get_row(0), TILE)
    for zd in range(1, 4):
        out = jnp.where(owner == zd, jnp.broadcast_to(get_row(zd), TILE), out)
    return out


def slots_of(p):
    right = p // 2
    out = []
    for w in range(7):
        x = p - CENTRE + w
        before = jnp.where(right == 0, x + 7, 7)
        after = jnp.where(right == 1, x, 7)
        out.append(jnp.where(x < 0, before, jnp.where(x > 3, after, x)))
    return out


def coarse_product(bx_ref, which, w, vec):
    left = lanes() < 64
    both = [None] * COMP
    for j in range(HALF):
        turned = pltpu.roll(vec[j], 64, 1)
        both[j] = jnp.where(left, vec[j], turned)
        both[j + HALF] = jnp.where(left, turned, vec[j])
    out = []
    for j in range(HALF):
        acc = None
        for d in range(COMP):
            term = bx_ref[w, j * COMP + d, which] * both[d]
            acc = term if acc is None else acc + term
        out.append(acc)
    return out


def coarse_smooth(bx_ref, mask, w, resid):
    prod = coarse_product(bx_ref, 0, w, resid)
    return [mask * a + (1.0 - mask) * r for a, r in zip(prod, resid)]


def expand_blocks(win_ref, bx_ref, slots):
    flat = jnp.concatenate([win_ref[slot, r] for slot in slots for r in range(9)], axis=0)
    pieces = jnp.concatenate(split(flat, 2), axis=1)
    l, o = rows((256, 256)) % 128, lanes((256, 256))
    target = (o // 128) * 8 + ((o % 128) // 64) * 4 + (o % 64) // 16
    for k in range(8):
        weights = jnp.where(l == 16 * k + target, 1.0, 0.0).astype(BF16)
        out = dot(pieces, weights)
        for w in range(7):
            for r in range(9):
                tile = out[(w * 9 + r) * 8 : (w * 9 + r) * 8 + 8]
                bx_ref[w, 9 * k + r, 0] = tile[:, :128]
                if 0 < w < 6:
                    bx_ref[w, 9 * k + r, 1] = tile[:, 128:]


def solve_coarse(diff_ref, rhs, slots, win_ref, bx_ref):
    s, lane = rows(), lanes()
    left = lane < 64
    inner_lane = lane % 64
    coeffs = [
        0.25 * jnp.where(left, diff_ref[j], diff_ref[j + HALF])
        for j in range(HALF)
    ]
    masks = [win_ref[slots[w], 9] for w in range(7)]
    b = [rhs(w) for w in range(7)]
    v = [coarse_smooth(bx_ref, masks[w], w, b[w]) for w in range(7)]
    for edge in (1, 2):
        mv = [[masks[w] * t for t in v[w]] if v[w] is not None else None for w in range(7)]
        new = [None] * 7
        for w in range(edge, 7 - edge):
            prod = coarse_product(bx_ref, 1, w, v[w])
            resid = []
            for j in range(HALF):
                t = mv[w][j]
                total = mv[w - 1][j] + mv[w + 1][j]
                total = total + jnp.where(s > 0, down(t, 1), 0.0) + jnp.where(s < 7, up(t, 1), 0.0)
                total = total + jnp.where(inner_lane > 0, pltpu.roll(t, 1, 1), 0.0)
                total = total + jnp.where(inner_lane < 63, pltpu.roll(t, 127, 1), 0.0)
                inner = prod[j] + coeffs[j] * (6.0 * v[w][j] - total)
                resid.append(b[w][j] - (masks[w] * inner + (1.0 - masks[w]) * v[w][j]))
            step = coarse_smooth(bx_ref, masks[w], w, resid)
            new[w] = [x + y for x, y in zip(v[w], step)]
        v = new
    return v[2:5]


def prolong(here, q):
    zd = here[1]
    o, k = rows((24, 24)), lanes((24, 24))
    group, s = o // 8, o % 8
    z = s % 4
    fx = jnp.where(group == 1, jnp.where(s < 4, -1, 2), s // 4)
    fz = jnp.where(group == 2, jnp.where(z == 0, -1, 4), z) + 4 * zd
    weights = hat(fx - 2 * (k // 8 - 1)) * hat(fz - 2 * (k % 8))
    unused = jnp.logical_and(group == 2, jnp.logical_or(z == 1, z == 2))
    weights = jnp.where(unused, 0.0, weights * 0.0625).astype(BF16)
    stacked = jnp.concatenate([jnp.concatenate(row, axis=1) for row in q], axis=0)
    xz = dot_left(weights, stacked)
    tall = jnp.concatenate([xz[:, 128 * j : 128 * j + 128] for j in range(HALF)], axis=0)
    a, f = rows((128, 256)), lanes((128, 256))
    along = hat(f % 128 - 2 * (a % 64)) * 0.25
    along = jnp.where(a // 64 == f // 128, along, 0.0).astype(BF16)
    fine = dot_right(tall, along)
    groups = []
    for g in range(3):
        tiles = [fine[24 * j + 8 * g : 24 * j + 8 * g + 8] for j in range(HALF)]
        groups.append([t[:, :128] for t in tiles] + [t[:, 128:] for t in tiles])
    return groups


def masks_around(zd, tile):
    own = pltpu.roll(tile, lax.rem(8 - 2 * zd, 8), 0)
    return own[7:8], own[:1], own[2:3]


def outside_masks(zd, tiles):
    s = rows()
    z = s % 4
    _, low_x, _ = masks_around(zd, tiles[0])
    low_z, _, high_z = masks_around(zd, tiles[1])
    _, high_x, _ = masks_around(zd, tiles[2])
    mask_x = jnp.where(s < 4, jnp.broadcast_to(low_x, TILE), jnp.broadcast_to(high_x, TILE))
    mask_z = jnp.where(
        jnp.logical_and(z == 0, zd > 0),
        jnp.broadcast_to(low_z, TILE),
        jnp.where(jnp.logical_and(z == 3, zd < 3), jnp.broadcast_to(high_z, TILE), 0.0),
    )
    return mask_x, mask_z


def layer_masks(zd, tiles):
    s = rows()
    z = s % 4
    around = [masks_around(zd, tile) for tile in tiles]
    below = [jnp.broadcast_to(a[0], TILE) for a in around]
    above = [jnp.broadcast_to(a[2], TILE) for a in around]
    low = jnp.where(z == 0, below[1], jnp.where(s < 4, below[0], below[2]))
    high = jnp.where(z == 3, above[1], jnp.where(s < 4, above[0], above[2]))
    low = jnp.where(zd > 0, low, 0.0)
    high = jnp.where(zd < 3, high, 0.0)
    return jnp.where(z < 2, low, high)


ZEROS = [0.0] * COMP


def first_kernel(here, src_ref, smoother_ref, u_ref, z_ref):
    mask = fine_mask_of(here)
    zd = here[1]
    u = smooth(smoother_ref, mask, load(src_ref))
    for c in range(COMP):
        u_ref[c] = u[c]
    high, low = z_messages([mask * v for v in u])
    for other in range(4):
        for n in range(3):
            z_ref[other, n] = pick(other > zd, high[n], low[n])


def blocks_kernel(here, smoother_ref, reaction_ref, out_ref, sums_ref):
    packed = packed_blocks(smoother_ref, reaction_ref, here, sums_ref)
    out_ref[0] = packed[:8]
    out_ref[1] = packed[8:]


def part_kernel(
    here, diff_ref, src_ref, reaction_ref, u_ref, z_ref, r_ref, chip_ref, cross_ref
):
    mask = fine_mask_of(here)
    zd = here[1]
    u = load(u_ref)
    below, above = jnp.maximum(zd - 1, 0), jnp.minimum(zd + 1, 3)
    hz = z_halo(zd, [z_ref[below, n] for n in range(3)], [z_ref[above, n] for n in range(3)])
    au = operator(reaction_ref, diff_ref, mask, u, ZEROS, hz)
    resid = [src_ref[c] - au[c] for c in range(COMP)]
    for c in range(COMP):
        r_ref[c] = resid[c]
    write_layers(here, mask, u, resid, chip_ref, cross_ref)


def send_kernel(
    again, here, diff_ref, u_ref, part_ref, chip_ref, cross_ref, extra_ref, r_ref, out_ref
):
    mask = fine_mask_of(here)
    zd = here[1]
    first = here[0] == 0
    low = [pick(first, cross_ref[n], chip_ref[n]) for n in range(13)]
    high = [pick(first, chip_ref[n], cross_ref[n]) for n in range(13)]
    hr = x_halo(low[:6], high[:6])
    hv = x_halo(low[6:12], high[6:12])
    mask_x = jnp.where(rows() < 4, low[12], high[12])
    mv = [mask * u_ref[c] for c in range(COMP)]
    own = [part_ref[c] + mask * (diff_ref[c] * hv[c]) for c in range(COMP)]
    beside = [hr[c] + mask_x * (diff_ref[c] * mv[c]) for c in range(COMP)]
    for c in range(COMP):
        r_ref[c] = own[c]
    above = None
    if again:
        z = rows() % 4
        inner = jnp.logical_or(z == 0, z == 3)
        edge = layer_masks(zd, [extra_ref[n] for n in range(3)])
        above = []
        for c in range(COMP):
            outer = jnp.where(z == 1, down(hv[c], 1), up(hv[c], 1))
            above.append(edge * (diff_ref[c] * jnp.where(inner, mv[c], outer)))
    tiles = restrict(own, beside, above)
    if not again:
        tiles = tiles + [extra_ref[0], extra_ref[1]]
    for n, tile in enumerate(tiles):
        for target in range(16):
            out_ref[target, n] = tile
    if again:
        z_high, z_low = z_messages(mv)
        for n in range(3):
            for other in range(4):
                tile = pick(other > zd, z_high[n], z_low[n])
                for q in range(4):
                    out_ref[q * 4 + other, 3 + n] = tile


def gather_kernel(with_blocks, here, recv_ref, own_ref, far_ref, near_ref):
    right = here[2] // 2
    s = rows()
    low_half = s < 4
    for q in range(4):
        for jj in range(3):
            m0, m1, m2, m3 = [recv_ref[q * 4 + zd, jj] for zd in range(4)]
            even = (jnp.where(low_half, m0, down(m2, 4)), jnp.where(low_half, down(m0, 4), m2))
            odd = (jnp.where(low_half, m1, down(m3, 4)), jnp.where(low_half, down(m1, 4), m3))
            for n in range(2):
                own_ref[q, jj + 3 * n] = jnp.where(s < 7, up(even[n], 1), 0.0) + jnp.where(
                    s > 0, down(odd[n], 1), 0.0
                )
    for e in range(3):
        for j in range(HALF):
            far_ref[e * 6 + j] = own_ref[right + e, j]
    for j in range(HALF):
        near_ref[j] = own_ref[3 * right, j]
    if with_blocks:
        for n in range(BRICK_TILES):
            for e in range(3):
                far_ref[18 + e * BRICK_TILES + n] = brick_tile(recv_ref, right + e, n)
            near_ref[6 + n] = brick_tile(recv_ref, 3 * right, n)


def brick_tile(recv_ref, q, n):
    s = rows()
    out = None
    for at in range(8):
        r = 2 * n + at // 4
        row = recv_ref[q * 4 + at % 4, 3 + r // 8, pl.ds(r % 8, 1), :]
        row = jnp.broadcast_to(row, TILE)
        out = row if out is None else jnp.where(s == at, row, out)
    return out


def fill_own(recv_ref, win_ref):
    for r in range(CHANNELS):
        at, tile = pl.ds(r % 8, 1), r // 8
        for q in range(4):
            win_ref[q, r] = expand_channel(lambda zd: recv_ref[q * 4 + zd, 3 + tile, at, :])


def fill_others(far_ref, near_ref, win_ref):
    for r in range(CHANNELS):
        tile, base = r // 2, 4 * (r % 2)
        for e in range(3):
            win_ref[4 + e, r] = expand_channel(
                lambda zd: far_ref[18 + e * BRICK_TILES + tile, pl.ds(base + zd, 1), :]
            )
        win_ref[7, r] = expand_channel(lambda zd: near_ref[6 + tile, pl.ds(base + zd, 1), :])


def correct_kernel(
    again,
    here,
    diff_ref,
    reaction_ref,
    smoother_ref,
    u_ref,
    r_ref,
    recv_ref,
    own_ref,
    far_ref,
    near_ref,
    *rest,
):
    zd, p, brick, bricks = here[1], here[2], here[3], here[4]
    if again:
        win_ref, new_ref, face_ref, swap_ref, rhs_ref, bx_ref = rest
    else:
        new_ref, face_ref, swap_ref, win_ref, around_ref, rhs_ref, bx_ref = rest
        fill_own(recv_ref, win_ref)
        fill_others(far_ref, near_ref, win_ref)
    slots = slots_of(p)
    expand_blocks(win_ref, bx_ref, slots)
    for j in range(HALF):
        for q in range(4):
            rhs_ref[q, j] = own_ref[q, j]
        for e in range(3):
            rhs_ref[4 + e, j] = far_ref[e * 6 + j]
        rhs_ref[7, j] = near_ref[j]

    def rhs(w):
        place = brick + (w - CENTRE)
        inside = jnp.logical_and(place >= 0, place < bricks)
        return [pick(inside, rhs_ref[slots[w], j], 0.0) for j in range(HALF)]

    q = solve_coarse(diff_ref, rhs, slots, win_ref, bx_ref)
    inside, hx, hz = prolong(here, q)
    fine_masks = [win_ref[slots[CENTRE + n], 10] for n in (-1, 0, 1)]
    if not again:
        for n in range(3):
            around_ref[n] = fine_masks[n]
    mask_x, mask_z = outside_masks(zd, fine_masks)
    hx = [mask_x * t for t in hx]
    hz = [mask_z * t for t in hz]
    mask = fine_mask_of(here)
    change = operator(reaction_ref, diff_ref, mask, inside, hx, hz)
    resid = [r_ref[c] - change[c] for c in range(COMP)]
    if again:
        below = p * 4 + jnp.maximum(zd - 1, 0)
        above = p * 4 + jnp.minimum(zd + 1, 3)
        halo = z_halo(
            zd, [recv_ref[below, 3 + n] for n in range(3)], [recv_ref[above, 3 + n] for n in range(3)]
        )
        resid = [r + mask * (diff_ref[c] * h) for c, (r, h) in enumerate(zip(resid, halo))]
    step = smooth(smoother_ref, mask, resid)
    new = [u_ref[c] + inside[c] + step[c] for c in range(COMP)]
    for c in range(COMP):
        new_ref[c] = new[c]
    write_faces(here, mask, new, face_ref, swap_ref)


def residual(here, diff_ref, src_ref, reaction_ref, u_ref, face_ref, swap_ref):
    mask = fine_mask_of(here)
    u = load(u_ref)
    hx, hz = read_faces(here, face_ref, swap_ref)
    au = operator(reaction_ref, diff_ref, mask, u, hx, hz)
    return mask, u, [src_ref[c] - au[c] for c in range(COMP)]


def sweep_kernel(
    here, diff_ref, src_ref, reaction_ref, u_ref, face_ref, swap_ref, smoother_ref,
    new_ref, part_ref, chip_ref, cross_ref,
):
    mask, u, resid = residual(
        here, diff_ref, src_ref, reaction_ref, u_ref, face_ref, swap_ref
    )
    step = smooth(smoother_ref, mask, resid)
    new = [a + b for a, b in zip(u, step)]
    au = operator(reaction_ref, diff_ref, mask, new, ZEROS, ZEROS)
    part = [src_ref[c] - au[c] for c in range(COMP)]
    for c in range(COMP):
        new_ref[c] = new[c]
        part_ref[c] = part[c]
    write_layers(here, mask, new, part, chip_ref, cross_ref)


def last_kernel(
    here, diff_ref, src_ref, reaction_ref, u_ref, face_ref, swap_ref, r_ref
):
    _, _, resid = residual(
        here, diff_ref, src_ref, reaction_ref, u_ref, face_ref, swap_ref
    )
    for c in range(COMP):
        r_ref[c] = resid[c]


VMEM_SPEC = pl.BlockSpec(memory_space=pltpu.VMEM)


def place():
    core = lax.axis_index("core")
    p = lax.axis_index("xc") * 2 + core
    brick = lax.axis_index("xg") * 4 + p
    return [core, lax.axis_index("gz"), p, brick, lax.axis_size("xg") * 4]


def spread(row_ref):
    return [
        jnp.broadcast_to(row_ref[:, n : n + 1], TILE).astype(F32) for n in range(row_ref.shape[1])
    ]


def call(kernel, name, small, arrays, outs, scratch=()):
    def body(*refs):
        tiles = [spread(ref) for ref in refs[: len(small)]]
        position = place() + (tiles[0] if tiles else [])
        kernel(position, *tiles[1:], *refs[len(small) :])

    return pl.pallas_call(
        body,
        name=name,
        in_specs=[VMEM_SPEC] * (len(small) + len(arrays)),
        out_specs=[VMEM_SPEC] * len(outs),
        out_shape=[jax.ShapeDtypeStruct(shape, F32) for shape in outs],
        scratch_shapes=[pltpu.VMEM(shape, F32) for shape in scratch],
        compiler_params=pltpu.CompilerParams(vmem_limit_bytes=VMEM_LIMIT),
    )(*small, *arrays)


VEC = (COMP, 8, 128)
FACE = (8, HALF, 8, 128)
SWAP = (HALF, 8, 128)
LAYER = (13, 8, 128)


def local(bricks, source, reaction, smoother, diffusion, active):
    act = active.reshape(1, 4)
    small = [act, diffusion.reshape(1, COMP)]
    src = source.reshape(VEC)
    react = reaction.reshape(COMP * COMP * 8, 128)
    smoo = smoother.reshape(COMP * COMP * 8, 128)
    groups = bricks // 4

    chip_pairs = [(i, i ^ 1) for i in range(bricks)]
    pairs = [(i, i + 1) for i in range(1, bricks - 1, 2)]
    swap_pairs = pairs + [(b, a) for a, b in pairs]
    far_pairs, near_pairs = [], []
    for i in range(bricks):
        g, p = divmod(i, 4)
        step = 1 if p >= 2 else -1
        if 0 <= g + step < groups:
            far_pairs.append((i, 4 * (g + step) + 3 - p))
            if p in (0, 3):
                near_pairs.append((i, i + 3 * step))

    def faces(face, swap):
        swap = lax.ppermute(swap, X_AXES, swap_pairs)
        face = lax.all_to_all(face, ("core", "gz"), 0, 0)
        return face, swap

    def layers(chip, cross):
        return lax.ppermute(chip, X_AXES, chip_pairs), lax.ppermute(cross, X_AXES, swap_pairs)

    def to_coarse(message, with_blocks):
        recv = lax.all_to_all(message, ("xc", "core", "gz"), 0, 0)
        far_rows, near_rows = (18 + 3 * BRICK_TILES, 6 + BRICK_TILES) if with_blocks else (18, 6)
        own, far, near = call(
            functools.partial(gather_kernel, with_blocks),
            "gather",
            [],
            [recv],
            [(4, HALF, 8, 128), (far_rows, 8, 128), (near_rows, 8, 128)],
        )
        far = lax.ppermute(far, X_AXES, far_pairs)
        near = lax.ppermute(near, X_AXES, near_pairs)
        return recv, own, far, near

    u, edges = call(first_kernel, "first", [act], [src, smoo], [VEC, (4, 3, 8, 128)])
    (packed,) = call(blocks_kernel, "blocks", [act], [smoo, react], [(2, 8, 128)], [(2, 160, 128)])
    edges = lax.all_to_all(edges, "gz", 0, 0)
    part, chip, cross = call(
        part_kernel, "part", small, [src, react, u, edges], [VEC, LAYER, LAYER]
    )
    chip, cross = layers(chip, cross)
    resid, message = call(
        functools.partial(send_kernel, False),
        "send",
        small,
        [u, part, chip, cross, packed],
        [VEC, (16, 5, 8, 128)],
    )
    recv, own, far, near = to_coarse(message, True)
    rhs_shape, bx_shape, win_shape = (8, HALF, 8, 128), (7, 72, 2, 8, 128), (8, CHANNELS, 8, 128)
    u, face, swap, window, around = call(
        functools.partial(correct_kernel, False),
        "correct",
        small,
        [react, smoo, u, resid, recv, own, far, near],
        [VEC, FACE, SWAP, win_shape, (3, 8, 128)],
        [rhs_shape, bx_shape],
    )
    face, swap = faces(face, swap)
    u, part, chip, cross = call(
        sweep_kernel, "sweep", small, [src, react, u, face, swap, smoo], [VEC, VEC, LAYER, LAYER]
    )
    chip, cross = layers(chip, cross)
    resid, message = call(
        functools.partial(send_kernel, True),
        "send",
        small,
        [u, part, chip, cross, around],
        [VEC, (16, 6, 8, 128)],
    )
    recv, own, far, near = to_coarse(message, False)
    u, face, swap = call(
        functools.partial(correct_kernel, True),
        "correct",
        small,
        [react, smoo, u, resid, recv, own, far, near, window],
        [VEC, FACE, SWAP],
        [rhs_shape, bx_shape],
    )
    face, swap = faces(face, swap)
    (resid,) = call(last_kernel, "last", small, [src, react, u, face, swap], [VEC])
    return u.reshape(source.shape), resid.reshape(source.shape)


def solution(mesh):
    bricks = mesh.shape["bricks"]
    gz = mesh.shape["gz"]
    inner = Mesh(mesh.devices.reshape(bricks // 4, 2, 2, gz), X_AXES + ("gz",))
    in_specs = (
        P(None, X_AXES, "gz", None),
        P(None, None, X_AXES, "gz", None),
        P(None, None, X_AXES, "gz", None),
        P(),
        P(X_AXES, "gz", None),
    )
    out_specs = (P(None, X_AXES, "gz", None), P(None, X_AXES, "gz", None))
    return jax.shard_map(
        functools.partial(local, bricks),
        mesh=inner,
        in_specs=in_specs,
        out_specs=out_specs,
        check_vma=False,
    )
```

```python
import functools

import jax
import jax.numpy as jnp
from jax import lax
from jax.experimental import pallas as pl
from jax.experimental.pallas import tpu as pltpu
from jax.sharding import Mesh
from jax.sharding import PartitionSpec as P

COMP = 12
HALF = 6
F32 = jnp.float32
BF16 = jnp.bfloat16
X_AXES = ("xg", "xc", "core")
TILE = (8, 128)
CHANNELS = 11
BRICK_TILES = 6
CENTRE = 3
VMEM_LIMIT = 16 * 1024 * 1024


def rows(shape=TILE):
    return lax.broadcasted_iota(jnp.int32, shape, 0)


def lanes(shape=TILE):
    return lax.broadcasted_iota(jnp.int32, shape, 1)


def up(x, by):
    return pltpu.roll(x, 8 - by, 0)


def down(x, by):
    return pltpu.roll(x, by, 0)


def pick(cond, a, b):
    return jnp.where(cond, a, b)


def hat(diff):
    inner = jnp.logical_or(diff == 0, diff == 1)
    outer = jnp.logical_or(diff == -1, diff == 2)
    return jnp.where(inner, 3.0, jnp.where(outer, 1.0, 0.0)).astype(F32)


def split(x, parts):
    pieces = []
    for _ in range(parts):
        piece = x.astype(BF16)
        pieces.append(piece)
        x = x - piece.astype(F32)
    return pieces


def dot(a, b):
    return jnp.dot(a, b, preferred_element_type=F32)


def dot_right(x, weights, parts=3):
    return dot(jnp.concatenate(split(x, parts), axis=1), jnp.concatenate([weights] * parts, axis=0))


def dot_left(weights, x, parts=3):
    return dot(jnp.concatenate([weights] * parts, axis=1), jnp.concatenate(split(x, parts), axis=0))


def fine_mask_of(here):
    brick = lanes() // 32
    out = jnp.zeros(TILE, F32)
    for b in range(4):
        out = jnp.where(brick == b, here[5 + b], out)
    return out


def packed_mask_of(here):
    brick = (lanes() % 64) // 16
    out = jnp.zeros(TILE, F32)
    for b in range(4):
        out = jnp.where(brick == b, here[5 + b], out)
    return out


def load(ref):
    return [ref[c] for c in range(COMP)]


def block_product(blocks_ref, vec):
    out = []
    for c in range(COMP):
        acc = None
        for d in range(0, COMP, 2):
            pair = blocks_ref[pl.ds((c * COMP + d) * 8, 16), :].astype(F32)
            term = pair[:8] * vec[d] + pair[8:] * vec[d + 1]
            acc = term if acc is None else acc + term
        out.append(acc)
    return out


def smooth(smoother_ref, mask, resid):
    prod = block_product(smoother_ref, resid)
    return [mask * a + (1.0 - mask) * r for a, r in zip(prod, resid)]


def neighbours(mv, hx, hz):
    z = rows() % 4
    lane = lanes()
    total = down(mv, 4) + hx + hz
    total = total + jnp.where(z > 0, down(mv, 1), 0.0) + jnp.where(z < 3, up(mv, 1), 0.0)
    total = total + jnp.where(lane > 0, pltpu.roll(mv, 1, 1), 0.0)
    return total + jnp.where(lane < 127, pltpu.roll(mv, 127, 1), 0.0)


def operator(reaction_ref, diff_ref, mask, vec, hx, hz):
    prod = block_product(reaction_ref, vec)
    out = []
    for c in range(COMP):
        v = vec[c]
        inner = prod[c] + diff_ref[c] * (6.0 * v - neighbours(mask * v, hx[c], hz[c]))
        out.append(mask * inner + (1.0 - mask) * v)
    return out


def x_messages(vec):
    low_half = rows() < 4
    to_high, to_low = [], []
    for j in range(HALF):
        a, b = vec[j], vec[j + HALF]
        to_high.append(jnp.where(low_half, down(a, 4), b))
        to_low.append(jnp.where(low_half, a, down(b, 4)))
    return to_high, to_low


def x_halo(low, high):
    low_half = rows() < 4
    first = [jnp.where(low_half, a, down(b, 4)) for a, b in zip(low, high)]
    second = [jnp.where(low_half, down(a, 4), b) for a, b in zip(low, high)]
    return first + second


def z_messages(vec):
    z = rows() % 4
    to_high, to_low = [], []
    for c in range(3):
        up_tile, down_tile = up(vec[c], 3), vec[c]
        for k in range(1, 4):
            t = vec[c + 3 * k]
            up_tile = jnp.where(z == k, up(t, 3 - k) if k < 3 else t, up_tile)
            down_tile = jnp.where(z == k, down(t, k), down_tile)
        to_high.append(up_tile)
        to_low.append(down_tile)
    return to_high, to_low


def z_halo(zd, low, high):
    z = rows() % 4
    has_low = jnp.logical_and(z == 0, zd > 0)
    has_high = jnp.logical_and(z == 3, zd < 3)
    out = []
    for c in range(COMP):
        k, at = c // 3, c % 3
        a = up(low[at], k) if k else low[at]
        b = down(high[at], 3 - k) if k < 3 else high[at]
        out.append(jnp.where(has_low, a, jnp.where(has_high, b, 0.0)))
    return out


def write_faces(here, mask, vec, face_ref, swap_ref):
    core, zd = here[0], here[1]
    first = core == 0
    mv = [mask * v for v in vec]
    x_high, x_low = x_messages(mv)
    z_high, z_low = z_messages(mv)
    for j in range(HALF):
        in_chip = pick(first, x_high[j], x_low[j])
        swap_ref[j] = pick(first, x_low[j], x_high[j])
        for other in range(4):
            along = pick(other > zd, z_high[j % 3], z_low[j % 3])
            face_ref[other, j] = pick(first, along, in_chip)
            face_ref[4 + other, j] = pick(first, in_chip, along)


def read_faces(here, face_ref, swap_ref):
    core, zd = here[0], here[1]
    first = core == 0
    chip_at = (1 - core) * 4 + zd
    low_at = core * 4 + jnp.maximum(zd - 1, 0)
    high_at = core * 4 + jnp.minimum(zd + 1, 3)
    low, high = [], []
    for j in range(HALF):
        chip, cross = face_ref[chip_at, j], swap_ref[j]
        low.append(pick(first, cross, chip))
        high.append(pick(first, chip, cross))
    hz = z_halo(zd, [face_ref[low_at, c] for c in range(3)], [face_ref[high_at, c] for c in range(3)])
    return x_halo(low, high), hz


def write_layers(here, mask, vec, resid, chip_ref, cross_ref):
    first = here[0] == 0
    r_high, r_low = x_messages(resid)
    v_high, v_low = x_messages([mask * v for v in vec])
    for n, (high, low) in enumerate(zip(r_high + v_high + [mask], r_low + v_low + [mask])):
        chip_ref[n] = pick(first, high, low)
        cross_ref[n] = pick(first, low, high)


def restrict(own, beside, above):
    kinds = [own, beside] + ([above] if above is not None else [])
    depth = 8 * len(kinds)
    l, o = rows((128, 128)), lanes((128, 128))
    low = jnp.where(o < 64, hat(l - 2 * o), 0.0).astype(BF16)
    high = jnp.where(o >= 64, hat(l - 2 * (o - 64)), 0.0).astype(BF16)
    a = jnp.concatenate([kind[j] for j in range(HALF) for kind in kinds], axis=0)
    b = jnp.concatenate([kind[j + HALF] for j in range(HALF) for kind in kinds], axis=0)
    along_y = (dot_right(a, low) + dot_right(b, high)) * 0.125
    blocks = [along_y[depth * j : depth * j + depth] for j in range(HALF)]
    stacked = jnp.concatenate(
        [jnp.concatenate(blocks[:3], axis=1), jnp.concatenate(blocks[3:], axis=1)], axis=0
    )
    o, k = rows((8, 2 * depth)), lanes((8, 2 * depth))
    kind, s = (k % depth) // 8, k % 8
    z = s % 4
    outer_x = jnp.where(s < 4, -1, 2)
    in_own = jnp.logical_or(z == 0, z == 3)
    x = jnp.where(kind == 0, s // 4, jnp.where(kind == 1, outer_x, jnp.where(in_own, s // 4, outer_x)))
    fine_z = jnp.where(kind == 2, jnp.where(z < 2, -1, 4), z)
    weights = hat(x) * hat(fine_z - 2 * (o % 4 - 1))
    weights = jnp.where(o // 4 == k // depth, weights, 0.0).astype(BF16)
    result = dot_left(weights, stacked) * (1.0 / 64.0)
    return [result[:, 128 * jj : 128 * jj + 128] for jj in range(3)]


def packed_blocks(smoother_ref, reaction_ref, here, sums_ref):
    l, o = rows((128, 128)), lanes((128, 128))
    weights = jnp.where(l // 32 == o % 4, 1.0 / 256.0, 0.0).astype(BF16)
    zero = jnp.zeros((16, 128), F32)
    for a, ref in enumerate((smoother_ref, reaction_ref)):
        for n in range(0, COMP * COMP, 2):
            pair = ref[pl.ds(n * 8, 16), :].astype(F32)
            sums_ref[a, pl.ds(n, 1), :] = jnp.sum(pair[:8], axis=0, keepdims=True)
            sums_ref[a, pl.ds(n + 1, 1), :] = jnp.sum(pair[8:], axis=0, keepdims=True)
        sums_ref[a, pl.ds(144, 16), :] = zero
        sums_ref[a] = dot_right(sums_ref[a], weights)
    s, lane = rows((16, 128)), lanes((16, 128))
    out = zero
    for k in range(8):
        for a in range(2):
            for half in range(2):
                part = sums_ref[a, pl.ds(72 * half + 9 * k, 16), :]
                out = jnp.where(lane // 4 == 4 * k + 2 * a + half, part, out)
    coarse = jnp.broadcast_to(packed_mask_of(here)[:1], (16, 128))
    fine = jnp.broadcast_to(fine_mask_of(here)[:1], (16, 128))
    return jnp.where(s < 9, out, jnp.where(s == 9, coarse, jnp.where(s == 10, fine, 0.0)))


def expand_channel(get_row):
    owner = rows() // 2
    out = jnp.broadcast_to(get_row(0), TILE)
    for zd in range(1, 4):
        out = jnp.where(owner == zd, jnp.broadcast_to(get_row(zd), TILE), out)
    return out


def slots_of(p):
    right = p // 2
    out = []
    for w in range(7):
        x = p - CENTRE + w
        before = jnp.where(right == 0, x + 7, 7)
        after = jnp.where(right == 1, x, 7)
        out.append(jnp.where(x < 0, before, jnp.where(x > 3, after, x)))
    return out


def coarse_product(bx_ref, which, w, vec):
    left = lanes() < 64
    both = [None] * COMP
    for j in range(HALF):
        turned = pltpu.roll(vec[j], 64, 1)
        both[j] = jnp.where(left, vec[j], turned)
        both[j + HALF] = jnp.where(left, turned, vec[j])
    out = []
    for j in range(HALF):
        acc = None
        for d in range(COMP):
            term = bx_ref[w, j * COMP + d, which] * both[d]
            acc = term if acc is None else acc + term
        out.append(acc)
    return out


def coarse_smooth(bx_ref, mask, w, resid):
    prod = coarse_product(bx_ref, 0, w, resid)
    return [mask * a + (1.0 - mask) * r for a, r in zip(prod, resid)]


def expand_blocks(win_ref, bx_ref, slots):
    flat = jnp.concatenate([win_ref[slot, r] for slot in slots for r in range(9)], axis=0)
    pieces = jnp.concatenate(split(flat, 2), axis=1)
    l, o = rows((256, 256)) % 128, lanes((256, 256))
    target = (o // 128) * 8 + ((o % 128) // 64) * 4 + (o % 64) // 16
    for k in range(8):
        weights = jnp.where(l == 16 * k + target, 1.0, 0.0).astype(BF16)
        out = dot(pieces, weights)
        for w in range(7):
            for r in range(9):
                tile = out[(w * 9 + r) * 8 : (w * 9 + r) * 8 + 8]
                bx_ref[w, 9 * k + r, 0] = tile[:, :128]
                if 0 < w < 6:
                    bx_ref[w, 9 * k + r, 1] = tile[:, 128:]


def solve_coarse(diff_ref, rhs, slots, win_ref, bx_ref):
    s, lane = rows(), lanes()
    left = lane < 64
    inner_lane = lane % 64
    coeffs = [
        0.25 * jnp.where(left, diff_ref[j], diff_ref[j + HALF])
        for j in range(HALF)
    ]
    masks = [win_ref[slots[w], 9] for w in range(7)]
    b = [rhs(w) for w in range(7)]
    v = [coarse_smooth(bx_ref, masks[w], w, b[w]) for w in range(7)]
    for edge in (1, 2):
        mv = [[masks[w] * t for t in v[w]] if v[w] is not None else None for w in range(7)]
        new = [None] * 7
        for w in range(edge, 7 - edge):
            prod = coarse_product(bx_ref, 1, w, v[w])
            resid = []
            for j in range(HALF):
                t = mv[w][j]
                total = mv[w - 1][j] + mv[w + 1][j]
                total = total + jnp.where(s > 0, down(t, 1), 0.0) + jnp.where(s < 7, up(t, 1), 0.0)
                total = total + jnp.where(inner_lane > 0, pltpu.roll(t, 1, 1), 0.0)
                total = total + jnp.where(inner_lane < 63, pltpu.roll(t, 127, 1), 0.0)
                inner = prod[j] + coeffs[j] * (6.0 * v[w][j] - total)
                resid.append(b[w][j] - (masks[w] * inner + (1.0 - masks[w]) * v[w][j]))
            step = coarse_smooth(bx_ref, masks[w], w, resid)
            new[w] = [x + y for x, y in zip(v[w], step)]
        v = new
    return v[2:5]


def prolong(here, q):
    zd = here[1]
    o, k = rows((24, 24)), lanes((24, 24))
    group, s = o // 8, o % 8
    z = s % 4
    fx = jnp.where(group == 1, jnp.where(s < 4, -1, 2), s // 4)
    fz = jnp.where(group == 2, jnp.where(z == 0, -1, 4), z) + 4 * zd
    weights = hat(fx - 2 * (k // 8 - 1)) * hat(fz - 2 * (k % 8))
    unused = jnp.logical_and(group == 2, jnp.logical_or(z == 1, z == 2))
    weights = jnp.where(unused, 0.0, weights * 0.0625).astype(BF16)
    stacked = jnp.concatenate([jnp.concatenate(row, axis=1) for row in q], axis=0)
    xz = dot_left(weights, stacked)
    tall = jnp.concatenate([xz[:, 128 * j : 128 * j + 128] for j in range(HALF)], axis=0)
    a, f = rows((128, 256)), lanes((128, 256))
    along = hat(f % 128 - 2 * (a % 64)) * 0.25
    along = jnp.where(a // 64 == f // 128, along, 0.0).astype(BF16)
    fine = dot_right(tall, along)
    groups = []
    for g in range(3):
        tiles = [fine[24 * j + 8 * g : 24 * j + 8 * g + 8] for j in range(HALF)]
        groups.append([t[:, :128] for t in tiles] + [t[:, 128:] for t in tiles])
    return groups


def masks_around(zd, tile):
    own = pltpu.roll(tile, lax.rem(8 - 2 * zd, 8), 0)
    return own[7:8], own[:1], own[2:3]


def outside_masks(zd, tiles):
    s = rows()
    z = s % 4
    _, low_x, _ = masks_around(zd, tiles[0])
    low_z, _, high_z = masks_around(zd, tiles[1])
    _, high_x, _ = masks_around(zd, tiles[2])
    mask_x = jnp.where(s < 4, jnp.broadcast_to(low_x, TILE), jnp.broadcast_to(high_x, TILE))
    mask_z = jnp.where(
        jnp.logical_and(z == 0, zd > 0),
        jnp.broadcast_to(low_z, TILE),
        jnp.where(jnp.logical_and(z == 3, zd < 3), jnp.broadcast_to(high_z, TILE), 0.0),
    )
    return mask_x, mask_z


def layer_masks(zd, tiles):
    s = rows()
    z = s % 4
    around = [masks_around(zd, tile) for tile in tiles]
    below = [jnp.broadcast_to(a[0], TILE) for a in around]
    above = [jnp.broadcast_to(a[2], TILE) for a in around]
    low = jnp.where(z == 0, below[1], jnp.where(s < 4, below[0], below[2]))
    high = jnp.where(z == 3, above[1], jnp.where(s < 4, above[0], above[2]))
    low = jnp.where(zd > 0, low, 0.0)
    high = jnp.where(zd < 3, high, 0.0)
    return jnp.where(z < 2, low, high)


ZEROS = [0.0] * COMP


def first_kernel(here, src_ref, smoother_ref, u_ref, z_ref):
    mask = fine_mask_of(here)
    zd = here[1]
    u = smooth(smoother_ref, mask, load(src_ref))
    for c in range(COMP):
        u_ref[c] = u[c]
    high, low = z_messages([mask * v for v in u])
    for other in range(4):
        for n in range(3):
            z_ref[other, n] = pick(other > zd, high[n], low[n])


def blocks_kernel(here, smoother_ref, reaction_ref, out_ref, sums_ref):
    packed = packed_blocks(smoother_ref, reaction_ref, here, sums_ref)
    out_ref[0] = packed[:8]
    out_ref[1] = packed[8:]


def part_kernel(
    here, diff_ref, src_ref, reaction_ref, u_ref, z_ref, r_ref, chip_ref, cross_ref
):
    mask = fine_mask_of(here)
    zd = here[1]
    u = load(u_ref)
    below, above = jnp.maximum(zd - 1, 0), jnp.minimum(zd + 1, 3)
    hz = z_halo(zd, [z_ref[below, n] for n in range(3)], [z_ref[above, n] for n in range(3)])
    au = operator(reaction_ref, diff_ref, mask, u, ZEROS, hz)
    resid = [src_ref[c] - au[c] for c in range(COMP)]
    for c in range(COMP):
        r_ref[c] = resid[c]
    write_layers(here, mask, u, resid, chip_ref, cross_ref)


def send_kernel(
    again, here, diff_ref, u_ref, part_ref, chip_ref, cross_ref, extra_ref, r_ref, out_ref
):
    mask = fine_mask_of(here)
    zd = here[1]
    first = here[0] == 0
    low = [pick(first, cross_ref[n], chip_ref[n]) for n in range(13)]
    high = [pick(first, chip_ref[n], cross_ref[n]) for n in range(13)]
    hr = x_halo(low[:6], high[:6])
    hv = x_halo(low[6:12], high[6:12])
    mask_x = jnp.where(rows() < 4, low[12], high[12])
    mv = [mask * u_ref[c] for c in range(COMP)]
    own = [part_ref[c] + mask * (diff_ref[c] * hv[c]) for c in range(COMP)]
    beside = [hr[c] + mask_x * (diff_ref[c] * mv[c]) for c in range(COMP)]
    for c in range(COMP):
        r_ref[c] = own[c]
    above = None
    if again:
        z = rows() % 4
        inner = jnp.logical_or(z == 0, z == 3)
        edge = layer_masks(zd, [extra_ref[n] for n in range(3)])
        above = []
        for c in range(COMP):
            outer = jnp.where(z == 1, down(hv[c], 1), up(hv[c], 1))
            above.append(edge * (diff_ref[c] * jnp.where(inner, mv[c], outer)))
    tiles = restrict(own, beside, above)
    if not again:
        tiles = tiles + [extra_ref[0], extra_ref[1]]
    for n, tile in enumerate(tiles):
        for target in range(16):
            out_ref[target, n] = tile
    if again:
        z_high, z_low = z_messages(mv)
        for n in range(3):
            for other in range(4):
                tile = pick(other > zd, z_high[n], z_low[n])
                for q in range(4):
                    out_ref[q * 4 + other, 3 + n] = tile


def gather_kernel(with_blocks, here, recv_ref, own_ref, far_ref, near_ref):
    right = here[2] // 2
    s = rows()
    low_half = s < 4
    for q in range(4):
        for jj in range(3):
            m0, m1, m2, m3 = [recv_ref[q * 4 + zd, jj] for zd in range(4)]
            even = (jnp.where(low_half, m0, down(m2, 4)), jnp.where(low_half, down(m0, 4), m2))
            odd = (jnp.where(low_half, m1, down(m3, 4)), jnp.where(low_half, down(m1, 4), m3))
            for n in range(2):
                own_ref[q, jj + 3 * n] = jnp.where(s < 7, up(even[n], 1), 0.0) + jnp.where(
                    s > 0, down(odd[n], 1), 0.0
                )
    for e in range(3):
        for j in range(HALF):
            far_ref[e * 6 + j] = own_ref[right + e, j]
    for j in range(HALF):
        near_ref[j] = own_ref[3 * right, j]
    if with_blocks:
        for n in range(BRICK_TILES):
            for e in range(3):
                far_ref[18 + e * BRICK_TILES + n] = brick_tile(recv_ref, right + e, n)
            near_ref[6 + n] = brick_tile(recv_ref, 3 * right, n)


def brick_tile(recv_ref, q, n):
    s = rows()
    out = None
    for at in range(8):
        r = 2 * n + at // 4
        row = recv_ref[q * 4 + at % 4, 3 + r // 8, pl.ds(r % 8, 1), :]
        row = jnp.broadcast_to(row, TILE)
        out = row if out is None else jnp.where(s == at, row, out)
    return out


def fill_own(recv_ref, win_ref):
    for r in range(CHANNELS):
        at, tile = pl.ds(r % 8, 1), r // 8
        for q in range(4):
            win_ref[q, r] = expand_channel(lambda zd: recv_ref[q * 4 + zd, 3 + tile, at, :])


def fill_others(far_ref, near_ref, win_ref):
    for r in range(CHANNELS):
        tile, base = r // 2, 4 * (r % 2)
        for e in range(3):
            win_ref[4 + e, r] = expand_channel(
                lambda zd: far_ref[18 + e * BRICK_TILES + tile, pl.ds(base + zd, 1), :]
            )
        win_ref[7, r] = expand_channel(lambda zd: near_ref[6 + tile, pl.ds(base + zd, 1), :])


def correct_kernel(
    again,
    here,
    diff_ref,
    reaction_ref,
    smoother_ref,
    u_ref,
    r_ref,
    recv_ref,
    own_ref,
    far_ref,
    near_ref,
    *rest,
):
    zd, p, brick, bricks = here[1], here[2], here[3], here[4]
    if again:
        win_ref, new_ref, face_ref, swap_ref, rhs_ref, bx_ref = rest
    else:
        new_ref, face_ref, swap_ref, win_ref, around_ref, rhs_ref, bx_ref = rest
        fill_own(recv_ref, win_ref)
        fill_others(far_ref, near_ref, win_ref)
    slots = slots_of(p)
    expand_blocks(win_ref, bx_ref, slots)
    for j in range(HALF):
        for q in range(4):
            rhs_ref[q, j] = own_ref[q, j]
        for e in range(3):
            rhs_ref[4 + e, j] = far_ref[e * 6 + j]
        rhs_ref[7, j] = near_ref[j]

    def rhs(w):
        place = brick + (w - CENTRE)
        inside = jnp.logical_and(place >= 0, place < bricks)
        return [pick(inside, rhs_ref[slots[w], j], 0.0) for j in range(HALF)]

    q = solve_coarse(diff_ref, rhs, slots, win_ref, bx_ref)
    inside, hx, hz = prolong(here, q)
    fine_masks = [win_ref[slots[CENTRE + n], 10] for n in (-1, 0, 1)]
    if not again:
        for n in range(3):
            around_ref[n] = fine_masks[n]
    mask_x, mask_z = outside_masks(zd, fine_masks)
    hx = [mask_x * t for t in hx]
    hz = [mask_z * t for t in hz]
    mask = fine_mask_of(here)
    change = operator(reaction_ref, diff_ref, mask, inside, hx, hz)
    resid = [r_ref[c] - change[c] for c in range(COMP)]
    if again:
        below = p * 4 + jnp.maximum(zd - 1, 0)
        above = p * 4 + jnp.minimum(zd + 1, 3)
        halo = z_halo(
            zd, [recv_ref[below, 3 + n] for n in range(3)], [recv_ref[above, 3 + n] for n in range(3)]
        )
        resid = [r + mask * (diff_ref[c] * h) for c, (r, h) in enumerate(zip(resid, halo))]
    step = smooth(smoother_ref, mask, resid)
    new = [u_ref[c] + inside[c] + step[c] for c in range(COMP)]
    for c in range(COMP):
        new_ref[c] = new[c]
    write_faces(here, mask, new, face_ref, swap_ref)


def residual(here, diff_ref, src_ref, reaction_ref, u_ref, face_ref, swap_ref):
    mask = fine_mask_of(here)
    u = load(u_ref)
    hx, hz = read_faces(here, face_ref, swap_ref)
    au = operator(reaction_ref, diff_ref, mask, u, hx, hz)
    return mask, u, [src_ref[c] - au[c] for c in range(COMP)]


def sweep_kernel(
    here, diff_ref, src_ref, reaction_ref, u_ref, face_ref, swap_ref, smoother_ref,
    new_ref, part_ref, chip_ref, cross_ref,
):
    mask, u, resid = residual(
        here, diff_ref, src_ref, reaction_ref, u_ref, face_ref, swap_ref
    )
    step = smooth(smoother_ref, mask, resid)
    new = [a + b for a, b in zip(u, step)]
    au = operator(reaction_ref, diff_ref, mask, new, ZEROS, ZEROS)
    part = [src_ref[c] - au[c] for c in range(COMP)]
    for c in range(COMP):
        new_ref[c] = new[c]
        part_ref[c] = part[c]
    write_layers(here, mask, new, part, chip_ref, cross_ref)


def last_kernel(
    here, diff_ref, src_ref, reaction_ref, u_ref, face_ref, swap_ref, r_ref
):
    _, _, resid = residual(
        here, diff_ref, src_ref, reaction_ref, u_ref, face_ref, swap_ref
    )
    for c in range(COMP):
        r_ref[c] = resid[c]


VMEM_SPEC = pl.BlockSpec(memory_space=pltpu.VMEM)


def place():
    core = lax.axis_index("core")
    p = lax.axis_index("xc") * 2 + core
    brick = lax.axis_index("xg") * 4 + p
    return [core, lax.axis_index("gz"), p, brick, lax.axis_size("xg") * 4]


def spread(row_ref):
    return [
        jnp.broadcast_to(row_ref[:, n : n + 1], TILE).astype(F32) for n in range(row_ref.shape[1])
    ]


def call(kernel, name, small, arrays, outs, scratch=()):
    def body(*refs):
        tiles = [spread(ref) for ref in refs[: len(small)]]
        position = place() + (tiles[0] if tiles else [])
        kernel(position, *tiles[1:], *refs[len(small) :])

    return pl.pallas_call(
        body,
        name=name,
        in_specs=[VMEM_SPEC] * (len(small) + len(arrays)),
        out_specs=[VMEM_SPEC] * len(outs),
        out_shape=[jax.ShapeDtypeStruct(shape, F32) for shape in outs],
        scratch_shapes=[pltpu.VMEM(shape, F32) for shape in scratch],
        compiler_params=pltpu.CompilerParams(vmem_limit_bytes=VMEM_LIMIT),
    )(*small, *arrays)


VEC = (COMP, 8, 128)
FACE = (8, HALF, 8, 128)
SWAP = (HALF, 8, 128)
LAYER = (13, 8, 128)


def local(bricks, source, reaction, smoother, diffusion, active):
    act = active.reshape(1, 4)
    small = [act, diffusion.reshape(1, COMP)]
    src = source.reshape(VEC)
    react = reaction.reshape(COMP * COMP * 8, 128)
    smoo = smoother.reshape(COMP * COMP * 8, 128)
    groups = bricks // 4

    chip_pairs = [(i, i ^ 1) for i in range(bricks)]
    pairs = [(i, i + 1) for i in range(1, bricks - 1, 2)]
    swap_pairs = pairs + [(b, a) for a, b in pairs]
    far_pairs, near_pairs = [], []
    for i in range(bricks):
        g, p = divmod(i, 4)
        step = 1 if p >= 2 else -1
        if 0 <= g + step < groups:
            far_pairs.append((i, 4 * (g + step) + 3 - p))
            if p in (1, 2):
                near_pairs.append((i, i + 4 * step))

    def faces(face, swap):
        swap = lax.ppermute(swap, X_AXES, swap_pairs)
        face = lax.all_to_all(face, ("core", "gz"), 0, 0)
        return face, swap

    def layers(chip, cross):
        return lax.ppermute(chip, X_AXES, chip_pairs), lax.ppermute(cross, X_AXES, swap_pairs)

    def to_coarse(message, with_blocks):
        recv = lax.all_to_all(message, ("xc", "core", "gz"), 0, 0)
        far_rows, near_rows = (18 + 3 * BRICK_TILES, 6 + BRICK_TILES) if with_blocks else (18, 6)
        own, far, near = call(
            functools.partial(gather_kernel, with_blocks),
            "gather",
            [],
            [recv],
            [(4, HALF, 8, 128), (far_rows, 8, 128), (near_rows, 8, 128)],
        )
        far = lax.ppermute(far, X_AXES, far_pairs)
        near = lax.ppermute(near, X_AXES, near_pairs)
        return recv, own, far, near

    u, edges = call(first_kernel, "first", [act], [src, smoo], [VEC, (4, 3, 8, 128)])
    (packed,) = call(blocks_kernel, "blocks", [act], [smoo, react], [(2, 8, 128)], [(2, 160, 128)])
    edges = lax.all_to_all(edges, "gz", 0, 0)
    part, chip, cross = call(
        part_kernel, "part", small, [src, react, u, edges], [VEC, LAYER, LAYER]
    )
    chip, cross = layers(chip, cross)
    resid, message = call(
        functools.partial(send_kernel, False),
        "send",
        small,
        [u, part, chip, cross, packed],
        [VEC, (16, 5, 8, 128)],
    )
    recv, own, far, near = to_coarse(message, True)
    rhs_shape, bx_shape, win_shape = (8, HALF, 8, 128), (7, 72, 2, 8, 128), (8, CHANNELS, 8, 128)
    u, face, swap, window, around = call(
        functools.partial(correct_kernel, False),
        "correct",
        small,
        [react, smoo, u, resid, recv, own, far, near],
        [VEC, FACE, SWAP, win_shape, (3, 8, 128)],
        [rhs_shape, bx_shape],
    )
    face, swap = faces(face, swap)
    u, part, chip, cross = call(
        sweep_kernel, "sweep", small, [src, react, u, face, swap, smoo], [VEC, VEC, LAYER, LAYER]
    )
    chip, cross = layers(chip, cross)
    resid, message = call(
        functools.partial(send_kernel, True),
        "send",
        small,
        [u, part, chip, cross, around],
        [VEC, (16, 6, 8, 128)],
    )
    recv, own, far, near = to_coarse(message, False)
    u, face, swap = call(
        functools.partial(correct_kernel, True),
        "correct",
        small,
        [react, smoo, u, resid, recv, own, far, near, window],
        [VEC, FACE, SWAP],
        [rhs_shape, bx_shape],
    )
    face, swap = faces(face, swap)
    (resid,) = call(last_kernel, "last", small, [src, react, u, face, swap], [VEC])
    return u.reshape(source.shape), resid.reshape(source.shape)


def solution(mesh):
    bricks = mesh.shape["bricks"]
    gz = mesh.shape["gz"]
    inner = Mesh(mesh.devices.reshape(bricks // 4, 2, 2, gz), X_AXES + ("gz",))
    in_specs = (
        P(None, X_AXES, "gz", None),
        P(None, None, X_AXES, "gz", None),
        P(None, None, X_AXES, "gz", None),
        P(),
        P(X_AXES, "gz", None),
    )
    out_specs = (P(None, X_AXES, "gz", None), P(None, X_AXES, "gz", None))
    return jax.shard_map(
        functools.partial(local, bricks),
        mesh=inner,
        in_specs=in_specs,
        out_specs=out_specs,
        check_vma=False,
    )
```

```python
import functools

import jax
import jax.numpy as jnp
from jax import lax
from jax.experimental import pallas as pl
from jax.experimental.pallas import tpu as pltpu
from jax.sharding import Mesh
from jax.sharding import PartitionSpec as P

COMP = 12
HALF = 6
F32 = jnp.float32
BF16 = jnp.bfloat16
X_AXES = ("xg", "xc", "core")
TILE = (8, 128)
CHANNELS = 11
BRICK_TILES = 6
CENTRE = 3
VMEM_LIMIT = 16 * 1024 * 1024


def rows(shape=TILE):
    return lax.broadcasted_iota(jnp.int32, shape, 0)


def lanes(shape=TILE):
    return lax.broadcasted_iota(jnp.int32, shape, 1)


def up(x, by):
    return pltpu.roll(x, 8 - by, 0)


def down(x, by):
    return pltpu.roll(x, by, 0)


def pick(cond, a, b):
    return jnp.where(cond, a, b)


def hat(diff):
    inner = jnp.logical_or(diff == 0, diff == 1)
    outer = jnp.logical_or(diff == -1, diff == 2)
    return jnp.where(inner, 3.0, jnp.where(outer, 1.0, 0.0)).astype(F32)


def split(x, parts):
    pieces = []
    for _ in range(parts):
        piece = x.astype(BF16)
        pieces.append(piece)
        x = x - piece.astype(F32)
    return pieces


def dot(a, b):
    return jnp.dot(a, b, preferred_element_type=F32)


def dot_right(x, weights, parts=2):
    return dot(jnp.concatenate(split(x, parts), axis=1), jnp.concatenate([weights] * parts, axis=0))


def dot_left(weights, x, parts=2):
    return dot(jnp.concatenate([weights] * parts, axis=1), jnp.concatenate(split(x, parts), axis=0))


def fine_mask_of(here):
    brick = lanes() // 32
    out = jnp.zeros(TILE, F32)
    for b in range(4):
        out = jnp.where(brick == b, here[5 + b], out)
    return out


def packed_mask_of(here):
    brick = (lanes() % 64) // 16
    out = jnp.zeros(TILE, F32)
    for b in range(4):
        out = jnp.where(brick == b, here[5 + b], out)
    return out


def load(ref):
    return [ref[c] for c in range(COMP)]


def block_product(blocks_ref, vec):
    out = []
    for c in range(COMP):
        acc = None
        for d in range(0, COMP, 2):
            pair = blocks_ref[pl.ds((c * COMP + d) * 8, 16), :].astype(F32)
            term = pair[:8] * vec[d] + pair[8:] * vec[d + 1]
            acc = term if acc is None else acc + term
        out.append(acc)
    return out


def smooth(smoother_ref, mask, resid):
    prod = block_product(smoother_ref, resid)
    return [mask * a + (1.0 - mask) * r for a, r in zip(prod, resid)]


def neighbours(mv, hx, hz):
    z = rows() % 4
    lane = lanes()
    total = down(mv, 4) + hx + hz
    total = total + jnp.where(z > 0, down(mv, 1), 0.0) + jnp.where(z < 3, up(mv, 1), 0.0)
    total = total + jnp.where(lane > 0, pltpu.roll(mv, 1, 1), 0.0)
    return total + jnp.where(lane < 127, pltpu.roll(mv, 127, 1), 0.0)


def operator(reaction_ref, diff_ref, mask, vec, hx, hz):
    prod = block_product(reaction_ref, vec)
    out = []
    for c in range(COMP):
        v = vec[c]
        inner = prod[c] + diff_ref[c] * (6.0 * v - neighbours(mask * v, hx[c], hz[c]))
        out.append(mask * inner + (1.0 - mask) * v)
    return out


def x_messages(vec):
    low_half = rows() < 4
    to_high, to_low = [], []
    for j in range(HALF):
        a, b = vec[j], vec[j + HALF]
        to_high.append(jnp.where(low_half, down(a, 4), b))
        to_low.append(jnp.where(low_half, a, down(b, 4)))
    return to_high, to_low


def x_halo(low, high):
    low_half = rows() < 4
    first = [jnp.where(low_half, a, down(b, 4)) for a, b in zip(low, high)]
    second = [jnp.where(low_half, down(a, 4), b) for a, b in zip(low, high)]
    return first + second


def z_messages(vec):
    z = rows() % 4
    to_high, to_low = [], []
    for c in range(3):
        up_tile, down_tile = up(vec[c], 3), vec[c]
        for k in range(1, 4):
            t = vec[c + 3 * k]
            up_tile = jnp.where(z == k, up(t, 3 - k) if k < 3 else t, up_tile)
            down_tile = jnp.where(z == k, down(t, k), down_tile)
        to_high.append(up_tile)
        to_low.append(down_tile)
    return to_high, to_low


def z_halo(zd, low, high):
    z = rows() % 4
    has_low = jnp.logical_and(z == 0, zd > 0)
    has_high = jnp.logical_and(z == 3, zd < 3)
    out = []
    for c in range(COMP):
        k, at = c // 3, c % 3
        a = up(low[at], k) if k else low[at]
        b = down(high[at], 3 - k) if k < 3 else high[at]
        out.append(jnp.where(has_low, a, jnp.where(has_high, b, 0.0)))
    return out


def write_faces(here, mask, vec, face_ref, swap_ref):
    core, zd = here[0], here[1]
    first = core == 0
    mv = [mask * v for v in vec]
    x_high, x_low = x_messages(mv)
    z_high, z_low = z_messages(mv)
    for j in range(HALF):
        in_chip = pick(first, x_high[j], x_low[j])
        swap_ref[j] = pick(first, x_low[j], x_high[j])
        for other in range(4):
            along = pick(other > zd, z_high[j % 3], z_low[j % 3])
            face_ref[other, j] = pick(first, along, in_chip)
            face_ref[4 + other, j] = pick(first, in_chip, along)


def read_faces(here, face_ref, swap_ref):
    core, zd = here[0], here[1]
    first = core == 0
    chip_at = (1 - core) * 4 + zd
    low_at = core * 4 + jnp.maximum(zd - 1, 0)
    high_at = core * 4 + jnp.minimum(zd + 1, 3)
    low, high = [], []
    for j in range(HALF):
        chip, cross = face_ref[chip_at, j], swap_ref[j]
        low.append(pick(first, cross, chip))
        high.append(pick(first, chip, cross))
    hz = z_halo(zd, [face_ref[low_at, c] for c in range(3)], [face_ref[high_at, c] for c in range(3)])
    return x_halo(low, high), hz


def write_layers(here, mask, vec, resid, chip_ref, cross_ref):
    first = here[0] == 0
    r_high, r_low = x_messages(resid)
    v_high, v_low = x_messages([mask * v for v in vec])
    for n, (high, low) in enumerate(zip(r_high + v_high + [mask], r_low + v_low + [mask])):
        chip_ref[n] = pick(first, high, low)
        cross_ref[n] = pick(first, low, high)


def restrict(own, beside, above):
    kinds = [own, beside] + ([above] if above is not None else [])
    depth = 8 * len(kinds)
    l, o = rows((128, 128)), lanes((128, 128))
    low = jnp.where(o < 64, hat(l - 2 * o), 0.0).astype(BF16)
    high = jnp.where(o >= 64, hat(l - 2 * (o - 64)), 0.0).astype(BF16)
    a = jnp.concatenate([kind[j] for j in range(HALF) for kind in kinds], axis=0)
    b = jnp.concatenate([kind[j + HALF] for j in range(HALF) for kind in kinds], axis=0)
    along_y = (dot_right(a, low) + dot_right(b, high)) * 0.125
    blocks = [along_y[depth * j : depth * j + depth] for j in range(HALF)]
    stacked = jnp.concatenate(
        [jnp.concatenate(blocks[:3], axis=1), jnp.concatenate(blocks[3:], axis=1)], axis=0
    )
    o, k = rows((8, 2 * depth)), lanes((8, 2 * depth))
    kind, s = (k % depth) // 8, k % 8
    z = s % 4
    outer_x = jnp.where(s < 4, -1, 2)
    in_own = jnp.logical_or(z == 0, z == 3)
    x = jnp.where(kind == 0, s // 4, jnp.where(kind == 1, outer_x, jnp.where(in_own, s // 4, outer_x)))
    fine_z = jnp.where(kind == 2, jnp.where(z < 2, -1, 4), z)
    weights = hat(x) * hat(fine_z - 2 * (o % 4 - 1))
    weights = jnp.where(o // 4 == k // depth, weights, 0.0).astype(BF16)
    result = dot_left(weights, stacked) * (1.0 / 64.0)
    return [result[:, 128 * jj : 128 * jj + 128] for jj in range(3)]


def packed_blocks(smoother_ref, reaction_ref, here, sums_ref):
    l, o = rows((128, 128)), lanes((128, 128))
    weights = jnp.where(l // 32 == o % 4, 1.0 / 256.0, 0.0).astype(BF16)
    zero = jnp.zeros((16, 128), F32)
    for a, ref in enumerate((smoother_ref, reaction_ref)):
        for n in range(0, COMP * COMP, 2):
            pair = ref[pl.ds(n * 8, 16), :].astype(F32)
            sums_ref[a, pl.ds(n, 1), :] = jnp.sum(pair[:8], axis=0, keepdims=True)
            sums_ref[a, pl.ds(n + 1, 1), :] = jnp.sum(pair[8:], axis=0, keepdims=True)
        sums_ref[a, pl.ds(144, 16), :] = zero
        sums_ref[a] = dot_right(sums_ref[a], weights)
    s, lane = rows((16, 128)), lanes((16, 128))
    out = zero
    for k in range(8):
        for a in range(2):
            for half in range(2):
                part = sums_ref[a, pl.ds(72 * half + 9 * k, 16), :]
                out = jnp.where(lane // 4 == 4 * k + 2 * a + half, part, out)
    coarse = jnp.broadcast_to(packed_mask_of(here)[:1], (16, 128))
    fine = jnp.broadcast_to(fine_mask_of(here)[:1], (16, 128))
    return jnp.where(s < 9, out, jnp.where(s == 9, coarse, jnp.where(s == 10, fine, 0.0)))


def expand_channel(get_row):
    owner = rows() // 2
    out = jnp.broadcast_to(get_row(0), TILE)
    for zd in range(1, 4):
        out = jnp.where(owner == zd, jnp.broadcast_to(get_row(zd), TILE), out)
    return out


def slots_of(p):
    right = p // 2
    out = []
    for w in range(7):
        x = p - CENTRE + w
        before = jnp.where(right == 0, x + 7, 7)
        after = jnp.where(right == 1, x, 7)
        out.append(jnp.where(x < 0, before, jnp.where(x > 3, after, x)))
    return out


def coarse_product(bx_ref, which, w, vec):
    left = lanes() < 64
    both = [None] * COMP
    for j in range(HALF):
        turned = pltpu.roll(vec[j], 64, 1)
        both[j] = jnp.where(left, vec[j], turned)
        both[j + HALF] = jnp.where(left, turned, vec[j])
    out = []
    for j in range(HALF):
        acc = None
        for d in range(COMP):
            term = bx_ref[w, j * COMP + d, which] * both[d]
            acc = term if acc is None else acc + term
        out.append(acc)
    return out


def coarse_smooth(bx_ref, mask, w, resid):
    prod = coarse_product(bx_ref, 0, w, resid)
    return [mask * a + (1.0 - mask) * r for a, r in zip(prod, resid)]


def expand_blocks(win_ref, bx_ref, slots):
    flat = jnp.concatenate([win_ref[slot, r] for slot in slots for r in range(9)], axis=0)
    pieces = jnp.concatenate(split(flat, 2), axis=1)
    l, o = rows((256, 256)) % 128, lanes((256, 256))
    target = (o // 128) * 8 + ((o % 128) // 64) * 4 + (o % 64) // 16
    for k in range(8):
        weights = jnp.where(l == 16 * k + target, 1.0, 0.0).astype(BF16)
        out = dot(pieces, weights)
        for w in range(7):
            for r in range(9):
                tile = out[(w * 9 + r) * 8 : (w * 9 + r) * 8 + 8]
                bx_ref[w, 9 * k + r, 0] = tile[:, :128]
                if 0 < w < 6:
                    bx_ref[w, 9 * k + r, 1] = tile[:, 128:]


def solve_coarse(diff_ref, rhs, slots, win_ref, bx_ref):
    s, lane = rows(), lanes()
    left = lane < 64
    inner_lane = lane % 64
    coeffs = [
        0.25 * jnp.where(left, diff_ref[j], diff_ref[j + HALF])
        for j in range(HALF)
    ]
    masks = [win_ref[slots[w], 9] for w in range(7)]
    b = [rhs(w) for w in range(7)]
    v = [coarse_smooth(bx_ref, masks[w], w, b[w]) for w in range(7)]
    for edge in (1, 2):
        mv = [[masks[w] * t for t in v[w]] if v[w] is not None else None for w in range(7)]
        new = [None] * 7
        for w in range(edge, 7 - edge):
            prod = coarse_product(bx_ref, 1, w, v[w])
            resid = []
            for j in range(HALF):
                t = mv[w][j]
                total = mv[w - 1][j] + mv[w + 1][j]
                total = total + jnp.where(s > 0, down(t, 1), 0.0) + jnp.where(s < 7, up(t, 1), 0.0)
                total = total + jnp.where(inner_lane > 0, pltpu.roll(t, 1, 1), 0.0)
                total = total + jnp.where(inner_lane < 63, pltpu.roll(t, 127, 1), 0.0)
                inner = prod[j] + coeffs[j] * (6.0 * v[w][j] - total)
                resid.append(b[w][j] - (masks[w] * inner + (1.0 - masks[w]) * v[w][j]))
            step = coarse_smooth(bx_ref, masks[w], w, resid)
            new[w] = [x + y for x, y in zip(v[w], step)]
        v = new
    return v[2:5]


def prolong(here, q):
    zd = here[1]
    o, k = rows((24, 24)), lanes((24, 24))
    group, s = o // 8, o % 8
    z = s % 4
    fx = jnp.where(group == 1, jnp.where(s < 4, -1, 2), s // 4)
    fz = jnp.where(group == 2, jnp.where(z == 0, -1, 4), z) + 4 * zd
    weights = hat(fx - 2 * (k // 8 - 1)) * hat(fz - 2 * (k % 8))
    unused = jnp.logical_and(group == 2, jnp.logical_or(z == 1, z == 2))
    weights = jnp.where(unused, 0.0, weights * 0.0625).astype(BF16)
    stacked = jnp.concatenate([jnp.concatenate(row, axis=1) for row in q], axis=0)
    xz = dot_left(weights, stacked)
    tall = jnp.concatenate([xz[:, 128 * j : 128 * j + 128] for j in range(HALF)], axis=0)
    a, f = rows((128, 256)), lanes((128, 256))
    along = hat(f % 128 - 2 * (a % 64)) * 0.25
    along = jnp.where(a // 64 == f // 128, along, 0.0).astype(BF16)
    fine = dot_right(tall, along)
    groups = []
    for g in range(3):
        tiles = [fine[24 * j + 8 * g : 24 * j + 8 * g + 8] for j in range(HALF)]
        groups.append([t[:, :128] for t in tiles] + [t[:, 128:] for t in tiles])
    return groups


def masks_around(zd, tile):
    own = pltpu.roll(tile, lax.rem(8 - 2 * zd, 8), 0)
    return own[7:8], own[:1], own[2:3]


def outside_masks(zd, tiles):
    s = rows()
    z = s % 4
    _, low_x, _ = masks_around(zd, tiles[0])
    low_z, _, high_z = masks_around(zd, tiles[1])
    _, high_x, _ = masks_around(zd, tiles[2])
    mask_x = jnp.where(s < 4, jnp.broadcast_to(low_x, TILE), jnp.broadcast_to(high_x, TILE))
    mask_z = jnp.where(
        jnp.logical_and(z == 0, zd > 0),
        jnp.broadcast_to(low_z, TILE),
        jnp.where(jnp.logical_and(z == 3, zd < 3), jnp.broadcast_to(high_z, TILE), 0.0),
    )
    return mask_x, mask_z


def layer_masks(zd, tiles):
    s = rows()
    z = s % 4
    around = [masks_around(zd, tile) for tile in tiles]
    below = [jnp.broadcast_to(a[0], TILE) for a in around]
    above = [jnp.broadcast_to(a[2], TILE) for a in around]
    low = jnp.where(z == 0, below[1], jnp.where(s < 4, below[0], below[2]))
    high = jnp.where(z == 3, above[1], jnp.where(s < 4, above[0], above[2]))
    low = jnp.where(zd > 0, low, 0.0)
    high = jnp.where(zd < 3, high, 0.0)
    return jnp.where(z < 2, low, high)


ZEROS = [0.0] * COMP


def first_kernel(here, src_ref, smoother_ref, u_ref, z_ref):
    mask = fine_mask_of(here)
    zd = here[1]
    u = smooth(smoother_ref, mask, load(src_ref))
    for c in range(COMP):
        u_ref[c] = u[c]
    high, low = z_messages([mask * v for v in u])
    for other in range(4):
        for n in range(3):
            z_ref[other, n] = pick(other > zd, high[n], low[n])


def blocks_kernel(here, smoother_ref, reaction_ref, out_ref, sums_ref):
    packed = packed_blocks(smoother_ref, reaction_ref, here, sums_ref)
    out_ref[0] = packed[:8]
    out_ref[1] = packed[8:]


def part_kernel(
    here, diff_ref, src_ref, reaction_ref, u_ref, z_ref, r_ref, chip_ref, cross_ref
):
    mask = fine_mask_of(here)
    zd = here[1]
    u = load(u_ref)
    below, above = jnp.maximum(zd - 1, 0), jnp.minimum(zd + 1, 3)
    hz = z_halo(zd, [z_ref[below, n] for n in range(3)], [z_ref[above, n] for n in range(3)])
    au = operator(reaction_ref, diff_ref, mask, u, ZEROS, hz)
    resid = [src_ref[c] - au[c] for c in range(COMP)]
    for c in range(COMP):
        r_ref[c] = resid[c]
    write_layers(here, mask, u, resid, chip_ref, cross_ref)


def send_kernel(
    again, here, diff_ref, u_ref, part_ref, chip_ref, cross_ref, extra_ref, r_ref, out_ref
):
    mask = fine_mask_of(here)
    zd = here[1]
    first = here[0] == 0
    low = [pick(first, cross_ref[n], chip_ref[n]) for n in range(13)]
    high = [pick(first, chip_ref[n], cross_ref[n]) for n in range(13)]
    hr = x_halo(low[:6], high[:6])
    hv = x_halo(low[6:12], high[6:12])
    mask_x = jnp.where(rows() < 4, low[12], high[12])
    mv = [mask * u_ref[c] for c in range(COMP)]
    own = [part_ref[c] + mask * (diff_ref[c] * hv[c]) for c in range(COMP)]
    beside = [hr[c] + mask_x * (diff_ref[c] * mv[c]) for c in range(COMP)]
    for c in range(COMP):
        r_ref[c] = own[c]
    above = None
    if again:
        z = rows() % 4
        inner = jnp.logical_or(z == 0, z == 3)
        edge = layer_masks(zd, [extra_ref[n] for n in range(3)])
        above = []
        for c in range(COMP):
            outer = jnp.where(z == 1, down(hv[c], 1), up(hv[c], 1))
            above.append(edge * (diff_ref[c] * jnp.where(inner, mv[c], outer)))
    tiles = restrict(own, beside, above)
    if not again:
        tiles = tiles + [extra_ref[0], extra_ref[1]]
    for n, tile in enumerate(tiles):
        for target in range(16):
            out_ref[target, n] = tile
    if again:
        z_high, z_low = z_messages(mv)
        for n in range(3):
            for other in range(4):
                tile = pick(other > zd, z_high[n], z_low[n])
                for q in range(4):
                    out_ref[q * 4 + other, 3 + n] = tile


def gather_kernel(with_blocks, here, recv_ref, own_ref, far_ref, near_ref):
    right = here[2] // 2
    s = rows()
    low_half = s < 4
    for q in range(4):
        for jj in range(3):
            m0, m1, m2, m3 = [recv_ref[q * 4 + zd, jj] for zd in range(4)]
            even = (jnp.where(low_half, m0, down(m2, 4)), jnp.where(low_half, down(m0, 4), m2))
            odd = (jnp.where(low_half, m1, down(m3, 4)), jnp.where(low_half, down(m1, 4), m3))
            for n in range(2):
                own_ref[q, jj + 3 * n] = jnp.where(s < 7, up(even[n], 1), 0.0) + jnp.where(
                    s > 0, down(odd[n], 1), 0.0
                )
    for e in range(3):
        for j in range(HALF):
            far_ref[e * 6 + j] = own_ref[right + e, j]
    for j in range(HALF):
        near_ref[j] = own_ref[3 * right, j]
    if with_blocks:
        for n in range(BRICK_TILES):
            for e in range(3):
                far_ref[18 + e * BRICK_TILES + n] = brick_tile(recv_ref, right + e, n)
            near_ref[6 + n] = brick_tile(recv_ref, 3 * right, n)


def brick_tile(recv_ref, q, n):
    s = rows()
    out = None
    for at in range(8):
        r = 2 * n + at // 4
        row = recv_ref[q * 4 + at % 4, 3 + r // 8, pl.ds(r % 8, 1), :]
        row = jnp.broadcast_to(row, TILE)
        out = row if out is None else jnp.where(s == at, row, out)
    return out


def fill_own(recv_ref, win_ref):
    for r in range(CHANNELS):
        at, tile = pl.ds(r % 8, 1), r // 8
        for q in range(4):
            win_ref[q, r] = expand_channel(lambda zd: recv_ref[q * 4 + zd, 3 + tile, at, :])


def fill_others(far_ref, near_ref, win_ref):
    for r in range(CHANNELS):
        tile, base = r // 2, 4 * (r % 2)
        for e in range(3):
            win_ref[4 + e, r] = expand_channel(
                lambda zd: far_ref[18 + e * BRICK_TILES + tile, pl.ds(base + zd, 1), :]
            )
        win_ref[7, r] = expand_channel(lambda zd: near_ref[6 + tile, pl.ds(base + zd, 1), :])


def correct_kernel(
    again,
    here,
    diff_ref,
    reaction_ref,
    smoother_ref,
    u_ref,
    r_ref,
    recv_ref,
    own_ref,
    far_ref,
    near_ref,
    *rest,
):
    zd, p, brick, bricks = here[1], here[2], here[3], here[4]
    if again:
        win_ref, new_ref, face_ref, swap_ref, rhs_ref, bx_ref = rest
    else:
        new_ref, face_ref, swap_ref, win_ref, around_ref, rhs_ref, bx_ref = rest
        fill_own(recv_ref, win_ref)
        fill_others(far_ref, near_ref, win_ref)
    slots = slots_of(p)
    expand_blocks(win_ref, bx_ref, slots)
    for j in range(HALF):
        for q in range(4):
            rhs_ref[q, j] = own_ref[q, j]
        for e in range(3):
            rhs_ref[4 + e, j] = far_ref[e * 6 + j]
        rhs_ref[7, j] = near_ref[j]

    def rhs(w):
        place = brick + (w - CENTRE)
        inside = jnp.logical_and(place >= 0, place < bricks)
        return [pick(inside, rhs_ref[slots[w], j], 0.0) for j in range(HALF)]

    q = solve_coarse(diff_ref, rhs, slots, win_ref, bx_ref)
    inside, hx, hz = prolong(here, q)
    fine_masks = [win_ref[slots[CENTRE + n], 10] for n in (-1, 0, 1)]
    if not again:
        for n in range(3):
            around_ref[n] = fine_masks[n]
    mask_x, mask_z = outside_masks(zd, fine_masks)
    hx = [mask_x * t for t in hx]
    hz = [mask_z * t for t in hz]
    mask = fine_mask_of(here)
    change = operator(reaction_ref, diff_ref, mask, inside, hx, hz)
    resid = [r_ref[c] - change[c] for c in range(COMP)]
    if again:
        below = p * 4 + jnp.maximum(zd - 1, 0)
        above = p * 4 + jnp.minimum(zd + 1, 3)
        halo = z_halo(
            zd, [recv_ref[below, 3 + n] for n in range(3)], [recv_ref[above, 3 + n] for n in range(3)]
        )
        resid = [r + mask * (diff_ref[c] * h) for c, (r, h) in enumerate(zip(resid, halo))]
    step = smooth(smoother_ref, mask, resid)
    new = [u_ref[c] + inside[c] + step[c] for c in range(COMP)]
    for c in range(COMP):
        new_ref[c] = new[c]
    write_faces(here, mask, new, face_ref, swap_ref)


def residual(here, diff_ref, src_ref, reaction_ref, u_ref, face_ref, swap_ref):
    mask = fine_mask_of(here)
    u = load(u_ref)
    hx, hz = read_faces(here, face_ref, swap_ref)
    au = operator(reaction_ref, diff_ref, mask, u, hx, hz)
    return mask, u, [src_ref[c] - au[c] for c in range(COMP)]


def sweep_kernel(
    here, diff_ref, src_ref, reaction_ref, u_ref, face_ref, swap_ref, smoother_ref,
    new_ref, part_ref, chip_ref, cross_ref,
):
    mask, u, resid = residual(
        here, diff_ref, src_ref, reaction_ref, u_ref, face_ref, swap_ref
    )
    step = smooth(smoother_ref, mask, resid)
    new = [a + b for a, b in zip(u, step)]
    au = operator(reaction_ref, diff_ref, mask, new, ZEROS, ZEROS)
    part = [src_ref[c] - au[c] for c in range(COMP)]
    for c in range(COMP):
        new_ref[c] = new[c]
        part_ref[c] = part[c]
    write_layers(here, mask, new, part, chip_ref, cross_ref)


def last_kernel(
    here, diff_ref, src_ref, reaction_ref, u_ref, face_ref, swap_ref, r_ref
):
    _, _, resid = residual(
        here, diff_ref, src_ref, reaction_ref, u_ref, face_ref, swap_ref
    )
    for c in range(COMP):
        r_ref[c] = resid[c]


VMEM_SPEC = pl.BlockSpec(memory_space=pltpu.VMEM)


def place():
    core = lax.axis_index("core")
    p = lax.axis_index("xc") * 2 + core
    brick = lax.axis_index("xg") * 4 + p
    return [core, lax.axis_index("gz"), p, brick, lax.axis_size("xg") * 4]


def spread(row_ref):
    return [
        jnp.broadcast_to(row_ref[:, n : n + 1], TILE).astype(F32) for n in range(row_ref.shape[1])
    ]


def call(kernel, name, small, arrays, outs, scratch=()):
    def body(*refs):
        tiles = [spread(ref) for ref in refs[: len(small)]]
        position = place() + (tiles[0] if tiles else [])
        kernel(position, *tiles[1:], *refs[len(small) :])

    return pl.pallas_call(
        body,
        name=name,
        in_specs=[VMEM_SPEC] * (len(small) + len(arrays)),
        out_specs=[VMEM_SPEC] * len(outs),
        out_shape=[jax.ShapeDtypeStruct(shape, F32) for shape in outs],
        scratch_shapes=[pltpu.VMEM(shape, F32) for shape in scratch],
        compiler_params=pltpu.CompilerParams(vmem_limit_bytes=VMEM_LIMIT),
    )(*small, *arrays)


VEC = (COMP, 8, 128)
FACE = (8, HALF, 8, 128)
SWAP = (HALF, 8, 128)
LAYER = (13, 8, 128)


def local(bricks, source, reaction, smoother, diffusion, active):
    act = active.reshape(1, 4)
    small = [act, diffusion.reshape(1, COMP)]
    src = source.reshape(VEC)
    react = reaction.reshape(COMP * COMP * 8, 128)
    smoo = smoother.reshape(COMP * COMP * 8, 128)
    groups = bricks // 4

    chip_pairs = [(i, i ^ 1) for i in range(bricks)]
    pairs = [(i, i + 1) for i in range(1, bricks - 1, 2)]
    swap_pairs = pairs + [(b, a) for a, b in pairs]
    far_pairs, near_pairs = [], []
    for i in range(bricks):
        g, p = divmod(i, 4)
        step = 1 if p >= 2 else -1
        if 0 <= g + step < groups:
            far_pairs.append((i, 4 * (g + step) + 3 - p))
            if p in (1, 2):
                near_pairs.append((i, i + 4 * step))

    def faces(face, swap):
        swap = lax.ppermute(swap, X_AXES, swap_pairs)
        face = lax.all_to_all(face, ("core", "gz"), 0, 0)
        return face, swap

    def layers(chip, cross):
        return lax.ppermute(chip, X_AXES, chip_pairs), lax.ppermute(cross, X_AXES, swap_pairs)

    def to_coarse(message, with_blocks):
        recv = lax.all_to_all(message, ("xc", "core", "gz"), 0, 0)
        far_rows, near_rows = (18 + 3 * BRICK_TILES, 6 + BRICK_TILES) if with_blocks else (18, 6)
        own, far, near = call(
            functools.partial(gather_kernel, with_blocks),
            "gather",
            [],
            [recv],
            [(4, HALF, 8, 128), (far_rows, 8, 128), (near_rows, 8, 128)],
        )
        far = lax.ppermute(far, X_AXES, far_pairs)
        near = lax.ppermute(near, X_AXES, near_pairs)
        return recv, own, far, near

    u, edges = call(first_kernel, "first", [act], [src, smoo], [VEC, (4, 3, 8, 128)])
    (packed,) = call(blocks_kernel, "blocks", [act], [smoo, react], [(2, 8, 128)], [(2, 160, 128)])
    edges = lax.all_to_all(edges, "gz", 0, 0)
    part, chip, cross = call(
        part_kernel, "part", small, [src, react, u, edges], [VEC, LAYER, LAYER]
    )
    chip, cross = layers(chip, cross)
    resid, message = call(
        functools.partial(send_kernel, False),
        "send",
        small,
        [u, part, chip, cross, packed],
        [VEC, (16, 5, 8, 128)],
    )
    recv, own, far, near = to_coarse(message, True)
    rhs_shape, bx_shape, win_shape = (8, HALF, 8, 128), (7, 72, 2, 8, 128), (8, CHANNELS, 8, 128)
    u, face, swap, window, around = call(
        functools.partial(correct_kernel, False),
        "correct",
        small,
        [react, smoo, u, resid, recv, own, far, near],
        [VEC, FACE, SWAP, win_shape, (3, 8, 128)],
        [rhs_shape, bx_shape],
    )
    face, swap = faces(face, swap)
    u, part, chip, cross = call(
        sweep_kernel, "sweep", small, [src, react, u, face, swap, smoo], [VEC, VEC, LAYER, LAYER]
    )
    chip, cross = layers(chip, cross)
    resid, message = call(
        functools.partial(send_kernel, True),
        "send",
        small,
        [u, part, chip, cross, around],
        [VEC, (16, 6, 8, 128)],
    )
    recv, own, far, near = to_coarse(message, False)
    u, face, swap = call(
        functools.partial(correct_kernel, True),
        "correct",
        small,
        [react, smoo, u, resid, recv, own, far, near, window],
        [VEC, FACE, SWAP],
        [rhs_shape, bx_shape],
    )
    face, swap = faces(face, swap)
    (resid,) = call(last_kernel, "last", small, [src, react, u, face, swap], [VEC])
    return u.reshape(source.shape), resid.reshape(source.shape)


def solution(mesh):
    bricks = mesh.shape["bricks"]
    gz = mesh.shape["gz"]
    inner = Mesh(mesh.devices.reshape(bricks // 4, 2, 2, gz), X_AXES + ("gz",))
    in_specs = (
        P(None, X_AXES, "gz", None),
        P(None, None, X_AXES, "gz", None),
        P(None, None, X_AXES, "gz", None),
        P(),
        P(X_AXES, "gz", None),
    )
    out_specs = (P(None, X_AXES, "gz", None), P(None, X_AXES, "gz", None))
    return jax.shard_map(
        functools.partial(local, bricks),
        mesh=inner,
        in_specs=in_specs,
        out_specs=out_specs,
        check_vma=False,
    )
```
